32 devices in a mesh: groups: 2 (over y), dp: 4 (over z), tensor: 4 (over x, core).
Axes of the slice: x: 2, y: 2, z: 4, core: 2. Of those that a mesh axis runs over, the one named last changes fastest.
Arguments:
- tokens: bfloat16 [2048, 8192], P(('groups', 'dp'), 'tensor'), parts along dimension 0, may hold values from -6 to 6
- value_weight: bfloat16 [8192, 1024], P('tensor', 'dp'), may hold values from -0.0625 to 0.0625
- adapter_down_weight: bfloat16 [8, 8192, 64], P('dp', 'tensor'), may hold values from -0.0625 to 0.0625
- adapter_up_weight: bfloat16 [8, 64, 1024], P('dp', None, 'tensor'), may hold values from -0.75 to 0.75
- adapter_slot_table: int32 [16], P('groups'), parts along dimension 0, may hold values from 0 to 7, as said below
- adapter_per_block: int32 [32], P(('groups', 'dp')), parts along dimension 0, may hold values from 0 to 7, as said below
- request_rows_per_block: int32 [32], P(('groups', 'dp')), parts along dimension 0, may hold values from 1 to 64
Outputs:
- mixed: bfloat16 [2048, 1024], P(('groups', 'dp'), 'tensor'), parts along dimension 0
The draws below stay inside these ranges and needn't reach their ends.
There are 2 independent parts, one for each index of `groups`. The reference program is written for one: setup_inputs(seed, part) draws one part's arguments, and reference() takes and returns one part's arrays. A program takes and returns all parts, laid end to end along the dimension named above; an argument that names none is the same for every part. Nothing has to cross between parts.
Inputs may be any that keep to these rules, and one draw needn't show every extreme that they name: `adapter_slot_table`: every slot once. Slot s is held by dp index s // 2. `adapter_per_block`: blocks k * 4 to (k + 1) * 4 - 1 stand on dp index k. The blocks of one dp index name adapters held by all 4 dp indices, one block each.
All inputs are finite; a program needn't handle non-finite values.
Results may differ from the reference program's by a relative error of at most 0.014.
Values may be sent and summed in bfloat16 or wider, within the bound.
No kernel may reach another device: no remote copies, remote signals or barrier semaphores. Data moves between devices by JAX's collectives and lax.ppermute only.
A program may use at most 64 MiB of HBM per device.

```python
import jax
import jax.numpy as jnp
from jax import lax

MODEL_WIDTH = 8192
VALUE_OUTPUTS = 1024
ADAPTER_RANK = 64
BLOCK = 64
ADAPT_DEV = 2
NBLK = 16
TOKENS = 1024
ADAPTER_COUNT = 8
N_DP = 4
N_TENSOR = 4


def placement_table(key):
    return jax.random.permutation(key, ADAPTER_COUNT).astype(jnp.int32)


def draw_adapter_slot_table(key, part):
    return placement_table(key)


def draw_adapter_per_block(key, part):
    table = placement_table(key)
    key = jax.random.fold_in(key, 5)
    adapter_at = jnp.argsort(table, stable=True).astype(jnp.int32)
    row_keys = jax.random.split(jax.random.fold_in(key, 2), N_DP)

    def holders(row_key):
        return jax.random.permutation(row_key, N_DP).astype(jnp.int32)
    holder_rows = jax.vmap(holders)(row_keys).reshape(-1)
    within = jax.random.randint(jax.random.fold_in(key, 3), (NBLK,), 0, ADAPT_DEV).astype(jnp.int32)
    slots = holder_rows * ADAPT_DEV + within
    return adapter_at[slots].astype(jnp.int32)


def with_ends(array, key, smallest, high):
    longest = array.shape.index(max(array.shape))
    spots = []
    for shift in (0, 1):
        where = [jax.random.randint(jax.random.fold_in(key, axis), (), 0, length) for axis, length in enumerate(array.shape)]
        where[longest] = (where[longest] + shift) % array.shape[longest]
        spots.append(tuple(where))
    return array.at[spots[0]].set(smallest).at[spots[1]].set(high)


def level_of(stream_key, shape, pieces, smallest, high):
    loudness, own = 1.0, jax.random.fold_in(stream_key, 6)
    for dim, shards_of in pieces:
        steps = jnp.exp(jax.random.uniform(jax.random.fold_in(own, dim), (shards_of,), jnp.float32, smallest / len(pieces), high / len(pieces)))
        loudness = loudness * jnp.repeat(steps, shape[dim] // shards_of).reshape([-1 if axis == dim else 1 for axis in range(len(shape))])
    return loudness


def normal_values(key, shape, spread, limit, cuts=(), held_as=jnp.bfloat16):
    result = spread * jax.random.normal(key, shape, jnp.float32)
    if cuts:
        result = result * level_of(key, shape, cuts, -0.22, 0.18)
    return jnp.clip(result, -limit, limit).astype(held_as)


def setup_inputs(seed: int = 0, part: int = 0) -> dict:
    streams_of = jax.random.split(jax.random.key(seed), 8)
    part_keys = jax.random.split(jax.random.fold_in(streams_of[7], part), 8)
    tokens = normal_values(part_keys[0], (TOKENS, MODEL_WIDTH), 1.0, 6.0, ((0, 4), (1, 4)))
    value_weight = normal_values(streams_of[1], (MODEL_WIDTH, VALUE_OUTPUTS), MODEL_WIDTH ** -0.5, 0.0625, ((0, 4), (1, 4)))
    adapter_down_weight = normal_values(streams_of[2], (ADAPTER_COUNT, MODEL_WIDTH, ADAPTER_RANK), MODEL_WIDTH ** -0.5, 0.0625, ((0, 4), (1, 4)))
    adapter_up_weight = normal_values(streams_of[3], (ADAPTER_COUNT, ADAPTER_RANK, VALUE_OUTPUTS), ADAPTER_RANK ** -0.5, 0.75, ((0, 4), (2, 4)))
    adapter_slot_table = draw_adapter_slot_table(jax.random.fold_in(jax.random.fold_in(streams_of[7], part), 71), part)
    adapter_per_block = draw_adapter_per_block(jax.random.fold_in(jax.random.fold_in(streams_of[7], part), 71), part)
    request_rows_per_block = with_ends(jax.random.randint(part_keys[6], (NBLK,), 1, BLOCK + 1), jax.random.fold_in(part_keys[6], 1), 1, BLOCK).astype(jnp.int32)
    return {"tokens": tokens, "value_weight": value_weight, "adapter_down_weight": adapter_down_weight, "adapter_up_weight": adapter_up_weight, "adapter_slot_table": adapter_slot_table, "adapter_per_block": adapter_per_block, "request_rows_per_block": request_rows_per_block}


def reference(tokens, value_weight, adapter_down_weight, adapter_up_weight, adapter_slot_table, adapter_per_block, request_rows_per_block):
    feature_total = MODEL_WIDTH // N_TENSOR

    def add_group(group_idx, total):
        token_piece = lax.dynamic_slice_in_dim(tokens, group_idx * feature_total, feature_total, 1)
        weight_piece = lax.dynamic_slice_in_dim(value_weight, group_idx * feature_total, feature_total, 0)
        rounded = jnp.dot(token_piece, weight_piece, preferred_element_type=jnp.float32).astype(jnp.bfloat16)
        rounded = lax.optimization_barrier(rounded)
        return total + rounded.astype(jnp.float32)

    base_sum = lax.fori_loop(0, N_TENSOR, add_group, jnp.zeros((TOKENS, VALUE_OUTPUTS), jnp.float32))
    slot_of_block = adapter_slot_table[adapter_per_block].astype(jnp.int32)
    block_tokens = tokens.reshape(NBLK, BLOCK, MODEL_WIDTH)

    def block_delta(pair):
        block_input, slot_index = pair
        reduced_input = jnp.dot(block_input, adapter_down_weight[slot_index], preferred_element_type=jnp.float32).astype(jnp.bfloat16)
        return jnp.dot(reduced_input, adapter_up_weight[slot_index], preferred_element_type=jnp.float32).astype(jnp.bfloat16)

    delta_rows = lax.map(block_delta, (block_tokens, slot_of_block))
    live_mask = jnp.arange(BLOCK, dtype=jnp.int32)[None, :] < request_rows_per_block[:, None]
    summed = base_sum.reshape(NBLK, BLOCK, VALUE_OUTPUTS) + delta_rows.astype(jnp.float32)
    mixed = jnp.where(live_mask[:, :, None], summed, jnp.float32(0.0))
    return mixed.astype(jnp.bfloat16).reshape(TOKENS, VALUE_OUTPUTS)
```

```python
import jax
import jax.numpy as jnp
from jax import lax
from jax.experimental import pallas as pl
from jax.experimental.pallas import tpu as pltpu
from jax.sharding import PartitionSpec as P

AXES = ("groups", "dp", "tensor")
LANES = 128
F32 = jnp.float32
BF16 = jnp.bfloat16
VMEM = pl.BlockSpec(memory_space=pltpu.VMEM)
SMEM = pl.BlockSpec(memory_space=pltpu.SMEM)


def call(body, name, outs, ins):
    return pl.pallas_call(
        body,
        name=name,
        out_shape=outs,
        in_specs=[SMEM] + [VMEM] * (len(ins) - 1),
        out_specs=jax.tree.map(lambda _: VMEM, outs),
        compiler_params=pltpu.CompilerParams(vmem_limit_bytes=40 * 2**20),
    )(*ins)


def local_line(sizes, tokens, value_weight, down, up, slot_table, per_block, live_rows):
    groups, dp, tensor = sizes
    y, z, t = (lax.axis_index(a) for a in AXES)
    rows, feats = tokens.shape
    blocks = per_block.shape[0]
    block_len = rows // blocks
    per_dev, _, rank = down.shape
    out_cols = up.shape[2]
    half_cols = value_weight.shape[1] // groups
    half = feats // 2
    low = half * rank // LANES
    up_rows = per_dev * rank * out_cols // LANES
    pairs = dp // 2

    def device(a, b, c):
        return (a * dp + b) * tensor + c

    def send(x, where):
        perm = []
        for a in range(groups):
            for b in range(dp):
                for c in range(tensor):
                    to = where(a, b, c)
                    if to is not None:
                        perm.append((device(a, b, c), device(*to)))
        return lax.ppermute(x, AXES, perm)

    def rise(x, hop):
        return send(x, lambda a, b, c: (a, b + 1, c) if hop - 1 <= b < dp - 1 else None)

    def fall(x, hop):
        return send(x, lambda a, b, c: (a, b - 1, c) if 0 < b <= dp - hop else None)

    own_ints = jnp.concatenate([per_block, slot_table])
    swap = lambda a, b, c: (1 - a, b, c)
    other_ints = send(own_ints, swap)
    place = jnp.stack([y, z, t]).astype(jnp.int32)
    ints = jnp.concatenate([place, own_ints, other_ints])
    n_ints = own_ints.shape[0]

    def slot_of(ints_ref, which, k):
        base = 3 + which * n_ints
        return ints_ref[base + blocks + ints_ref[base + k]]

    def pack(ints_ref, w_ref, d_ref, u_ref, l_ref, h_ref):
        me = ints_ref[0]
        cols = pl.ds(pl.multiple_of(me * half_cols, LANES), half_cols)
        for part, ref in ((0, l_ref), (1, h_ref)):
            ref[0:half, :] = w_ref[pl.ds(part * half, half), cols]
            for i in range(half // LANES):
                at = part * half + i * LANES
                ref[half + i * rank : half + (i + 1) * rank, :] = d_ref[me, :, at : at + LANES]
        for s in range(per_dev):
            for v in range(out_cols // LANES):
                at = half + low + (s * (out_cols // LANES) + v) * rank
                l_ref[at : at + rank, :] = u_ref[s, :, v * LANES : (v + 1) * LANES]

    l_shape = jax.ShapeDtypeStruct((half + low + up_rows, LANES), BF16)
    h_shape = jax.ShapeDtypeStruct((half + low, LANES), BF16)
    own_l, own_h = call(
        pack,
        "pack",
        (l_shape, h_shape),
        (place, value_weight, jnp.transpose(down, (0, 2, 1)), up),
    )

    rise_l, rise_h, fall_l, fall_h = [own_l], [own_h], [own_l], [own_h]
    rise_l.append(rise(own_l, 1))
    fall_l.append(fall(own_l, 1))
    other_tokens = send(tokens, swap)
    rise_h.append(rise(own_h, 1))
    fall_h.append(fall(own_h, 1))
    for hop in range(2, dp):
        rise_l.append(rise(rise_l[-1], hop))
        fall_l.append(fall(fall_l[-1], hop))
        rise_h.append(rise(rise_h[-1], hop))
        fall_h.append(fall(fall_h[-1], hop))

    def product(ints_ref, tok_refs, l_ref, h_ref, holder, out_ref, s_ref):
        mine = per_dev * holder + ints_ref[0]
        for which, tok in enumerate(tok_refs):
            x_l, x_h = tok[:, 0:half], tok[:, half:feats]
            at = pl.ds(which * rows, rows)
            out_ref[at, :] = jnp.dot(
                x_l, l_ref[0:half, :], preferred_element_type=F32
            ) + jnp.dot(x_h, h_ref[0:half, :], preferred_element_type=F32)
            shrink = jnp.zeros((rows, rank), F32)
            for x, ref in ((x_l, l_ref), (x_h, h_ref)):
                flat = jnp.concatenate(
                    [
                        ref[half + i * rank : half + (i + 1) * rank, :]
                        for i in range(half // LANES)
                    ],
                    axis=1,
                )
                shrink += lax.dot_general(
                    x, flat, (((1,), (1,)), ((), ())), preferred_element_type=F32
                )
            for k in range(blocks):
                @pl.when(slot_of(ints_ref, which, k) == mine)
                def _():
                    s_ref[pl.ds(which * rows + k * block_len, block_len), :] = shrink[
                        k * block_len : (k + 1) * block_len, :
                    ]

    part_shape = jax.ShapeDtypeStruct((groups * rows, half_cols), F32)
    s_shape = jax.ShapeDtypeStruct((groups * rows, rank), F32)

    def own_product(ints_ref, a_ref, b_ref, l_ref, h_ref, out_ref, s_ref):
        s_ref[...] = jnp.zeros_like(s_ref)
        product(ints_ref, (a_ref, b_ref), l_ref, h_ref, ints_ref[1], out_ref, s_ref)

    def hop_product(hop):
        def body(ints_ref, a_ref, b_ref, rl, rh, fl, fh, s_in, r_out, f_out, s_ref):
            here = ints_ref[1]
            s_ref[...] = s_in[...]

            @pl.when(here >= hop)
            def _():
                product(ints_ref, (a_ref, b_ref), rl, rh, here - hop, r_out, s_ref)

            @pl.when(here + hop < dp)
            def _():
                product(ints_ref, (a_ref, b_ref), fl, fh, here + hop, f_out, s_ref)

        return body

    parts = []
    first, shrunk = call(
        own_product,
        "own_columns",
        (part_shape, s_shape),
        (ints, tokens, other_tokens, own_l, own_h),
    )
    for hop in range(1, dp):
        r_part, f_part, shrunk = call(
            hop_product(hop),
            "hop_columns",
            (part_shape, part_shape, s_shape),
            (ints, tokens, other_tokens, rise_l[hop], rise_h[hop], fall_l[hop], fall_h[hop], shrunk),
        )
        parts += [r_part, f_part]

    both = groups * rows
    s_rows = both * rank // LANES

    def sort(ints_ref, *refs):
        o_ref, *p_refs = refs[: 1 + len(parts)]
        s_in = refs[1 + len(parts)]
        keep, away = refs[2 + len(parts) :]
        here, mine = ints_ref[1], ints_ref[2] % 2

        def put(ref, holder):
            at = pl.ds(pl.multiple_of((holder // 2) * both, both), both)

            @pl.when(holder % 2 == mine)
            def _():
                keep[at, :] = ref[...]

            @pl.when(holder % 2 != mine)
            def _():
                away[at, :] = ref[...].astype(BF16)

        put(o_ref, here)
        for hop in range(1, dp):
            pl.when(here >= hop)(lambda hop=hop: put(p_refs[2 * hop - 2], here - hop))
            pl.when(here + hop < dp)(lambda hop=hop: put(p_refs[2 * hop - 1], here + hop))
        for g in range(groups):
            s = jnp.concatenate(
                [s_in[g * rows : g * rows + rows // 2, :], s_in[g * rows + rows // 2 : (g + 1) * rows, :]],
                axis=1,
            )
            at = pairs * both + g * (rows // 2)
            keep[at : at + rows // 2, :] = s
            away[at : at + rows // 2, :] = s.astype(BF16)

    total = pairs * both + s_rows
    keep, away = call(
        sort,
        "sort",
        (
            jax.ShapeDtypeStruct((total, LANES), F32),
            jax.ShapeDtypeStruct((total, LANES), BF16),
        ),
        (ints, first, *parts, shrunk),
    )
    came = send(away, lambda a, b, c: (a, b, c ^ 1))

    msg_rows = rows + rows // 2

    def add_cores(ints_ref, keep_ref, came_ref, own_out, x_out, y_out, d_out):
        side = ints_ref[2] // 2

        def tile(side_at, group_at):
            at = pl.ds(pl.multiple_of(side_at * both + group_at * rows, rows), rows)
            return keep_ref[at, :] + came_ref[at, :].astype(F32)

        def low_rank(group_at):
            at = pl.ds(pairs * both + group_at * (rows // 2), rows // 2)
            return keep_ref[at, :] + came_ref[at, :].astype(F32)

        own_out[0:rows, :] = tile(side, 0)
        x_out[0:rows, :] = tile(1 - side, 0).astype(BF16)
        y_out[0:rows, :] = tile(side, 1).astype(BF16)
        d_out[0:rows, :] = tile(1 - side, 1).astype(BF16)
        s_a, s_b = low_rank(0), low_rank(1)
        own_out[rows:, :] = s_a
        x_out[rows:, :] = s_a.astype(BF16)
        y_out[rows:, :] = s_b.astype(BF16)
        d_out[rows:, :] = s_b.astype(BF16)

    msg = jax.ShapeDtypeStruct((msg_rows, LANES), BF16)
    mine, to_x, to_y, to_d = call(
        add_cores,
        "add_cores",
        (jax.ShapeDtypeStruct((msg_rows, LANES), F32), msg, msg, msg),
        (ints, keep, came),
    )
    from_d = send(to_d, lambda a, b, c: (1 - a, b, c ^ 2))
    from_x = send(to_x, lambda a, b, c: (a, b, c ^ 2))
    from_y = send(to_y, lambda a, b, c: (1 - a, b, c))

    def ups(ints_ref, o_ref, *refs):
        p_refs, out = refs[:-1], refs[-1]
        here = ints_ref[1]
        at = half + low

        def put(ref, holder):
            out[holder] = ref[at : at + up_rows, :]

        put(o_ref, here)
        for hop in range(1, dp):
            pl.when(here >= hop)(lambda hop=hop: put(p_refs[2 * hop - 2], here - hop))
            pl.when(here + hop < dp)(lambda hop=hop: put(p_refs[2 * hop - 1], here + hop))

    up_all = call(
        ups,
        "ups",
        jax.ShapeDtypeStruct((dp, up_rows, LANES), BF16),
        (ints, own_l, *[a[h] for h in range(1, dp) for a in (rise_l, fall_l)]),
    )

    def finish(ints_ref, live_ref, up_ref, mine_ref, x_ref, y_ref, d_ref, out_ref):
        me = ints_ref[0]
        here_half = mine_ref[0:rows, :] + x_ref[0:rows, :].astype(F32)
        there_half = y_ref[0:rows, :].astype(F32) + d_ref[0:rows, :].astype(F32)
        s = mine_ref[rows:, :]
        for ref in (x_ref, y_ref, d_ref):
            s = s + ref[rows:, :].astype(F32)
        s = s.astype(BF16)
        halves = (
            jnp.where(me == 0, here_half, there_half),
            jnp.where(me == 0, there_half, here_half),
        )
        for k in range(blocks):
            slot = slot_of(ints_ref, 0, k)
            holder, local_slot = slot // per_dev, slot % per_dev
            per_lane = blocks // 2
            piece = s[
                (k % per_lane) * block_len : (k % per_lane + 1) * block_len,
                (k // per_lane) * rank : (k // per_lane + 1) * rank,
            ]
            row = lax.broadcasted_iota(jnp.int32, (block_len, LANES), 0)
            for v in range(out_cols // LANES):
                at = pl.ds(
                    pl.multiple_of((local_slot * (out_cols // LANES) + v) * rank, rank), rank
                )
                delta = jnp.dot(piece, up_ref[holder, at, :], preferred_element_type=F32)
                base = halves[v][k * block_len : (k + 1) * block_len, :]
                mixed = jnp.where(
                    row < live_ref[k], base + delta.astype(BF16).astype(F32), 0.0
                )
                out_ref[
                    k * block_len : (k + 1) * block_len, v * LANES : (v + 1) * LANES
                ] = mixed.astype(BF16)

    return pl.pallas_call(
        finish,
        name="finish",
        out_shape=jax.ShapeDtypeStruct((rows, out_cols), BF16),
        in_specs=[SMEM, SMEM] + [VMEM] * 5,
        out_specs=VMEM,
        compiler_params=pltpu.CompilerParams(vmem_limit_bytes=40 * 2**20),
    )(ints, live_rows, up_all, mine, from_x, from_y, from_d)


def local(
    tokens,
    value_weight,
    adapter_down_weight,
    adapter_up_weight,
    adapter_slot_table,
    adapter_per_block,
    request_rows_per_block,
):
    dp_count = lax.axis_size("dp")
    blocks = adapter_per_block.shape[0]
    tok_rows = tokens.shape[0]
    block_len = tok_rows // blocks
    feature_total = tokens.shape[1]
    adapter_total = adapter_down_weight.shape[0]
    adapter_rank_width = adapter_down_weight.shape[2]
    column_total = adapter_up_weight.shape[2]
    partial_value = jnp.dot(
        tokens,
        lax.all_gather(value_weight, "dp", axis=1, tiled=True),
        preferred_element_type=jnp.float32,
    )
    summed = lax.psum(partial_value.astype(jnp.bfloat16), "tensor").astype(jnp.float32)
    base_cols = lax.dynamic_slice_in_dim(
        summed, lax.axis_index("tensor") * column_total, column_total, 1
    )
    matches = (
        adapter_per_block[:, None]
        == jnp.arange(adapter_slot_table.shape[0], dtype=jnp.int32)[None, :]
    )
    slot_index = jnp.sum(jnp.where(matches, adapter_slot_table[None, :], 0), axis=1)
    holder = slot_index // adapter_total
    local_slot = slot_index % adapter_total
    route_map = (holder[None, :] == jnp.arange(dp_count, dtype=jnp.int32)[:, None]).astype(
        jnp.bfloat16
    )
    local_onehot = (
        local_slot[:, None] == jnp.arange(adapter_total, dtype=jnp.int32)[None, :]
    ).astype(jnp.bfloat16)
    wanted_hot = jnp.dot(route_map, local_onehot, preferred_element_type=jnp.bfloat16)
    block_input = tokens.reshape(blocks, block_len, feature_total)
    sent_x = jnp.dot(
        route_map,
        block_input.reshape(blocks, block_len * feature_total),
        preferred_element_type=jnp.bfloat16,
    )
    sent_x = sent_x.reshape(dp_count, block_len, feature_total)
    recv_x, recv_hot = (
        lax.all_to_all(sent_x, "dp", split_axis=0, concat_axis=0, tiled=True),
        lax.all_to_all(wanted_hot, "dp", split_axis=0, concat_axis=0, tiled=True),
    )
    flat_down_weight = jnp.transpose(adapter_down_weight, (1, 0, 2)).reshape(
        feature_total, adapter_total * adapter_rank_width
    )
    every = jnp.einsum("nbf,fq->nbq", recv_x, flat_down_weight, preferred_element_type=jnp.float32)
    every = every.reshape(dp_count, block_len, adapter_total, adapter_rank_width)
    picked = jnp.sum(every * recv_hot.astype(jnp.float32)[:, None, :, None], axis=2)
    reduced_input = lax.psum(picked.astype(jnp.bfloat16), "tensor")
    spread_rows = (recv_hot[:, None, :, None] * reduced_input[:, :, None, :]).reshape(
        dp_count, block_len, adapter_total * adapter_rank_width
    )
    flat_up_weight = adapter_up_weight.reshape(adapter_total * adapter_rank_width, column_total)
    delta_rows = jnp.einsum(
        "nbq,qc->nbc", spread_rows, flat_up_weight, preferred_element_type=jnp.float32
    ).astype(jnp.bfloat16)
    returned = lax.all_to_all(delta_rows, "dp", split_axis=0, concat_axis=0, tiled=True)
    own_delta = jnp.dot(
        route_map.T,
        returned.reshape(dp_count, block_len * column_total),
        preferred_element_type=jnp.bfloat16,
    )
    own_delta = own_delta.reshape(tok_rows, column_total)
    live_rows = (
        jnp.arange(block_len, dtype=jnp.int32)[None, :] < request_rows_per_block[:, None]
    ).reshape(tok_rows)
    mixed = jnp.where(
        live_rows[:, None], base_cols + own_delta.astype(jnp.float32), jnp.float32(0.0)
    )
    return mixed.astype(jnp.bfloat16)


def solution(mesh):
    placed = (
        P(("groups", "dp"), "tensor"),
        P("tensor", "dp"),
        P("dp", "tensor", None),
        P("dp", None, "tensor"),
        P("groups"),
        P(("groups", "dp")),
        P(("groups", "dp")),
    )
    sizes = tuple(mesh.shape[a] for a in AXES)
    if sizes == (2, 4, 4):
        body = lambda *args: local_line(sizes, *args)
    else:
        body = local
    return jax.shard_map(
        body, mesh=mesh, in_specs=placed, out_specs=P(("groups", "dp"), "tensor"), check_vma=False
    )
```

```python
import jax
import jax.numpy as jnp
from jax import lax
from jax.experimental import pallas as pl
from jax.experimental.pallas import tpu as pltpu
from jax.sharding import PartitionSpec as P

AXES = ("groups", "dp", "tensor")
LANES = 128
CODE_ROWS = 16
F32 = jnp.float32
BF16 = jnp.bfloat16
VMEM = pl.BlockSpec(memory_space=pltpu.VMEM)
SMEM = pl.BlockSpec(memory_space=pltpu.SMEM)
ANY = pl.BlockSpec(memory_space=pl.ANY)


def call(body, name, outs, specs, ins, scratch=()):
    return pl.pallas_call(
        body,
        name=name,
        out_shape=outs,
        in_specs=specs,
        out_specs=jax.tree.map(lambda _: VMEM, outs),
        scratch_shapes=scratch,
        compiler_params=pltpu.CompilerParams(vmem_limit_bytes=16 * 2**20),
    )(*ins)


def like(rows, cols, dtype=BF16):
    return jax.ShapeDtypeStruct((rows, cols), dtype)


def local_line(sizes, tokens, value_weight, down, up, slot_table, per_block, live_rows):
    groups, dp, tensor = sizes
    y, z, t = (lax.axis_index(a) for a in AXES)
    place = jnp.stack([y, z, t]).astype(jnp.int32)
    rows, feats = tokens.shape
    blocks = per_block.shape[0]
    block_len = rows // blocks
    per_dev, _, rank = down.shape
    out_cols = up.shape[2]
    half_cols = value_weight.shape[1] // groups
    half = feats // 2
    quarter = half // 2
    up_at = half + quarter
    up_rows = per_dev * rank * out_cols // LANES
    col_tiles = out_cols // LANES
    pairs = dp // 2
    both = groups * rows
    s_rows = both * rank // LANES
    total = pairs * both + s_rows
    msg_rows = rows + rows // 2

    def device(a, b, c):
        return (a * dp + b) * tensor + c

    def send(x, where, planes=range(4)):
        perm = []
        for a in range(groups):
            for b in planes:
                for c in range(tensor):
                    perm.append((device(a, b, c), device(*where(a, b, c))))
        return lax.ppermute(x, AXES, perm)

    outer, inner = (0, 3), (1, 2)

    def inward(x):
        return send(x, lambda a, b, c: (a, b ^ 1, c), outer)

    def outward(x):
        return send(x, lambda a, b, c: (a, b ^ 1, c), inner)

    def middle(x):
        return send(x, lambda a, b, c: (a, 3 - b, c), inner)

    def swap(x, planes=range(4)):
        return send(x, lambda a, b, c: (1 - a, b, c), planes)

    def pack(ints_ref, w_ref, d_ref, u_ref, l_ref, h_ref, d_held, sems):
        me = ints_ref[0]
        cols = pl.ds(pl.multiple_of(me * half_cols, LANES), half_cols)
        copies = [
            pltpu.make_async_copy(d_ref.at[me], d_held, sems.at[0]),
            pltpu.make_async_copy(w_ref.at[pl.ds(0, half), cols], l_ref.at[pl.ds(0, half)], sems.at[1]),
            pltpu.make_async_copy(w_ref.at[pl.ds(half, half), cols], h_ref.at[pl.ds(0, half)], sems.at[2]),
        ]
        for s in range(per_dev):
            for v in range(col_tiles):
                n = s * col_tiles + v
                copies.append(
                    pltpu.make_async_copy(
                        u_ref.at[s, :, pl.ds(v * LANES, LANES)],
                        l_ref.at[pl.ds(up_at + n * rank, rank)],
                        sems.at[3 + n],
                    )
                )
        for c in copies:
            c.start()
        copies[0].wait()
        for part, ref in ((0, l_ref), (1, h_ref)):
            at = part * half
            ref[half:up_at, :] = jnp.concatenate(
                [d_held[:, at : at + quarter], d_held[:, at + quarter : at + half]], axis=0
            ).T
        for c in copies[1:]:
            c.wait()

    own_l, own_h = call(
        pack,
        "pack_weights",
        (like(up_at + up_rows, LANES), like(up_at, LANES)),
        [SMEM, ANY, ANY, ANY],
        (place, value_weight, jnp.transpose(down, (0, 2, 1)), up),
        [pltpu.VMEM((rank, feats), BF16), pltpu.SemaphoreType.DMA((3 + per_dev * col_tiles,))],
    )

    def pack_tokens(table_ref, block_ref, tok_ref, low_ref, high_ref, a_ref, b_ref, sems):
        copies = [
            pltpu.make_async_copy(tok_ref.at[:, pl.ds(0, half)], low_ref.at[pl.ds(0, rows)], sems.at[0]),
            pltpu.make_async_copy(tok_ref.at[:, pl.ds(half, half)], high_ref, sems.at[1]),
            pltpu.make_async_copy(tok_ref.at[:, pl.ds(half, quarter)], a_ref.at[pl.ds(0, rows)], sems.at[2]),
            pltpu.make_async_copy(tok_ref.at[:, pl.ds(half + quarter, quarter)], b_ref, sems.at[3]),
        ]
        for c in copies:
            c.start()
        row = lax.broadcasted_iota(jnp.int32, (CODE_ROWS, half), 0)
        code = jnp.zeros((CODE_ROWS, half), jnp.int32)
        for k in range(blocks):
            code = jnp.where(row == k, table_ref[block_ref[k]], code)
        code = code.astype(F32).astype(BF16)
        low_ref[rows:, :] = code
        a_ref[rows:, :] = code[:, 0:quarter]
        for c in copies:
            c.wait()

    tok_l, tok_h, tok_a, tok_b = call(
        pack_tokens,
        "pack_tokens",
        (like(rows + CODE_ROWS, half), like(rows, half), like(rows + CODE_ROWS, quarter), like(rows, quarter)),
        [SMEM, SMEM, ANY],
        (slot_table, per_block, tokens),
        [pltpu.SemaphoreType.DMA((4,))],
    )

    mid_l = middle(own_l)
    in_l = inward(own_l)
    out_l1 = outward(own_l)
    other_l = swap(tok_l)
    mid_h = middle(own_h)
    in_a = inward(tok_a)
    in_h = inward(own_h)
    in_b = inward(tok_b)
    other_h = swap(tok_h, inner)
    out_l2 = outward(mid_l)
    far_l = middle(in_l)
    far_h = middle(in_h)
    out_l3 = outward(far_l)
    other_a = swap(in_a, inner)
    other_b = swap(in_b, inner)

    def product(tiles, w_ref):
        base = s = None
        for q, x in tiles:
            rhs = jnp.concatenate(
                [w_ref[q * quarter : (q + 1) * quarter, :], w_ref[half:up_at, :]], axis=1
            )
            got = jnp.dot(x, rhs, preferred_element_type=F32)
            b = got[:, 0:LANES]
            e = got[:, LANES + q * rank : LANES + (q + 1) * rank]
            base, s = (b, e) if base is None else (base + b, s + e)
        return base, s

    def chosen(s, code_ref, mine):
        codes = code_ref[rows : rows + CODE_ROWS, 0:LANES].astype(F32)
        pieces = []
        for k in range(blocks):
            hit = codes[k : k + 1, 0:rank] == mine
            pieces.append(jnp.where(hit, s[k * block_len : (k + 1) * block_len, :], 0.0))
        return jnp.concatenate(pieces, axis=0)

    def halves(ref):
        return [(q, ref[0:rows, q * quarter : (q + 1) * quarter]) for q in (0, 1)]

    def number(ints_ref, holder):
        return (per_dev * holder + ints_ref[0]).astype(F32)

    def where_from(here, slot):
        near = here ^ 1
        is_outer = (here == 0) | (here == 3)
        if slot == 0:
            return here
        if slot == 1:
            return near
        if slot == 2:
            return jnp.where(is_outer, 3 - near, 3 - here)
        return jnp.where(is_outer, 3 - here, 3 - near)

    def own_rows(ints_ref, toks, slot, l_ref, h_ref, out_ref, out_at, s_ref):
        mine = number(ints_ref, where_from(ints_ref[1], slot))
        for g, (low, high) in enumerate(toks):
            base, s = product(halves(low), l_ref)
            if h_ref is not None:
                b, e = product(halves(high), h_ref)
                base, s = base + b, s + e
            at = pl.ds(out_at + g * rows, rows)
            out_ref[at, :] = base
            s_ref[pl.ds(g * rows, rows), :] += chosen(s, low, mine)

    def early(ints_ref, low_a, high_a, low_b, high_b, own_l, own_h, in_l, in_h, mid_l, mid_h, out1, out2, part_ref, s_ref):
        toks = ((low_a, high_a), (low_b, high_b))
        here = ints_ref[1]
        is_outer = (here == 0) | (here == 3)
        s_ref[...] = jnp.zeros_like(s_ref)

        @pl.when(is_outer)
        def _():
            for slot, ref in enumerate((own_l, out1, out2)):
                own_rows(ints_ref, toks, slot, ref, None, part_ref, slot * both, s_ref)

        @pl.when(jnp.logical_not(is_outer))
        def _():
            for slot, (l, h) in enumerate(((own_l, own_h), (in_l, in_h), (mid_l, mid_h))):
                own_rows(ints_ref, toks, slot, l, h, part_ref, slot * both, s_ref)

    part, shrunk = call(
        early,
        "early_columns",
        (like(3 * both, LANES, F32), like(both, rank, F32)),
        [SMEM] + [VMEM] * 12,
        (place, tok_l, tok_h, other_l, other_h, own_l, own_h, in_l, in_h, mid_l, mid_h, out_l1, out_l2),
    )

    def late(
        ints_ref, low_a, high_a, low_b, high_b, na, nb, oa, ob, own_h, in_h, mid_h, far_l, far_h, out3,
        part_ref, s_in, keep, away, last_ref, s_ref, near_ref, near_s,
    ):
        toks = ((low_a, high_a), (low_b, high_b))
        here, core = ints_ref[1], ints_ref[2] % 2
        is_outer = (here == 0) | (here == 3)
        s_ref[...] = s_in[...]

        def put(ref, ref_at, holder, base):
            at = pl.ds(pl.multiple_of(base + (holder // 2) * both, both // 2), both)

            @pl.when(holder % 2 == core)
            def _():
                keep[at, :] = ref[ref_at : ref_at + both, :]

            @pl.when(holder % 2 != core)
            def _():
                away[at, :] = ref[ref_at : ref_at + both, :].astype(BF16)

        def put_shrunk(ref, base):
            for g in range(groups):
                s = jnp.concatenate(
                    [
                        ref[g * rows : g * rows + rows // 2, :],
                        ref[g * rows + rows // 2 : (g + 1) * rows, :],
                    ],
                    axis=1,
                )
                at = base + pairs * both + g * (rows // 2)
                keep[at : at + rows // 2, :] = s
                away[at : at + rows // 2, :] = s.astype(BF16)

        @pl.when(is_outer)
        def _():
            own_rows(ints_ref, toks, 3, out3, None, last_ref, 0, s_ref)

        @pl.when(jnp.logical_not(is_outer))
        def _():
            own_rows(ints_ref, toks, 3, far_l, far_h, last_ref, 0, s_ref)
            near_s[...] = jnp.zeros_like(near_s)
            for slot, w_ref in enumerate((own_h, in_h, mid_h, far_h)):
                mine = number(ints_ref, where_from(here, slot))
                for g, (a, b) in enumerate(((na, nb), (oa, ob))):
                    base, s = product([(0, a[0:rows, :]), (1, b[...])], w_ref)
                    near_ref[g * rows : (g + 1) * rows, :] = base
                    near_s[g * rows : (g + 1) * rows, :] += chosen(s, a, mine)
                put(near_ref, 0, where_from(here, slot), total)
            put_shrunk(near_s, total)

        for slot in range(3):
            put(part_ref, slot * both, where_from(here, slot), 0)
        put(last_ref, 0, where_from(here, 3), 0)
        put_shrunk(s_ref, 0)

    keep, away = call(
        late,
        "late_columns",
        (like(2 * total, LANES, F32), like(2 * total, LANES)),
        [SMEM] + [VMEM] * 16,
        (
            place, tok_l, tok_h, other_l, other_h, in_a, in_b, other_a, other_b,
            own_h, in_h, mid_h, far_l, far_h, out_l3, part, shrunk,
        ),
        [
            pltpu.VMEM((both, LANES), F32),
            pltpu.VMEM((both, rank), F32),
            pltpu.VMEM((both, LANES), F32),
            pltpu.VMEM((both, rank), F32),
        ],
    )
    came = send(away, lambda a, b, c: (a, b, c ^ 1))

    def add_cores(ints_ref, keep_ref, came_ref, own_out, *outs):
        side = ints_ref[2] // 2

        def fill(out, base, side_at, g):
            at = pl.ds(pl.multiple_of(base + side_at * both + g * rows, rows), rows)
            s_at = pl.ds(base + pairs * both + g * (rows // 2), rows // 2)
            out[0:rows, :] = (keep_ref[at, :] + came_ref[at, :].astype(F32)).astype(out.dtype)
            out[rows:, :] = (keep_ref[s_at, :] + came_ref[s_at, :].astype(F32)).astype(out.dtype)

        fill(own_out, 0, side, 0)
        for n, out in enumerate(outs[0:3]):
            flip, g = ((0, 1), (1, 0), (1, 1))[n]
            fill(out, 0, jnp.where(flip == 1, 1 - side, side), g)
        for n, out in enumerate(outs[3:]):
            flip, g = n // 2, n % 2
            fill(out, total, jnp.where(flip == 1, 1 - side, side), g)

    msg = like(msg_rows, LANES)
    mine, *sent = call(
        add_cores,
        "add_cores",
        (like(msg_rows, LANES, F32),) + (msg,) * 7,
        [SMEM, VMEM, VMEM],
        (place, keep, came),
    )
    came_msgs = []
    for flip, g, x in ((0, 0, sent[3]), (0, 1, sent[4]), (1, 0, sent[5]), (1, 1, sent[6])):
        came_msgs.append((g, send(x, lambda a, b, c: (a ^ g, b ^ 1, c ^ (2 * flip)), inner)))
    for flip, g, x in ((1, 1, sent[2]), (1, 0, sent[1]), (0, 1, sent[0])):
        came_msgs.append((g, send(x, lambda a, b, c: (a ^ g, b, c ^ (2 * flip)))))

    def ups(ints_ref, own, in_l, mid_l, far_l, out1, out2, out3, out):
        here = ints_ref[1]
        is_outer = (here == 0) | (here == 3)

        def put(ref, slot):
            out[where_from(here, slot)] = ref[up_at : up_at + up_rows, :]

        put(own, 0)

        @pl.when(is_outer)
        def _():
            for slot, ref in ((1, out1), (2, out2), (3, out3)):
                put(ref, slot)

        @pl.when(jnp.logical_not(is_outer))
        def _():
            for slot, ref in ((1, in_l), (2, mid_l), (3, far_l)):
                put(ref, slot)

    up_all = call(
        ups,
        "ups",
        jax.ShapeDtypeStruct((dp, up_rows, LANES), BF16),
        [SMEM] + [VMEM] * 7,
        (place, own_l, in_l, mid_l, far_l, out_l1, out_l2, out_l3),
    )
    groups_of = [g for g, _ in came_msgs]

    def finish(ints_ref, table_ref, block_ref, live_ref, up_ref, mine_ref, *refs):
        msgs, out_ref = refs[:-1], refs[-1]
        me = ints_ref[0]
        sums = [mine_ref[0:rows, :], jnp.zeros((rows, LANES), F32)]
        s = mine_ref[rows:, :]
        for g, ref in zip(groups_of, msgs):
            sums[g] = sums[g] + ref[0:rows, :].astype(F32)
            s = s + ref[rows:, :].astype(F32)
        s = s.astype(BF16)
        split = (jnp.where(me == 0, sums[0], sums[1]), jnp.where(me == 0, sums[1], sums[0]))
        per_lane = blocks // 2
        row = lax.broadcasted_iota(jnp.int32, (block_len, LANES), 0)
        for k in range(blocks):
            slot = table_ref[block_ref[k]]
            holder, local_slot = slot // per_dev, slot % per_dev
            piece = s[
                (k % per_lane) * block_len : (k % per_lane + 1) * block_len,
                (k // per_lane) * rank : (k // per_lane + 1) * rank,
            ]
            for v in range(col_tiles):
                at = pl.ds(pl.multiple_of((local_slot * col_tiles + v) * rank, rank), rank)
                delta = jnp.dot(piece, up_ref[holder, at, :], preferred_element_type=F32)
                base = split[v][k * block_len : (k + 1) * block_len, :]
                mixed = jnp.where(row < live_ref[k], base + delta.astype(BF16).astype(F32), 0.0)
                out_ref[
                    k * block_len : (k + 1) * block_len, v * LANES : (v + 1) * LANES
                ] = mixed.astype(BF16)

    return call(
        finish,
        "finish",
        like(rows, out_cols),
        [SMEM] * 4 + [VMEM] * 9,
        (place, slot_table, per_block, live_rows, up_all, mine, *[m for _, m in came_msgs]),
    )


def local(
    tokens,
    value_weight,
    adapter_down_weight,
    adapter_up_weight,
    adapter_slot_table,
    adapter_per_block,
    request_rows_per_block,
):
    dp_count = lax.axis_size("dp")
    blocks = adapter_per_block.shape[0]
    tok_rows = tokens.shape[0]
    block_len = tok_rows // blocks
    feature_total = tokens.shape[1]
    adapter_total = adapter_down_weight.shape[0]
    adapter_rank_width = adapter_down_weight.shape[2]
    column_total = adapter_up_weight.shape[2]
    partial_value = jnp.dot(
        tokens,
        lax.all_gather(value_weight, "dp", axis=1, tiled=True),
        preferred_element_type=jnp.float32,
    )
    summed = lax.psum(partial_value.astype(jnp.bfloat16), "tensor").astype(jnp.float32)
    base_cols = lax.dynamic_slice_in_dim(
        summed, lax.axis_index("tensor") * column_total, column_total, 1
    )
    matches = (
        adapter_per_block[:, None]
        == jnp.arange(adapter_slot_table.shape[0], dtype=jnp.int32)[None, :]
    )
    slot_index = jnp.sum(jnp.where(matches, adapter_slot_table[None, :], 0), axis=1)
    holder = slot_index // adapter_total
    local_slot = slot_index % adapter_total
    route_map = (holder[None, :] == jnp.arange(dp_count, dtype=jnp.int32)[:, None]).astype(
        jnp.bfloat16
    )
    local_onehot = (
        local_slot[:, None] == jnp.arange(adapter_total, dtype=jnp.int32)[None, :]
    ).astype(jnp.bfloat16)
    wanted_hot = jnp.dot(route_map, local_onehot, preferred_element_type=jnp.bfloat16)
    block_input = tokens.reshape(blocks, block_len, feature_total)
    sent_x = jnp.dot(
        route_map,
        block_input.reshape(blocks, block_len * feature_total),
        preferred_element_type=jnp.bfloat16,
    )
    sent_x = sent_x.reshape(dp_count, block_len, feature_total)
    recv_x, recv_hot = (
        lax.all_to_all(sent_x, "dp", split_axis=0, concat_axis=0, tiled=True),
        lax.all_to_all(wanted_hot, "dp", split_axis=0, concat_axis=0, tiled=True),
    )
    flat_down_weight = jnp.transpose(adapter_down_weight, (1, 0, 2)).reshape(
        feature_total, adapter_total * adapter_rank_width
    )
    every = jnp.einsum("nbf,fq->nbq", recv_x, flat_down_weight, preferred_element_type=jnp.float32)
    every = every.reshape(dp_count, block_len, adapter_total, adapter_rank_width)
    picked = jnp.sum(every * recv_hot.astype(jnp.float32)[:, None, :, None], axis=2)
    reduced_input = lax.psum(picked.astype(jnp.bfloat16), "tensor")
    spread_rows = (recv_hot[:, None, :, None] * reduced_input[:, :, None, :]).reshape(
        dp_count, block_len, adapter_total * adapter_rank_width
    )
    flat_up_weight = adapter_up_weight.reshape(adapter_total * adapter_rank_width, column_total)
    delta_rows = jnp.einsum(
        "nbq,qc->nbc", spread_rows, flat_up_weight, preferred_element_type=jnp.float32
    ).astype(jnp.bfloat16)
    returned = lax.all_to_all(delta_rows, "dp", split_axis=0, concat_axis=0, tiled=True)
    own_delta = jnp.dot(
        route_map.T,
        returned.reshape(dp_count, block_len * column_total),
        preferred_element_type=jnp.bfloat16,
    )
    own_delta = own_delta.reshape(tok_rows, column_total)
    live_rows = (
        jnp.arange(block_len, dtype=jnp.int32)[None, :] < request_rows_per_block[:, None]
    ).reshape(tok_rows)
    mixed = jnp.where(
        live_rows[:, None], base_cols + own_delta.astype(jnp.float32), jnp.float32(0.0)
    )
    return mixed.astype(jnp.bfloat16)


def solution(mesh):
    placed = (
        P(("groups", "dp"), "tensor"),
        P("tensor", "dp"),
        P("dp", "tensor", None),
        P("dp", None, "tensor"),
        P("groups"),
        P(("groups", "dp")),
        P(("groups", "dp")),
    )
    sizes = tuple(mesh.shape[a] for a in AXES)
    if sizes == (2, 4, 4):
        body = lambda *args: local_line(sizes, *args)
    else:
        body = local
    return jax.shard_map(
        body, mesh=mesh, in_specs=placed, out_specs=P(("groups", "dp"), "tensor"), check_vma=False
    )
```

```python
import jax
import jax.numpy as jnp
from jax import lax
from jax.experimental import pallas as pl
from jax.experimental.pallas import tpu as pltpu
from jax.sharding import PartitionSpec as P

AXES = ("groups", "dp", "tensor")
LANES = 128
CODE_ROWS = 16
F32 = jnp.float32
BF16 = jnp.bfloat16
VMEM = pl.BlockSpec(memory_space=pltpu.VMEM)
SMEM = pl.BlockSpec(memory_space=pltpu.SMEM)
HBM = pl.BlockSpec(memory_space=pltpu.HBM)


def call(body, name, outs, specs, ins, scratch=(), mib=16):
    return pl.pallas_call(
        body,
        name=name,
        out_shape=outs,
        in_specs=specs,
        out_specs=jax.tree.map(lambda _: VMEM, outs),
        scratch_shapes=scratch,
        compiler_params=pltpu.CompilerParams(vmem_limit_bytes=mib * 2**20),
    )(*ins)


def like(rows, cols, dtype=BF16):
    return jax.ShapeDtypeStruct((rows, cols), dtype)


def local_line(sizes, tokens, value_weight, down, up, slot_table, per_block, live_rows):
    groups, dp, tensor = sizes
    y, z, t = (lax.axis_index(a) for a in AXES)
    place = jnp.stack([y, z, t]).astype(jnp.int32)
    rows, feats = tokens.shape
    blocks = per_block.shape[0]
    block_len = rows // blocks
    per_dev, _, rank = down.shape
    out_cols = up.shape[2]
    half_cols = value_weight.shape[1] // groups
    half = feats // 2
    up_rows = per_dev * rank * out_cols // LANES
    col_tiles = out_cols // LANES
    pairs = dp // 2
    both = groups * rows
    s_msg = rows // 2
    total = pairs * both + 3 * s_msg

    def device(a, b, c):
        return (a * dp + b) * tensor + c

    def swap(x, where):
        perm = [
            (device(a, b, c), device(*where(a, b, c)))
            for a in range(groups)
            for b in range(dp)
            for c in range(tensor)
        ]
        return lax.ppermute(x, AXES, perm)

    def to_neighbour(x):
        return swap(x, lambda a, b, c: (a, b ^ 1, c))

    def to_middle(x):
        return swap(x, lambda a, b, c: (a, 3 - b, c) if b in (1, 2) else (a, b, c ^ 1))

    def to_group(x):
        return swap(x, lambda a, b, c: (1 - a, b, c))

    def tie(x, *earlier):
        return lax.optimization_barrier((x, *earlier))[0]

    def outer_plane(here):
        return (here == 0) | (here == 3)

    def where_from(here, slot):
        near = here ^ 1
        if slot == 0:
            return here
        if slot == 1:
            return near
        if slot == 2:
            return jnp.where(outer_plane(here), 3 - near, 3 - here)
        return jnp.where(outer_plane(here), 3 - here, 3 - near)

    def block_at(table_ref, block_ref, holder):
        which, local_slot = jnp.int32(0), jnp.int32(0)
        for k in range(blocks):
            s = table_ref[block_ref[k]]
            hit = s // per_dev == holder
            which = jnp.where(hit, k, which)
            local_slot = jnp.where(hit, s % per_dev, local_slot)
        return which, local_slot

    def pack(ints_ref, w_ref, d_ref, u_ref, wide_ref, own_ref, other_ref, d_held, sems):
        me = ints_ref[0]
        cols = pl.ds(pl.multiple_of(me * half_cols, LANES), half_cols)
        copies = [
            pltpu.make_async_copy(d_ref.at[me], d_held.at[0], sems.at[0]),
            pltpu.make_async_copy(d_ref.at[1 - me], d_held.at[1], sems.at[1]),
            pltpu.make_async_copy(w_ref.at[:, cols], wide_ref.at[pl.ds(0, feats)], sems.at[2]),
        ]
        for s in range(per_dev):
            for v in range(col_tiles):
                n = s * col_tiles + v
                copies.append(
                    pltpu.make_async_copy(
                        u_ref.at[s, :, pl.ds(v * LANES, LANES)],
                        wide_ref.at[pl.ds(feats + n * rank, rank)],
                        sems.at[3 + n],
                    )
                )
        for c in copies:
            c.start()
        for n, ref in ((0, own_ref), (1, other_ref)):
            copies[n].wait()
            ref[...] = jnp.concatenate([d_held[n, :, 0:half], d_held[n, :, half:feats]], axis=0).T
        for c in copies[2:]:
            c.wait()

    own_w, own_d, own_e = call(
        pack,
        "pack_weights",
        (like(feats + up_rows, LANES), like(half, LANES), like(half, LANES)),
        [SMEM, HBM, HBM, HBM],
        (place, value_weight, jnp.transpose(down, (0, 2, 1)), up),
        [
            pltpu.VMEM((per_dev, rank, feats), BF16),
            pltpu.SemaphoreType.DMA((3 + per_dev * col_tiles,)),
        ],
        mib=56,
    )

    tiles = feats // LANES
    tile_rows = tiles * block_len
    wide_rows = feats + up_rows
    code_at = half + tile_rows

    def pack_tokens(
        ints_ref, table_ref, block_ref, tok_ref, d_ref, sorted_ref, first_ref, second_ref, sems
    ):
        here = ints_ref[1]
        copies = []
        row = lax.broadcasted_iota(jnp.int32, (CODE_ROWS, LANES), 0)
        code = jnp.zeros((CODE_ROWS, LANES), jnp.int32)
        for slot in range(dp):
            which, local_slot = block_at(table_ref, block_ref, where_from(here, slot))
            src = tok_ref.at[pl.ds(pl.multiple_of(which * block_len, block_len), block_len)]
            to = sorted_ref.at[pl.ds(slot * block_len, block_len)]
            copies.append(pltpu.make_async_copy(src, to, sems.at[slot]))
            copies[-1].start()
            code = jnp.where(row == slot, local_slot, code)
        code = code.astype(F32).astype(BF16)
        sorted_ref[rows:, 0:LANES] = code
        first_ref[code_at : code_at + CODE_ROWS, :] = code
        first_ref[0:half, :] = d_ref[...]
        for c in copies:
            c.wait()
        for n, (ref, at) in enumerate(((first_ref, half), (second_ref, 0), (second_ref, tile_rows))):
            for i in range(tiles):
                ref[at + i * block_len : at + (i + 1) * block_len, :] = sorted_ref[
                    (n + 1) * block_len : (n + 2) * block_len, i * LANES : (i + 1) * LANES
                ]

    in_order, first, second = call(
        pack_tokens,
        "pack_blocks",
        (
            like(rows + CODE_ROWS, feats),
            like(wide_rows, LANES),
            like(wide_rows, LANES),
        ),
        [SMEM, SMEM, SMEM, HBM, VMEM],
        (place, slot_table, per_block, tokens, own_d),
        [pltpu.SemaphoreType.DMA((dp,))],
        mib=56,
    )

    def choose(ints_ref, outer_ref, inner_ref, out_ref):
        is_outer = outer_plane(ints_ref[1])

        @pl.when(is_outer)
        def _():
            out_ref[...] = outer_ref[...]

        @pl.when(jnp.logical_not(is_outer))
        def _():
            out_ref[...] = inner_ref[...]

    def chosen(x, y):
        return call(choose, "choose", like(wide_rows, LANES), [SMEM, VMEM, VMEM], (place, x, y))

    near_w = to_neighbour(own_w)
    mid_w = to_middle(own_w)
    others = to_group(in_order)
    two = to_neighbour(chosen(first, mid_w))
    far_w = to_middle(near_w)
    mid_d = to_middle(tie(own_d, near_w))
    three = to_neighbour(chosen(second, far_w))
    mid_e = to_group(tie(mid_d, others))
    far_d = to_middle(tie(two[0:half], mid_d))
    far_e = to_group(tie(far_d, mid_e))

    def columns(a_ref, b_ref, w_ref, out_ref, at):
        for g, x in enumerate((a_ref, b_ref)):
            out_ref[at + g * rows : at + (g + 1) * rows, :] = jnp.dot(
                x[0:rows, :], w_ref[0:feats, :], preferred_element_type=F32
            )

    def early(ints_ref, a_ref, b_ref, w0, w1, mid, out, part_ref):
        columns(a_ref, b_ref, w0, part_ref, 0)
        columns(a_ref, b_ref, w1, part_ref, both)
        is_outer = outer_plane(ints_ref[1])
        pl.when(is_outer)(lambda: columns(a_ref, b_ref, out, part_ref, 2 * both))
        pl.when(jnp.logical_not(is_outer))(lambda: columns(a_ref, b_ref, mid, part_ref, 2 * both))

    part = call(
        early,
        "early_columns",
        like(3 * both, LANES, F32),
        [SMEM] + [VMEM] * 6,
        (place, in_order, others, own_w, near_w, mid_w, two),
    )

    def late(
        ints_ref, a_ref, b_ref, two_ref, three_ref, d0, e0, d2, e2, d3, e3,
        far, part_ref, keep, away, last_ref, s_ref,
    ):
        me, here, core = ints_ref[0], ints_ref[1], ints_ref[2] % 2
        is_outer = outer_plane(here)

        def put(ref, ref_at, holder):
            at = pl.ds(pl.multiple_of((holder // 2) * both, both), both)

            @pl.when(holder % 2 == core)
            def _():
                keep[at, :] = ref[ref_at : ref_at + both, :]

            @pl.when(holder % 2 != core)
            def _():
                away[at, :] = ref[ref_at : ref_at + both, :].astype(BF16)

        number = me.astype(F32)
        codes = [ref[rows:, 0:LANES].astype(F32) for ref in (a_ref, b_ref)]
        near_codes = two_ref[code_at : code_at + CODE_ROWS, :].astype(F32)
        s_ref[...] = jnp.zeros_like(s_ref)

        def shrink(slot, d_ref, e_ref=None, theirs=0):
            at = slice(slot * block_len, (slot + 1) * block_len)
            x = [a_ref[at, :], b_ref[at, :]]
            rhs = d_ref[0:half, :]
            if theirs:
                ref, near_at = ((two_ref, half), (three_ref, 0), (three_ref, tile_rows))[theirs - 1]
                x.append(
                    jnp.concatenate(
                        [
                            ref[near_at + i * block_len : near_at + (i + 1) * block_len, :]
                            for i in range(tiles)
                        ],
                        axis=1,
                    )
                )
                rhs = jnp.concatenate([rhs, e_ref[...]], axis=1)
            x = jnp.concatenate(x, axis=0)
            low = jnp.dot(x[:, 0:half], rhs, preferred_element_type=F32)
            high = jnp.dot(x[:, half:feats], rhs, preferred_element_type=F32)
            mine = low[:, 0:rank] + high[:, rank : 2 * rank]
            for g in range(groups):
                hit = codes[g][slot : slot + 1, 0:rank] == number
                s_ref[g, at, :] = jnp.where(hit, mine[g * block_len : (g + 1) * block_len, :], 0.0)
            if theirs:
                last = slice(groups * block_len, (groups + 1) * block_len)
                other = (
                    low[last, LANES : LANES + rank] + high[last, LANES + rank : LANES + 2 * rank]
                )
                hit = near_codes[theirs : theirs + 1, 0:rank] == number
                s_ref[2, theirs * block_len : (theirs + 1) * block_len, :] = jnp.where(
                    hit, mine[last, :], other
                )

        @pl.when(is_outer)
        def _():
            columns(a_ref, b_ref, three_ref, last_ref, 0)
            shrink(0, d0)

        @pl.when(jnp.logical_not(is_outer))
        def _():
            columns(a_ref, b_ref, far, last_ref, 0)
            shrink(0, d0, e0, 1)
            shrink(1, two_ref)
            shrink(2, d2, e2, 2)
            shrink(3, d3, e3, 3)

        for slot in range(3):
            put(part_ref, slot * both, where_from(here, slot))
        put(last_ref, 0, where_from(here, 3))
        for g in range(3):
            s = jnp.concatenate([s_ref[g, 0:s_msg, :], s_ref[g, s_msg:rows, :]], axis=1)
            at = pairs * both + g * s_msg
            keep[at : at + s_msg, :] = s
            away[at : at + s_msg, :] = s.astype(BF16)

    keep, away = call(
        late,
        "late_columns",
        (like(total, LANES, F32), like(total, LANES)),
        [SMEM] + [VMEM] * 12,
        (
            place, in_order, others, two, three, own_d, own_e, mid_d, mid_e,
            far_d, far_e, far_w, part,
        ),
        [pltpu.VMEM((both, LANES), F32), pltpu.VMEM((3, rows, rank), F32)],
    )
    came = swap(away, lambda a, b, c: (a, b, c ^ 1))

    def add_cores(ints_ref, keep_ref, came_ref, mine_out, x_out, y_out, d_out, near_out):
        side = ints_ref[2] // 2

        def tile(out, side_at, g):
            at = pl.ds(pl.multiple_of(side_at * both + g * rows, rows), rows)
            out[0:rows, :] = (keep_ref[at, :] + came_ref[at, :].astype(F32)).astype(out.dtype)

        def low_rank(out, at, g):
            s = pl.ds(pairs * both + g * s_msg, s_msg)
            out[at : at + s_msg, :] = (keep_ref[s, :] + came_ref[s, :].astype(F32)).astype(out.dtype)

        tile(mine_out, side, 0)
        tile(x_out, 1 - side, 0)
        tile(y_out, side, 1)
        tile(d_out, 1 - side, 1)
        low_rank(mine_out, rows, 0)
        low_rank(x_out, rows, 0)
        low_rank(y_out, rows, 1)
        low_rank(d_out, rows, 1)
        low_rank(near_out, 0, 2)

    mine, to_x, to_y, to_d, to_near = call(
        add_cores,
        "add_cores",
        (
            like(rows + s_msg, LANES, F32),
            like(rows + s_msg, LANES),
            like(rows + s_msg, LANES),
            like(rows + s_msg, LANES),
            like(s_msg, LANES),
        ),
        [SMEM, VMEM, VMEM],
        (place, keep, came),
    )
    from_d = swap(to_d, lambda a, b, c: (1 - a, b, c ^ 2))
    from_nearx = swap(to_near, lambda a, b, c: (a, b ^ 1, c ^ 2))
    from_x = swap(to_x, lambda a, b, c: (a, b, c ^ 2))
    from_y = to_group(to_y)
    from_near = to_neighbour(to_near)

    def ups(ints_ref, own, near, mid, far, out2, out3, out):
        here = ints_ref[1]
        is_outer = outer_plane(here)

        def put(ref, slot):
            out[where_from(here, slot)] = ref[feats : feats + up_rows, :]

        put(own, 0)
        put(near, 1)

        @pl.when(is_outer)
        def _():
            put(out2, 2)
            put(out3, 3)

        @pl.when(jnp.logical_not(is_outer))
        def _():
            put(mid, 2)
            put(far, 3)

    up_all = call(
        ups,
        "ups",
        jax.ShapeDtypeStruct((dp, up_rows, LANES), BF16),
        [SMEM] + [VMEM] * 6,
        (place, own_w, near_w, mid_w, far_w, two, three),
    )

    def finish(
        ints_ref, table_ref, block_ref, live_ref, up_ref, mine_ref, x_ref, y_ref, d_ref, n_ref,
        nx_ref, out_ref,
    ):
        me, here = ints_ref[0], ints_ref[1]
        ours = mine_ref[0:rows, :] + x_ref[0:rows, :].astype(F32)
        theirs = y_ref[0:rows, :].astype(F32) + d_ref[0:rows, :].astype(F32)
        split = (jnp.where(me == 0, ours, theirs), jnp.where(me == 0, theirs, ours))
        s = mine_ref[rows:, :] + n_ref[...].astype(F32) + nx_ref[...].astype(F32)
        for ref in (x_ref, y_ref, d_ref):
            s = s + ref[rows:, :].astype(F32)
        s = s.astype(BF16)
        per_lane = dp // 2
        row = lax.broadcasted_iota(jnp.int32, (block_len, LANES), 0)
        for slot in range(dp):
            holder = where_from(here, slot)
            which, local_slot = block_at(table_ref, block_ref, holder)
            piece = s[
                (slot % per_lane) * block_len : (slot % per_lane + 1) * block_len,
                (slot // per_lane) * rank : (slot // per_lane + 1) * rank,
            ]
            to = pl.ds(pl.multiple_of(which * block_len, block_len), block_len)
            for v in range(col_tiles):
                at = pl.ds(pl.multiple_of((local_slot * col_tiles + v) * rank, rank), rank)
                delta = jnp.dot(piece, up_ref[holder, at, :], preferred_element_type=F32)
                base = split[v][slot * block_len : (slot + 1) * block_len, :]
                mixed = jnp.where(row < live_ref[which], base + delta.astype(BF16).astype(F32), 0.0)
                out_ref[to, v * LANES : (v + 1) * LANES] = mixed.astype(BF16)

    return call(
        finish,
        "finish",
        like(rows, out_cols),
        [SMEM] * 4 + [VMEM] * 7,
        (
            place, slot_table, per_block, live_rows, up_all, mine, from_x, from_y, from_d,
            from_near, from_nearx,
        ),
    )


def local(
    tokens,
    value_weight,
    adapter_down_weight,
    adapter_up_weight,
    adapter_slot_table,
    adapter_per_block,
    request_rows_per_block,
):
    dp_count = lax.axis_size("dp")
    blocks = adapter_per_block.shape[0]
    tok_rows = tokens.shape[0]
    block_len = tok_rows // blocks
    feature_total = tokens.shape[1]
    adapter_total = adapter_down_weight.shape[0]
    adapter_rank_width = adapter_down_weight.shape[2]
    column_total = adapter_up_weight.shape[2]
    partial_value = jnp.dot(
        tokens,
        lax.all_gather(value_weight, "dp", axis=1, tiled=True),
        preferred_element_type=jnp.float32,
    )
    summed = lax.psum(partial_value.astype(jnp.bfloat16), "tensor").astype(jnp.float32)
    base_cols = lax.dynamic_slice_in_dim(
        summed, lax.axis_index("tensor") * column_total, column_total, 1
    )
    matches = (
        adapter_per_block[:, None]
        == jnp.arange(adapter_slot_table.shape[0], dtype=jnp.int32)[None, :]
    )
    slot_index = jnp.sum(jnp.where(matches, adapter_slot_table[None, :], 0), axis=1)
    holder = slot_index // adapter_total
    local_slot = slot_index % adapter_total
    route_map = (holder[None, :] == jnp.arange(dp_count, dtype=jnp.int32)[:, None]).astype(
        jnp.bfloat16
    )
    local_onehot = (
        local_slot[:, None] == jnp.arange(adapter_total, dtype=jnp.int32)[None, :]
    ).astype(jnp.bfloat16)
    wanted_hot = jnp.dot(route_map, local_onehot, preferred_element_type=jnp.bfloat16)
    block_input = tokens.reshape(blocks, block_len, feature_total)
    sent_x = jnp.dot(
        route_map,
        block_input.reshape(blocks, block_len * feature_total),
        preferred_element_type=jnp.bfloat16,
    )
    sent_x = sent_x.reshape(dp_count, block_len, feature_total)
    recv_x, recv_hot = (
        lax.all_to_all(sent_x, "dp", split_axis=0, concat_axis=0, tiled=True),
        lax.all_to_all(wanted_hot, "dp", split_axis=0, concat_axis=0, tiled=True),
    )
    flat_down_weight = jnp.transpose(adapter_down_weight, (1, 0, 2)).reshape(
        feature_total, adapter_total * adapter_rank_width
    )
    every = jnp.einsum("nbf,fq->nbq", recv_x, flat_down_weight, preferred_element_type=jnp.float32)
    every = every.reshape(dp_count, block_len, adapter_total, adapter_rank_width)
    picked = jnp.sum(every * recv_hot.astype(jnp.float32)[:, None, :, None], axis=2)
    reduced_input = lax.psum(picked.astype(jnp.bfloat16), "tensor")
    spread_rows = (recv_hot[:, None, :, None] * reduced_input[:, :, None, :]).reshape(
        dp_count, block_len, adapter_total * adapter_rank_width
    )
    flat_up_weight = adapter_up_weight.reshape(adapter_total * adapter_rank_width, column_total)
    delta_rows = jnp.einsum(
        "nbq,qc->nbc", spread_rows, flat_up_weight, preferred_element_type=jnp.float32
    ).astype(jnp.bfloat16)
    returned = lax.all_to_all(delta_rows, "dp", split_axis=0, concat_axis=0, tiled=True)
    own_delta = jnp.dot(
        route_map.T,
        returned.reshape(dp_count, block_len * column_total),
        preferred_element_type=jnp.bfloat16,
    )
    own_delta = own_delta.reshape(tok_rows, column_total)
    live_rows = (
        jnp.arange(block_len, dtype=jnp.int32)[None, :] < request_rows_per_block[:, None]
    ).reshape(tok_rows)
    mixed = jnp.where(
        live_rows[:, None], base_cols + own_delta.astype(jnp.float32), jnp.float32(0.0)
    )
    return mixed.astype(jnp.bfloat16)


def solution(mesh):
    placed = (
        P(("groups", "dp"), "tensor"),
        P("tensor", "dp"),
        P("dp", "tensor", None),
        P("dp", None, "tensor"),
        P("groups"),
        P(("groups", "dp")),
        P(("groups", "dp")),
    )
    sizes = tuple(mesh.shape[a] for a in AXES)
    if sizes == (2, 4, 4):
        body = lambda *args: local_line(sizes, *args)
    else:
        body = local
    return jax.shard_map(
        body, mesh=mesh, in_specs=placed, out_specs=P(("groups", "dp"), "tensor"), check_vma=False
    )
```

```python
import jax
import jax.numpy as jnp
from jax import lax
from jax.experimental import pallas as pl
from jax.experimental.pallas import tpu as pltpu
from jax.sharding import PartitionSpec as P

AXES = ("groups", "dp", "tensor")
LANES = 128
CODE_ROWS = 16
F32 = jnp.float32
BF16 = jnp.bfloat16
VMEM = pl.BlockSpec(memory_space=pltpu.VMEM)
SMEM = pl.BlockSpec(memory_space=pltpu.SMEM)
HBM = pl.BlockSpec(memory_space=pltpu.HBM)


def call(body, name, outs, specs, ins, scratch=(), mib=16):
    return pl.pallas_call(
        body,
        name=name,
        out_shape=outs,
        in_specs=specs,
        out_specs=jax.tree.map(lambda _: VMEM, outs),
        scratch_shapes=scratch,
        compiler_params=pltpu.CompilerParams(vmem_limit_bytes=mib * 2**20),
    )(*ins)


def like(rows, cols, dtype=BF16):
    return jax.ShapeDtypeStruct((rows, cols), dtype)


def local_line(sizes, tokens, value_weight, down, up, slot_table, per_block, live_rows):
    groups, dp, tensor = sizes
    y, z, t = (lax.axis_index(a) for a in AXES)
    place = jnp.stack([y, z, t]).astype(jnp.int32)
    rows, feats = tokens.shape
    blocks = per_block.shape[0]
    block_len = rows // blocks
    per_dev, _, rank = down.shape
    out_cols = up.shape[2]
    half_cols = value_weight.shape[1] // groups
    half = feats // 2
    up_rows = per_dev * rank * out_cols // LANES
    col_tiles = out_cols // LANES
    pairs = dp // 2
    both = groups * rows
    s_msg = rows // 2

    def device(a, b, c):
        return (a * dp + b) * tensor + c

    def swap(x, where):
        perm = [
            (device(a, b, c), device(*where(a, b, c)))
            for a in range(groups)
            for b in range(dp)
            for c in range(tensor)
        ]
        return lax.ppermute(x, AXES, perm)

    def to_neighbour(x):
        return swap(x, lambda a, b, c: (a, b ^ 1, c))

    def to_middle(x):
        return swap(x, lambda a, b, c: (a, 3 - b, c) if b in (1, 2) else (a, b, c ^ 1))

    def to_group(x):
        return swap(x, lambda a, b, c: (1 - a, b, c))

    def tie(x, *earlier):
        return lax.optimization_barrier((x, *earlier))[0]

    def outer_plane(here):
        return (here == 0) | (here == 3)

    def where_from(here, slot):
        near = here ^ 1
        if slot == 0:
            return here
        if slot == 1:
            return near
        if slot == 2:
            return jnp.where(outer_plane(here), 3 - near, 3 - here)
        return jnp.where(outer_plane(here), 3 - here, 3 - near)

    def block_at(table_ref, block_ref, holder):
        which, local_slot = jnp.int32(0), jnp.int32(0)
        for k in range(blocks):
            s = table_ref[block_ref[k]]
            hit = s // per_dev == holder
            which = jnp.where(hit, k, which)
            local_slot = jnp.where(hit, s % per_dev, local_slot)
        return which, local_slot

    def pack_columns(ints_ref, w_ref, u_ref, wide_ref, sems):
        me = ints_ref[0]
        cols = pl.ds(pl.multiple_of(me * half_cols, LANES), half_cols)
        copies = [
            pltpu.make_async_copy(w_ref.at[:, cols], wide_ref.at[pl.ds(0, feats)], sems.at[0]),
        ]
        for s in range(per_dev):
            for v in range(col_tiles):
                n = s * col_tiles + v
                copies.append(
                    pltpu.make_async_copy(
                        u_ref.at[s, :, pl.ds(v * LANES, LANES)],
                        wide_ref.at[pl.ds(feats + n * rank, rank)],
                        sems.at[1 + n],
                    )
                )
        for c in copies:
            c.start()
        for c in copies:
            c.wait()

    own_w = call(
        pack_columns,
        "pack_columns",
        like(feats + up_rows, LANES),
        [SMEM, HBM, HBM],
        (place, value_weight, up),
        [pltpu.SemaphoreType.DMA((1 + per_dev * col_tiles,))],
        mib=16,
    )

    tiles = feats // LANES
    tile_rows = tiles * block_len
    wide_rows = feats + up_rows
    code_at = half + tile_rows

    def sort_blocks(ints_ref, table_ref, block_ref, tok_ref, sorted_ref, sems):
        here = ints_ref[1]
        copies = []
        row = lax.broadcasted_iota(jnp.int32, (CODE_ROWS, LANES), 0)
        code = jnp.zeros((CODE_ROWS, LANES), jnp.int32)
        for slot in range(dp):
            which, local_slot = block_at(table_ref, block_ref, where_from(here, slot))
            src = tok_ref.at[pl.ds(pl.multiple_of(which * block_len, block_len), block_len)]
            to = sorted_ref.at[pl.ds(slot * block_len, block_len)]
            copies.append(pltpu.make_async_copy(src, to, sems.at[slot]))
            copies[-1].start()
            code = jnp.where(row == slot, local_slot, code)
        sorted_ref[rows:, 0:LANES] = code.astype(F32).astype(BF16)
        for c in copies:
            c.wait()

    in_order = call(
        sort_blocks,
        "sort_blocks",
        like(rows + CODE_ROWS, feats),
        [SMEM, SMEM, SMEM, HBM],
        (place, slot_table, per_block, tokens),
        [pltpu.SemaphoreType.DMA((dp,))],
        mib=16,
    )

    def pack_shrinks(ints_ref, sorted_ref, d_ref, own_ref, other_ref, first_ref, second_ref):
        me = ints_ref[0]
        for which, ref in ((me, own_ref), (1 - me, other_ref)):
            d = d_ref[which]
            ref[...] = jnp.concatenate([d[:, 0:half], d[:, half:feats]], axis=0).T
        first_ref[0:half, :] = own_ref[...]
        first_ref[code_at : code_at + CODE_ROWS, :] = sorted_ref[rows:, 0:LANES]
        for n, (ref, at) in enumerate(((first_ref, half), (second_ref, 0), (second_ref, tile_rows))):
            for i in range(tiles):
                ref[at + i * block_len : at + (i + 1) * block_len, :] = sorted_ref[
                    (n + 1) * block_len : (n + 2) * block_len, i * LANES : (i + 1) * LANES
                ]

    own_d, own_e, first, second = call(
        pack_shrinks,
        "pack_shrinks",
        (like(half, LANES), like(half, LANES), like(wide_rows, LANES), like(wide_rows, LANES)),
        [SMEM, VMEM, VMEM],
        (place, in_order, jnp.transpose(down, (0, 2, 1))),
    )

    def choose(ints_ref, outer_ref, inner_ref, out_ref):
        is_outer = outer_plane(ints_ref[1])

        @pl.when(is_outer)
        def _():
            out_ref[...] = outer_ref[...]

        @pl.when(jnp.logical_not(is_outer))
        def _():
            out_ref[...] = inner_ref[...]

    def chosen(x, y):
        return call(choose, "choose", like(wide_rows, LANES), [SMEM, VMEM, VMEM], (place, x, y))

    near_w = to_neighbour(own_w)
    mid_w = to_middle(own_w)
    others = to_group(in_order)
    two = to_neighbour(chosen(first, mid_w))
    far_w = to_middle(near_w)
    mid_d = to_middle(tie(own_d, near_w))
    three = to_neighbour(chosen(second, far_w))
    mid_e = to_group(tie(mid_d, others))
    far_d = to_middle(two[0:half])
    far_e = to_group(tie(far_d, mid_e))

    def columns(a_ref, b_ref, w_ref, out_ref, at):
        for g, x in enumerate((a_ref, b_ref)):
            out_ref[at + g * rows : at + (g + 1) * rows, :] = jnp.dot(
                x[0:rows, :], w_ref[0:feats, :], preferred_element_type=F32
            )

    def shrinker(me, a_ref, b_ref, two_ref, three_ref, s_ref):
        number = me.astype(F32)
        codes = [ref[rows:, 0:LANES].astype(F32) for ref in (a_ref, b_ref)]
        near_codes = two_ref[code_at : code_at + CODE_ROWS, :].astype(F32)

        def shrink(slot, d_ref, e_ref=None, theirs=0):
            at = slice(slot * block_len, (slot + 1) * block_len)
            x = [a_ref[at, :], b_ref[at, :]]
            rhs = d_ref[0:half, :]
            if theirs:
                ref = two_ref if theirs == 1 else three_ref
                near_at = (half, 0, tile_rows)[theirs - 1]
                x.append(
                    jnp.concatenate(
                        [
                            ref[near_at + i * block_len : near_at + (i + 1) * block_len, :]
                            for i in range(tiles)
                        ],
                        axis=1,
                    )
                )
                rhs = jnp.concatenate([rhs, e_ref[...]], axis=1)
            x = jnp.concatenate(x, axis=0)
            low = jnp.dot(x[:, 0:half], rhs, preferred_element_type=F32)
            high = jnp.dot(x[:, half:feats], rhs, preferred_element_type=F32)
            mine = low[:, 0:rank] + high[:, rank : 2 * rank]
            for g in range(groups):
                hit = codes[g][slot : slot + 1, 0:rank] == number
                s_ref[g, at, :] = jnp.where(hit, mine[g * block_len : (g + 1) * block_len, :], 0.0)
            if theirs:
                last = slice(groups * block_len, (groups + 1) * block_len)
                other = (
                    low[last, LANES : LANES + rank] + high[last, LANES + rank : LANES + 2 * rank]
                )
                hit = near_codes[theirs : theirs + 1, 0:rank] == number
                s_ref[2, theirs * block_len : (theirs + 1) * block_len, :] = jnp.where(
                    hit, mine[last, :], other
                )

        return shrink

    def early(ints_ref, a_ref, b_ref, w0, w1, mid, two_ref, d0, e0, part_ref, s_ref):
        columns(a_ref, b_ref, w0, part_ref, 0)
        columns(a_ref, b_ref, w1, part_ref, both)
        is_outer = outer_plane(ints_ref[1])
        shrink = shrinker(ints_ref[0], a_ref, b_ref, two_ref, None, s_ref)
        s_ref[...] = jnp.zeros_like(s_ref)

        @pl.when(is_outer)
        def _():
            columns(a_ref, b_ref, two_ref, part_ref, 2 * both)
            shrink(0, d0)

        @pl.when(jnp.logical_not(is_outer))
        def _():
            columns(a_ref, b_ref, mid, part_ref, 2 * both)
            shrink(0, d0, e0, 1)
            shrink(1, two_ref)

    s_shape = jax.ShapeDtypeStruct((3, rows, rank), F32)
    part, shrunk = call(
        early,
        "early_columns",
        (like(3 * both, LANES, F32), s_shape),
        [SMEM] + [VMEM] * 8,
        (place, in_order, others, own_w, near_w, mid_w, two, own_d, own_e),
    )

    def last_columns(ints_ref, a_ref, b_ref, three_ref, far, part_ref, keep, away, last_ref):
        here, core = ints_ref[1], ints_ref[2] % 2
        is_outer = outer_plane(here)

        def put(ref, ref_at, holder):
            at = pl.ds(pl.multiple_of((holder // 2) * both, both), both)

            @pl.when(holder % 2 == core)
            def _():
                keep[at, :] = ref[ref_at : ref_at + both, :]

            @pl.when(holder % 2 != core)
            def _():
                away[at, :] = ref[ref_at : ref_at + both, :].astype(BF16)

        pl.when(is_outer)(lambda: columns(a_ref, b_ref, three_ref, last_ref, 0))
        pl.when(jnp.logical_not(is_outer))(lambda: columns(a_ref, b_ref, far, last_ref, 0))
        for slot in range(3):
            put(part_ref, slot * both, where_from(here, slot))
        put(last_ref, 0, where_from(here, 3))

    keep, away = call(
        last_columns,
        "last_columns",
        (like(pairs * both, LANES, F32), like(pairs * both, LANES)),
        [SMEM] + [VMEM] * 5,
        (place, in_order, others, three, far_w, part),
        [pltpu.VMEM((both, LANES), F32)],
    )
    came = swap(away, lambda a, b, c: (a, b, c ^ 1))

    def last_shrinks(ints_ref, a_ref, b_ref, two_ref, three_ref, d2, e2, d3, e3, s_in, keep, away, s_ref):
        shrink = shrinker(ints_ref[0], a_ref, b_ref, two_ref, three_ref, s_ref)
        s_ref[...] = s_in[...]

        @pl.when(jnp.logical_not(outer_plane(ints_ref[1])))
        def _():
            shrink(2, d2, e2, 2)
            shrink(3, d3, e3, 3)

        for g in range(3):
            s = jnp.concatenate([s_ref[g, 0:s_msg, :], s_ref[g, s_msg:rows, :]], axis=1)
            keep[g * s_msg : (g + 1) * s_msg, :] = s
            away[g * s_msg : (g + 1) * s_msg, :] = s.astype(BF16)

    s_keep, s_away = call(
        last_shrinks,
        "last_shrinks",
        (like(3 * s_msg, LANES, F32), like(3 * s_msg, LANES)),
        [SMEM] + [VMEM] * 9,
        (place, in_order, others, two, three, mid_d, mid_e, far_d, far_e, shrunk),
        [pltpu.VMEM((3, rows, rank), F32)],
    )
    s_came = swap(s_away, lambda a, b, c: (a, b, c ^ 1))

    def add_cores(
        ints_ref, keep_ref, came_ref, s_keep, s_came, mine_out, x_out, y_out, d_out, near_out,
    ):
        side = ints_ref[2] // 2

        def tile(out, side_at, g):
            at = pl.ds(pl.multiple_of(side_at * both + g * rows, rows), rows)
            out[0:rows, :] = (keep_ref[at, :] + came_ref[at, :].astype(F32)).astype(out.dtype)

        def low_rank(out, at, g):
            s = pl.ds(g * s_msg, s_msg)
            out[at : at + s_msg, :] = (s_keep[s, :] + s_came[s, :].astype(F32)).astype(out.dtype)

        tile(mine_out, side, 0)
        tile(x_out, 1 - side, 0)
        tile(y_out, side, 1)
        tile(d_out, 1 - side, 1)
        low_rank(mine_out, rows, 0)
        low_rank(x_out, rows, 0)
        low_rank(y_out, rows, 1)
        low_rank(d_out, rows, 1)
        low_rank(near_out, 0, 2)

    mine, to_x, to_y, to_d, to_near = call(
        add_cores,
        "add_cores",
        (
            like(rows + s_msg, LANES, F32),
            like(rows + s_msg, LANES),
            like(rows + s_msg, LANES),
            like(rows + s_msg, LANES),
            like(s_msg, LANES),
        ),
        [SMEM] + [VMEM] * 4,
        (place, keep, came, s_keep, s_came),
    )
    from_d = swap(to_d, lambda a, b, c: (1 - a, b, c ^ 2))
    from_nearx = swap(to_near, lambda a, b, c: (a, b ^ 1, c ^ 2))
    from_x = swap(to_x, lambda a, b, c: (a, b, c ^ 2))
    from_y = to_group(to_y)
    from_near = to_neighbour(to_near)

    def ups(ints_ref, own, near, mid, far, out2, out3, out):
        here = ints_ref[1]
        is_outer = outer_plane(here)

        def put(ref, slot):
            out[where_from(here, slot)] = ref[feats : feats + up_rows, :]

        put(own, 0)
        put(near, 1)

        @pl.when(is_outer)
        def _():
            put(out2, 2)
            put(out3, 3)

        @pl.when(jnp.logical_not(is_outer))
        def _():
            put(mid, 2)
            put(far, 3)

    up_all = call(
        ups,
        "ups",
        jax.ShapeDtypeStruct((dp, up_rows, LANES), BF16),
        [SMEM] + [VMEM] * 6,
        (place, own_w, near_w, mid_w, far_w, two, three),
    )

    def finish(
        ints_ref, table_ref, block_ref, live_ref, up_ref, mine_ref, x_ref, y_ref, d_ref, n_ref,
        nx_ref, out_ref,
    ):
        me, here = ints_ref[0], ints_ref[1]
        ours = mine_ref[0:rows, :] + x_ref[0:rows, :].astype(F32)
        theirs = y_ref[0:rows, :].astype(F32) + d_ref[0:rows, :].astype(F32)
        split = (jnp.where(me == 0, ours, theirs), jnp.where(me == 0, theirs, ours))
        s = mine_ref[rows:, :] + n_ref[...].astype(F32) + nx_ref[...].astype(F32)
        for ref in (x_ref, y_ref, d_ref):
            s = s + ref[rows:, :].astype(F32)
        s = s.astype(BF16)
        per_lane = dp // 2
        row = lax.broadcasted_iota(jnp.int32, (block_len, LANES), 0)
        for slot in range(dp):
            holder = where_from(here, slot)
            which, local_slot = block_at(table_ref, block_ref, holder)
            piece = s[
                (slot % per_lane) * block_len : (slot % per_lane + 1) * block_len,
                (slot // per_lane) * rank : (slot // per_lane + 1) * rank,
            ]
            to = pl.ds(pl.multiple_of(which * block_len, block_len), block_len)
            for v in range(col_tiles):
                at = pl.ds(pl.multiple_of((local_slot * col_tiles + v) * rank, rank), rank)
                delta = jnp.dot(piece, up_ref[holder, at, :], preferred_element_type=F32)
                base = split[v][slot * block_len : (slot + 1) * block_len, :]
                mixed = jnp.where(row < live_ref[which], base + delta.astype(BF16).astype(F32), 0.0)
                out_ref[to, v * LANES : (v + 1) * LANES] = mixed.astype(BF16)

    return call(
        finish,
        "finish",
        like(rows, out_cols),
        [SMEM] * 4 + [VMEM] * 7,
        (
            place, slot_table, per_block, live_rows, up_all, mine, from_x, from_y, from_d,
            from_near, from_nearx,
        ),
    )


def local(
    tokens,
    value_weight,
    adapter_down_weight,
    adapter_up_weight,
    adapter_slot_table,
    adapter_per_block,
    request_rows_per_block,
):
    dp_count = lax.axis_size("dp")
    blocks = adapter_per_block.shape[0]
    tok_rows = tokens.shape[0]
    block_len = tok_rows // blocks
    feature_total = tokens.shape[1]
    adapter_total = adapter_down_weight.shape[0]
    adapter_rank_width = adapter_down_weight.shape[2]
    column_total = adapter_up_weight.shape[2]
    partial_value = jnp.dot(
        tokens,
        lax.all_gather(value_weight, "dp", axis=1, tiled=True),
        preferred_element_type=jnp.float32,
    )
    summed = lax.psum(partial_value.astype(jnp.bfloat16), "tensor").astype(jnp.float32)
    base_cols = lax.dynamic_slice_in_dim(
        summed, lax.axis_index("tensor") * column_total, column_total, 1
    )
    matches = (
        adapter_per_block[:, None]
        == jnp.arange(adapter_slot_table.shape[0], dtype=jnp.int32)[None, :]
    )
    slot_index = jnp.sum(jnp.where(matches, adapter_slot_table[None, :], 0), axis=1)
    holder = slot_index // adapter_total
    local_slot = slot_index % adapter_total
    route_map = (holder[None, :] == jnp.arange(dp_count, dtype=jnp.int32)[:, None]).astype(
        jnp.bfloat16
    )
    local_onehot = (
        local_slot[:, None] == jnp.arange(adapter_total, dtype=jnp.int32)[None, :]
    ).astype(jnp.bfloat16)
    wanted_hot = jnp.dot(route_map, local_onehot, preferred_element_type=jnp.bfloat16)
    block_input = tokens.reshape(blocks, block_len, feature_total)
    sent_x = jnp.dot(
        route_map,
        block_input.reshape(blocks, block_len * feature_total),
        preferred_element_type=jnp.bfloat16,
    )
    sent_x = sent_x.reshape(dp_count, block_len, feature_total)
    recv_x, recv_hot = (
        lax.all_to_all(sent_x, "dp", split_axis=0, concat_axis=0, tiled=True),
        lax.all_to_all(wanted_hot, "dp", split_axis=0, concat_axis=0, tiled=True),
    )
    flat_down_weight = jnp.transpose(adapter_down_weight, (1, 0, 2)).reshape(
        feature_total, adapter_total * adapter_rank_width
    )
    every = jnp.einsum("nbf,fq->nbq", recv_x, flat_down_weight, preferred_element_type=jnp.float32)
    every = every.reshape(dp_count, block_len, adapter_total, adapter_rank_width)
    picked = jnp.sum(every * recv_hot.astype(jnp.float32)[:, None, :, None], axis=2)
    reduced_input = lax.psum(picked.astype(jnp.bfloat16), "tensor")
    spread_rows = (recv_hot[:, None, :, None] * reduced_input[:, :, None, :]).reshape(
        dp_count, block_len, adapter_total * adapter_rank_width
    )
    flat_up_weight = adapter_up_weight.reshape(adapter_total * adapter_rank_width, column_total)
    delta_rows = jnp.einsum(
        "nbq,qc->nbc", spread_rows, flat_up_weight, preferred_element_type=jnp.float32
    ).astype(jnp.bfloat16)
    returned = lax.all_to_all(delta_rows, "dp", split_axis=0, concat_axis=0, tiled=True)
    own_delta = jnp.dot(
        route_map.T,
        returned.reshape(dp_count, block_len * column_total),
        preferred_element_type=jnp.bfloat16,
    )
    own_delta = own_delta.reshape(tok_rows, column_total)
    live_rows = (
        jnp.arange(block_len, dtype=jnp.int32)[None, :] < request_rows_per_block[:, None]
    ).reshape(tok_rows)
    mixed = jnp.where(
        live_rows[:, None], base_cols + own_delta.astype(jnp.float32), jnp.float32(0.0)
    )
    return mixed.astype(jnp.bfloat16)


def solution(mesh):
    placed = (
        P(("groups", "dp"), "tensor"),
        P("tensor", "dp"),
        P("dp", "tensor", None),
        P("dp", None, "tensor"),
        P("groups"),
        P(("groups", "dp")),
        P(("groups", "dp")),
    )
    sizes = tuple(mesh.shape[a] for a in AXES)
    if sizes == (2, 4, 4):
        body = lambda *args: local_line(sizes, *args)
    else:
        body = local
    return jax.shard_map(
        body, mesh=mesh, in_specs=placed, out_specs=P(("groups", "dp"), "tensor"), check_vma=False
    )
```

```python
import jax
import jax.numpy as jnp
from jax import lax
from jax.experimental import pallas as pl
from jax.experimental.pallas import tpu as pltpu
from jax.sharding import PartitionSpec as P

AXES = ("groups", "dp", "tensor")
LANES = 128
CODE_ROWS = 16
F32 = jnp.float32
BF16 = jnp.bfloat16
VMEM = pl.BlockSpec(memory_space=pltpu.VMEM)
SMEM = pl.BlockSpec(memory_space=pltpu.SMEM)
HBM = pl.BlockSpec(memory_space=pltpu.HBM)


class Place:
    def __getitem__(self, n):
        return lax.axis_index(AXES[n]).astype(jnp.int32)


def call(body, name, outs, specs, ins, scratch=(), mib=16):
    return pl.pallas_call(
        lambda *refs: body(Place(), *refs),
        name=name,
        out_shape=outs,
        in_specs=specs,
        out_specs=jax.tree.map(lambda _: VMEM, outs),
        scratch_shapes=scratch,
        compiler_params=pltpu.CompilerParams(vmem_limit_bytes=mib * 2**20),
    )(*ins)


def like(rows, cols, dtype=BF16):
    return jax.ShapeDtypeStruct((rows, cols), dtype)


def local_line(sizes, tokens, value_weight, down, up, slot_table, per_block, live_rows):
    groups, dp, tensor = sizes
    rows, feats = tokens.shape
    blocks = per_block.shape[0]
    block_len = rows // blocks
    per_dev, _, rank = down.shape
    out_cols = up.shape[2]
    half_cols = value_weight.shape[1] // groups
    half = feats // 2
    up_rows = per_dev * rank * out_cols // LANES
    col_tiles = out_cols // LANES
    pairs = dp // 2
    both = groups * rows
    s_msg = rows // 2

    def device(a, b, c):
        return (a * dp + b) * tensor + c

    def swap(x, where):
        perm = [
            (device(a, b, c), device(*where(a, b, c)))
            for a in range(groups)
            for b in range(dp)
            for c in range(tensor)
        ]
        return lax.ppermute(x, AXES, perm)

    def to_neighbour(x):
        return swap(x, lambda a, b, c: (a, b ^ 1, c))

    def to_middle(x):
        return swap(x, lambda a, b, c: (a, 3 - b, c) if b in (1, 2) else (a, b, c ^ 1))

    def to_group(x):
        return swap(x, lambda a, b, c: (1 - a, b, c))

    def tie(x, *earlier):
        return lax.optimization_barrier((x, *earlier))[0]

    def outer_plane(here):
        return (here == 0) | (here == 3)

    def where_from(here, slot):
        near = here ^ 1
        if slot == 0:
            return here
        if slot == 1:
            return near
        if slot == 2:
            return jnp.where(outer_plane(here), 3 - near, 3 - here)
        return jnp.where(outer_plane(here), 3 - here, 3 - near)

    adapters = slot_table.shape[0]
    info = jnp.concatenate([slot_table, per_block, live_rows])

    def block_at(info_ref, holder):
        which, local_slot = jnp.int32(0), jnp.int32(0)
        for k in range(blocks):
            s = info_ref[info_ref[adapters + k]]
            hit = s // per_dev == holder
            which = jnp.where(hit, k, which)
            local_slot = jnp.where(hit, s % per_dev, local_slot)
        return which, local_slot

    def pack_columns(ints_ref, w_ref, u_ref, wide_ref, sems):
        me = ints_ref[0]
        cols = pl.ds(pl.multiple_of(me * half_cols, LANES), half_cols)
        copies = [
            pltpu.make_async_copy(w_ref.at[:, cols], wide_ref.at[pl.ds(0, feats)], sems.at[0]),
        ]
        for s in range(per_dev):
            for v in range(col_tiles):
                n = s * col_tiles + v
                copies.append(
                    pltpu.make_async_copy(
                        u_ref.at[s, :, pl.ds(v * LANES, LANES)],
                        wide_ref.at[pl.ds(feats + n * rank, rank)],
                        sems.at[1 + n],
                    )
                )
        for c in copies:
            c.start()
        for c in copies:
            c.wait()

    own_w = call(
        pack_columns,
        "pack_columns",
        like(feats + up_rows, LANES),
        [HBM, HBM],
        (value_weight, up),
        [pltpu.SemaphoreType.DMA((1 + per_dev * col_tiles,))],
        mib=16,
    )

    tiles = feats // LANES
    tile_rows = tiles * block_len
    wide_rows = feats + up_rows
    code_at = half + tile_rows

    def sort_blocks(ints_ref, info_ref, tok_ref, sorted_ref, sems):
        here = ints_ref[1]
        copies = []
        row = lax.broadcasted_iota(jnp.int32, (CODE_ROWS, LANES), 0)
        code = jnp.zeros((CODE_ROWS, LANES), jnp.int32)
        for slot in range(dp):
            which, local_slot = block_at(info_ref, where_from(here, slot))
            src = tok_ref.at[pl.ds(pl.multiple_of(which * block_len, block_len), block_len)]
            to = sorted_ref.at[pl.ds(slot * block_len, block_len)]
            copies.append(pltpu.make_async_copy(src, to, sems.at[slot]))
            copies[-1].start()
            code = jnp.where(row == slot, local_slot, code)
        sorted_ref[rows:, 0:LANES] = code.astype(F32).astype(BF16)
        for c in copies:
            c.wait()

    in_order = call(
        sort_blocks,
        "sort_blocks",
        like(rows + CODE_ROWS, feats),
        [SMEM, HBM],
        (info, tokens),
        [pltpu.SemaphoreType.DMA((dp,))],
        mib=16,
    )

    def pack_shrinks(ints_ref, sorted_ref, d_ref, own_ref, other_ref, first_ref, second_ref):
        me = ints_ref[0]
        for which, ref in ((me, own_ref), (1 - me, other_ref)):
            d = d_ref[which]
            ref[...] = jnp.concatenate([d[:, 0:half], d[:, half:feats]], axis=0).T
        first_ref[0:half, :] = own_ref[...]
        first_ref[code_at : code_at + CODE_ROWS, :] = sorted_ref[rows:, 0:LANES]
        for n, (ref, at) in enumerate(((first_ref, half), (second_ref, 0), (second_ref, tile_rows))):
            for i in range(tiles):
                ref[at + i * block_len : at + (i + 1) * block_len, :] = sorted_ref[
                    (n + 1) * block_len : (n + 2) * block_len, i * LANES : (i + 1) * LANES
                ]

    own_d, own_e, first, second = call(
        pack_shrinks,
        "pack_shrinks",
        (like(half, LANES), like(half, LANES), like(wide_rows, LANES), like(wide_rows, LANES)),
        [VMEM, VMEM],
        (in_order, jnp.transpose(down, (0, 2, 1))),
    )

    def choose(ints_ref, outer_ref, inner_ref, out_ref):
        is_outer = outer_plane(ints_ref[1])

        @pl.when(is_outer)
        def _():
            out_ref[...] = outer_ref[...]

        @pl.when(jnp.logical_not(is_outer))
        def _():
            out_ref[...] = inner_ref[...]

    def chosen(x, y):
        return call(choose, "choose", like(wide_rows, LANES), [VMEM, VMEM], (x, y))

    near_w = to_neighbour(own_w)
    mid_w = to_middle(own_w)
    others = to_group(in_order)
    two = to_neighbour(chosen(first, mid_w))
    far_w = to_middle(near_w)
    mid_d = to_middle(tie(own_d, near_w))
    three = to_neighbour(chosen(second, far_w))
    mid_e = to_group(tie(mid_d, others))
    far_d = to_middle(two[0:half])
    far_e = to_group(tie(far_d, mid_e))

    def columns(a_ref, b_ref, w_ref, out_ref, at):
        for g, x in enumerate((a_ref, b_ref)):
            out_ref[at + g * rows : at + (g + 1) * rows, :] = jnp.dot(
                x[0:rows, :], w_ref[0:feats, :], preferred_element_type=F32
            )

    def shrinker(me, a_ref, b_ref, two_ref, three_ref, s_ref):
        number = me.astype(F32)
        codes = [ref[rows:, 0:LANES].astype(F32) for ref in (a_ref, b_ref)]
        near_codes = two_ref[code_at : code_at + CODE_ROWS, :].astype(F32)

        def shrink(slot, d_ref, e_ref=None, theirs=0):
            at = slice(slot * block_len, (slot + 1) * block_len)
            x = [a_ref[at, :], b_ref[at, :]]
            rhs = d_ref[0:half, :]
            if theirs:
                ref = two_ref if theirs == 1 else three_ref
                near_at = (half, 0, tile_rows)[theirs - 1]
                x.append(
                    jnp.concatenate(
                        [
                            ref[near_at + i * block_len : near_at + (i + 1) * block_len, :]
                            for i in range(tiles)
                        ],
                        axis=1,
                    )
                )
                rhs = jnp.concatenate([rhs, e_ref[...]], axis=1)
            x = jnp.concatenate(x, axis=0)
            low = jnp.dot(x[:, 0:half], rhs, preferred_element_type=F32)
            high = jnp.dot(x[:, half:feats], rhs, preferred_element_type=F32)
            mine = low[:, 0:rank] + high[:, rank : 2 * rank]
            for g in range(groups):
                hit = codes[g][slot : slot + 1, 0:rank] == number
                s_ref[g, at, :] = jnp.where(hit, mine[g * block_len : (g + 1) * block_len, :], 0.0)
            if theirs:
                last = slice(groups * block_len, (groups + 1) * block_len)
                other = (
                    low[last, LANES : LANES + rank] + high[last, LANES + rank : LANES + 2 * rank]
                )
                hit = near_codes[theirs : theirs + 1, 0:rank] == number
                s_ref[2, theirs * block_len : (theirs + 1) * block_len, :] = jnp.where(
                    hit, mine[last, :], other
                )

        return shrink

    def early(ints_ref, a_ref, b_ref, w0, w1, mid, two_ref, d0, e0, part_ref, s_ref):
        columns(a_ref, b_ref, w0, part_ref, 0)
        columns(a_ref, b_ref, w1, part_ref, both)
        is_outer = outer_plane(ints_ref[1])
        shrink = shrinker(ints_ref[0], a_ref, b_ref, two_ref, None, s_ref)
        s_ref[...] = jnp.zeros_like(s_ref)

        @pl.when(is_outer)
        def _():
            columns(a_ref, b_ref, two_ref, part_ref, 2 * both)
            shrink(0, d0)

        @pl.when(jnp.logical_not(is_outer))
        def _():
            columns(a_ref, b_ref, mid, part_ref, 2 * both)
            shrink(0, d0, e0, 1)
            shrink(1, two_ref)

    s_shape = jax.ShapeDtypeStruct((3, rows, rank), F32)
    part, shrunk = call(
        early,
        "early_columns",
        (like(3 * both, LANES, F32), s_shape),
        [VMEM] * 8,
        (in_order, others, own_w, near_w, mid_w, two, own_d, own_e),
    )

    def last_columns(
        ints_ref, a_ref, b_ref, two_ref, three_ref, d2, e2, far, part_ref, s_in,
        keep, away, s_ref, last_ref,
    ):
        here, core = ints_ref[1], ints_ref[2] % 2
        is_outer = outer_plane(here)

        def put(ref, ref_at, holder):
            at = pl.ds(pl.multiple_of((holder // 2) * both, both), both)

            @pl.when(holder % 2 == core)
            def _():
                keep[at, :] = ref[ref_at : ref_at + both, :]

            @pl.when(holder % 2 != core)
            def _():
                away[at, :] = ref[ref_at : ref_at + both, :].astype(BF16)

        pl.when(is_outer)(lambda: columns(a_ref, b_ref, three_ref, last_ref, 0))
        shrink = shrinker(ints_ref[0], a_ref, b_ref, two_ref, three_ref, s_ref)
        s_ref[...] = s_in[...]

        @pl.when(jnp.logical_not(is_outer))
        def _():
            columns(a_ref, b_ref, far, last_ref, 0)
            shrink(2, d2, e2, 2)

        for slot in range(3):
            put(part_ref, slot * both, where_from(here, slot))
        put(last_ref, 0, where_from(here, 3))

    keep, away, shrunk = call(
        last_columns,
        "last_columns",
        (like(pairs * both, LANES, F32), like(pairs * both, LANES), s_shape),
        [VMEM] * 9,
        (in_order, others, two, three, mid_d, mid_e, far_w, part, shrunk),
        [pltpu.VMEM((both, LANES), F32)],
    )
    came = swap(away, lambda a, b, c: (a, b, c ^ 1))

    def last_shrinks(ints_ref, a_ref, b_ref, two_ref, three_ref, d3, e3, s_in, keep, away, s_ref):
        shrink = shrinker(ints_ref[0], a_ref, b_ref, two_ref, three_ref, s_ref)
        s_ref[...] = s_in[...]

        @pl.when(jnp.logical_not(outer_plane(ints_ref[1])))
        def _():
            shrink(3, d3, e3, 3)

        for g in range(3):
            s = jnp.concatenate([s_ref[g, 0:s_msg, :], s_ref[g, s_msg:rows, :]], axis=1)
            keep[g * s_msg : (g + 1) * s_msg, :] = s
            away[g * s_msg : (g + 1) * s_msg, :] = s.astype(BF16)

    s_keep, s_away = call(
        last_shrinks,
        "last_shrinks",
        (like(3 * s_msg, LANES, F32), like(3 * s_msg, LANES)),
        [VMEM] * 7,
        (in_order, others, two, three, far_d, far_e, shrunk),
        [pltpu.VMEM((3, rows, rank), F32)],
    )
    s_came = swap(s_away, lambda a, b, c: (a, b, c ^ 1))

    def add_cores(
        ints_ref, keep_ref, came_ref, s_keep, s_came, mine_out, x_out, y_out, d_out, near_out,
    ):
        side = ints_ref[2] // 2

        def tile(out, side_at, g):
            at = pl.ds(pl.multiple_of(side_at * both + g * rows, rows), rows)
            out[0:rows, :] = (keep_ref[at, :] + came_ref[at, :].astype(F32)).astype(out.dtype)

        def low_rank(out, at, g):
            s = pl.ds(g * s_msg, s_msg)
            out[at : at + s_msg, :] = (s_keep[s, :] + s_came[s, :].astype(F32)).astype(out.dtype)

        tile(mine_out, side, 0)
        tile(x_out, 1 - side, 0)
        tile(y_out, side, 1)
        tile(d_out, 1 - side, 1)
        low_rank(mine_out, rows, 0)
        low_rank(x_out, rows, 0)
        low_rank(y_out, rows, 1)
        low_rank(d_out, rows, 1)
        low_rank(near_out, 0, 2)

    mine, to_x, to_y, to_d, to_near = call(
        add_cores,
        "add_cores",
        (
            like(rows + s_msg, LANES, F32),
            like(rows + s_msg, LANES),
            like(rows + s_msg, LANES),
            like(rows + s_msg, LANES),
            like(s_msg, LANES),
        ),
        [VMEM] * 4,
        (keep, came, s_keep, s_came),
    )
    from_d = swap(to_d, lambda a, b, c: (1 - a, b, c ^ 2))
    from_nearx = swap(to_near, lambda a, b, c: (a, b ^ 1, c ^ 2))
    from_x = swap(to_x, lambda a, b, c: (a, b, c ^ 2))
    from_y = to_group(to_y)
    from_near = to_neighbour(to_near)

    def ups(ints_ref, own, near, mid, far, out2, out3, out):
        here = ints_ref[1]
        is_outer = outer_plane(here)

        def put(ref, slot):
            out[where_from(here, slot)] = ref[feats : feats + up_rows, :]

        put(own, 0)
        put(near, 1)

        @pl.when(is_outer)
        def _():
            put(out2, 2)
            put(out3, 3)

        @pl.when(jnp.logical_not(is_outer))
        def _():
            put(mid, 2)
            put(far, 3)

    up_all = call(
        ups,
        "ups",
        jax.ShapeDtypeStruct((dp, up_rows, LANES), BF16),
        [VMEM] * 6,
        (own_w, near_w, mid_w, far_w, two, three),
    )

    def finish(
        ints_ref, info_ref, up_ref, mine_ref, x_ref, y_ref, d_ref, n_ref,
        nx_ref, out_ref,
    ):
        me, here = ints_ref[0], ints_ref[1]
        ours = mine_ref[0:rows, :] + x_ref[0:rows, :].astype(F32)
        theirs = y_ref[0:rows, :].astype(F32) + d_ref[0:rows, :].astype(F32)
        split = (jnp.where(me == 0, ours, theirs), jnp.where(me == 0, theirs, ours))
        s = mine_ref[rows:, :] + n_ref[...].astype(F32) + nx_ref[...].astype(F32)
        for ref in (x_ref, y_ref, d_ref):
            s = s + ref[rows:, :].astype(F32)
        s = s.astype(BF16)
        per_lane = dp // 2
        row = lax.broadcasted_iota(jnp.int32, (block_len, LANES), 0)
        for slot in range(dp):
            holder = where_from(here, slot)
            which, local_slot = block_at(info_ref, holder)
            piece = s[
                (slot % per_lane) * block_len : (slot % per_lane + 1) * block_len,
                (slot // per_lane) * rank : (slot // per_lane + 1) * rank,
            ]
            to = pl.ds(pl.multiple_of(which * block_len, block_len), block_len)
            for v in range(col_tiles):
                at = pl.ds(pl.multiple_of((local_slot * col_tiles + v) * rank, rank), rank)
                delta = jnp.dot(piece, up_ref[holder, at, :], preferred_element_type=F32)
                base = split[v][slot * block_len : (slot + 1) * block_len, :]
                mixed = jnp.where(row < info_ref[adapters + blocks + which], base + delta.astype(BF16).astype(F32), 0.0)
                out_ref[to, v * LANES : (v + 1) * LANES] = mixed.astype(BF16)

    return call(
        finish,
        "finish",
        like(rows, out_cols),
        [SMEM] + [VMEM] * 7,
        (
            info, up_all, mine, from_x, from_y, from_d,
            from_near, from_nearx,
        ),
    )


def local(
    tokens,
    value_weight,
    adapter_down_weight,
    adapter_up_weight,
    adapter_slot_table,
    adapter_per_block,
    request_rows_per_block,
):
    dp_count = lax.axis_size("dp")
    blocks = adapter_per_block.shape[0]
    tok_rows = tokens.shape[0]
    block_len = tok_rows // blocks
    feature_total = tokens.shape[1]
    adapter_total = adapter_down_weight.shape[0]
    adapter_rank_width = adapter_down_weight.shape[2]
    column_total = adapter_up_weight.shape[2]
    partial_value = jnp.dot(
        tokens,
        lax.all_gather(value_weight, "dp", axis=1, tiled=True),
        preferred_element_type=jnp.float32,
    )
    summed = lax.psum(partial_value.astype(jnp.bfloat16), "tensor").astype(jnp.float32)
    base_cols = lax.dynamic_slice_in_dim(
        summed, lax.axis_index("tensor") * column_total, column_total, 1
    )
    matches = (
        adapter_per_block[:, None]
        == jnp.arange(adapter_slot_table.shape[0], dtype=jnp.int32)[None, :]
    )
    slot_index = jnp.sum(jnp.where(matches, adapter_slot_table[None, :], 0), axis=1)
    holder = slot_index // adapter_total
    local_slot = slot_index % adapter_total
    route_map = (holder[None, :] == jnp.arange(dp_count, dtype=jnp.int32)[:, None]).astype(
        jnp.bfloat16
    )
    local_onehot = (
        local_slot[:, None] == jnp.arange(adapter_total, dtype=jnp.int32)[None, :]
    ).astype(jnp.bfloat16)
    wanted_hot = jnp.dot(route_map, local_onehot, preferred_element_type=jnp.bfloat16)
    block_input = tokens.reshape(blocks, block_len, feature_total)
    sent_x = jnp.dot(
        route_map,
        block_input.reshape(blocks, block_len * feature_total),
        preferred_element_type=jnp.bfloat16,
    )
    sent_x = sent_x.reshape(dp_count, block_len, feature_total)
    recv_x, recv_hot = (
        lax.all_to_all(sent_x, "dp", split_axis=0, concat_axis=0, tiled=True),
        lax.all_to_all(wanted_hot, "dp", split_axis=0, concat_axis=0, tiled=True),
    )
    flat_down_weight = jnp.transpose(adapter_down_weight, (1, 0, 2)).reshape(
        feature_total, adapter_total * adapter_rank_width
    )
    every = jnp.einsum("nbf,fq->nbq", recv_x, flat_down_weight, preferred_element_type=jnp.float32)
    every = every.reshape(dp_count, block_len, adapter_total, adapter_rank_width)
    picked = jnp.sum(every * recv_hot.astype(jnp.float32)[:, None, :, None], axis=2)
    reduced_input = lax.psum(picked.astype(jnp.bfloat16), "tensor")
    spread_rows = (recv_hot[:, None, :, None] * reduced_input[:, :, None, :]).reshape(
        dp_count, block_len, adapter_total * adapter_rank_width
    )
    flat_up_weight = adapter_up_weight.reshape(adapter_total * adapter_rank_width, column_total)
    delta_rows = jnp.einsum(
        "nbq,qc->nbc", spread_rows, flat_up_weight, preferred_element_type=jnp.float32
    ).astype(jnp.bfloat16)
    returned = lax.all_to_all(delta_rows, "dp", split_axis=0, concat_axis=0, tiled=True)
    own_delta = jnp.dot(
        route_map.T,
        returned.reshape(dp_count, block_len * column_total),
        preferred_element_type=jnp.bfloat16,
    )
    own_delta = own_delta.reshape(tok_rows, column_total)
    live_rows = (
        jnp.arange(block_len, dtype=jnp.int32)[None, :] < request_rows_per_block[:, None]
    ).reshape(tok_rows)
    mixed = jnp.where(
        live_rows[:, None], base_cols + own_delta.astype(jnp.float32), jnp.float32(0.0)
    )
    return mixed.astype(jnp.bfloat16)


def solution(mesh):
    placed = (
        P(("groups", "dp"), "tensor"),
        P("tensor", "dp"),
        P("dp", "tensor", None),
        P("dp", None, "tensor"),
        P("groups"),
        P(("groups", "dp")),
        P(("groups", "dp")),
    )
    sizes = tuple(mesh.shape[a] for a in AXES)
    if sizes == (2, 4, 4):
        body = lambda *args: local_line(sizes, *args)
    else:
        body = local
    return jax.shard_map(
        body, mesh=mesh, in_specs=placed, out_specs=P(("groups", "dp"), "tensor"), check_vma=False
    )
```

```python
import jax
import jax.numpy as jnp
from jax import lax
from jax.experimental import pallas as pl
from jax.experimental.pallas import tpu as pltpu
from jax.sharding import PartitionSpec as P

AXES = ("groups", "dp", "tensor")
LANES = 128
CODE_ROWS = 16
F32 = jnp.float32
BF16 = jnp.bfloat16
VMEM = pl.BlockSpec(memory_space=pltpu.VMEM)
SMEM = pl.BlockSpec(memory_space=pltpu.SMEM)
HBM = pl.BlockSpec(memory_space=pltpu.HBM)


class Place:
    def __getitem__(self, n):
        return lax.axis_index(AXES[n]).astype(jnp.int32)


def call(body, name, outs, specs, ins, scratch=(), mib=16):
    return pl.pallas_call(
        lambda *refs: body(Place(), *refs),
        name=name,
        out_shape=outs,
        in_specs=specs,
        out_specs=jax.tree.map(lambda _: VMEM, outs),
        scratch_shapes=scratch,
        compiler_params=pltpu.CompilerParams(vmem_limit_bytes=mib * 2**20),
    )(*ins)


def like(rows, cols, dtype=BF16):
    return jax.ShapeDtypeStruct((rows, cols), dtype)


def local_line(sizes, tokens, value_weight, down, up, slot_table, per_block, live_rows):
    groups, dp, tensor = sizes
    rows, feats = tokens.shape
    blocks = per_block.shape[0]
    block_len = rows // blocks
    per_dev, _, rank = down.shape
    out_cols = up.shape[2]
    half_cols = value_weight.shape[1] // groups
    half = feats // 2
    up_rows = per_dev * rank * out_cols // LANES
    col_tiles = out_cols // LANES
    pairs = dp // 2
    both = groups * rows
    s_msg = rows // 2

    def device(a, b, c):
        return (a * dp + b) * tensor + c

    def swap(x, where):
        perm = [
            (device(a, b, c), device(*where(a, b, c)))
            for a in range(groups)
            for b in range(dp)
            for c in range(tensor)
        ]
        return lax.ppermute(x, AXES, perm)

    def to_neighbour(x):
        return swap(x, lambda a, b, c: (a, b ^ 1, c))

    def to_middle(x):
        return swap(x, lambda a, b, c: (a, 3 - b, c) if b in (1, 2) else (a, b, c ^ 1))

    def to_group(x):
        return swap(x, lambda a, b, c: (1 - a, b, c))

    def tie(x, *earlier):
        return lax.optimization_barrier((x, *earlier))[0]

    def outer_plane(here):
        return (here == 0) | (here == 3)

    def where_from(here, slot):
        near = here ^ 1
        if slot == 0:
            return here
        if slot == 1:
            return near
        if slot == 2:
            return jnp.where(outer_plane(here), 3 - near, 3 - here)
        return jnp.where(outer_plane(here), 3 - here, 3 - near)

    adapters = slot_table.shape[0]
    info = jnp.concatenate([slot_table, per_block, live_rows])

    def block_at(info_ref, holder):
        which, local_slot = jnp.int32(0), jnp.int32(0)
        for k in range(blocks):
            s = info_ref[info_ref[adapters + k]]
            hit = s // per_dev == holder
            which = jnp.where(hit, k, which)
            local_slot = jnp.where(hit, s % per_dev, local_slot)
        return which, local_slot

    mine_at = lax.axis_index("groups") * half_cols
    up_tiles = up.reshape(per_dev, rank, col_tiles, LANES).transpose(0, 2, 1, 3)
    own_w = jnp.concatenate(
        [
            lax.dynamic_slice_in_dim(value_weight, mine_at, half_cols, 1),
            up_tiles.reshape(up_rows, LANES),
        ]
    )

    tiles = feats // LANES
    tile_rows = tiles * block_len
    wide_rows = feats + up_rows
    code_at = half + tile_rows

    def sort_blocks(ints_ref, info_ref, tok_ref, sorted_ref, sems):
        here = ints_ref[1]
        copies = []
        row = lax.broadcasted_iota(jnp.int32, (CODE_ROWS, LANES), 0)
        code = jnp.zeros((CODE_ROWS, LANES), jnp.int32)
        for slot in range(dp):
            which, local_slot = block_at(info_ref, where_from(here, slot))
            src = tok_ref.at[pl.ds(pl.multiple_of(which * block_len, block_len), block_len)]
            to = sorted_ref.at[pl.ds(slot * block_len, block_len)]
            copies.append(pltpu.make_async_copy(src, to, sems.at[slot]))
            copies[-1].start()
            code = jnp.where(row == slot, local_slot, code)
        sorted_ref[rows:, 0:LANES] = code.astype(F32).astype(BF16)
        for c in copies:
            c.wait()

    in_order = call(
        sort_blocks,
        "sort_blocks",
        like(rows + CODE_ROWS, feats),
        [SMEM, HBM],
        (info, tokens),
        [pltpu.SemaphoreType.DMA((dp,))],
        mib=16,
    )

    def pack_shrinks(ints_ref, sorted_ref, d_ref, own_ref, other_ref, first_ref, second_ref):
        me = ints_ref[0]
        for which, ref in ((me, own_ref), (1 - me, other_ref)):
            d = d_ref[which]
            ref[...] = jnp.concatenate([d[:, 0:half], d[:, half:feats]], axis=0).T
        first_ref[0:half, :] = own_ref[...]
        first_ref[code_at : code_at + CODE_ROWS, :] = sorted_ref[rows:, 0:LANES]
        for n, (ref, at) in enumerate(((first_ref, half), (second_ref, 0), (second_ref, tile_rows))):
            for i in range(tiles):
                ref[at + i * block_len : at + (i + 1) * block_len, :] = sorted_ref[
                    (n + 1) * block_len : (n + 2) * block_len, i * LANES : (i + 1) * LANES
                ]

    own_d, own_e, first, second = call(
        pack_shrinks,
        "pack_shrinks",
        (like(half, LANES), like(half, LANES), like(wide_rows, LANES), like(wide_rows, LANES)),
        [VMEM, VMEM],
        (in_order, jnp.transpose(down, (0, 2, 1))),
    )

    def choose(ints_ref, outer_ref, inner_ref, out_ref):
        is_outer = outer_plane(ints_ref[1])

        @pl.when(is_outer)
        def _():
            out_ref[...] = outer_ref[...]

        @pl.when(jnp.logical_not(is_outer))
        def _():
            out_ref[...] = inner_ref[...]

    def chosen(x, y):
        return call(choose, "choose", like(wide_rows, LANES), [VMEM, VMEM], (x, y))

    near_w = to_neighbour(own_w)
    mid_w = to_middle(own_w)
    others = to_group(in_order)
    two = to_neighbour(chosen(first, mid_w))
    far_w = to_middle(near_w)
    mid_d = to_middle(tie(own_d, near_w))
    three = to_neighbour(chosen(second, far_w))
    mid_e = to_group(tie(mid_d, others))
    far_d = to_middle(two[0:half])
    far_e = to_group(tie(far_d, mid_e))

    def columns(a_ref, b_ref, w_ref, out_ref, at):
        for g, x in enumerate((a_ref, b_ref)):
            out_ref[at + g * rows : at + (g + 1) * rows, :] = jnp.dot(
                x[0:rows, :], w_ref[0:feats, :], preferred_element_type=F32
            )

    def shrinker(me, a_ref, b_ref, two_ref, three_ref, s_ref):
        number = me.astype(F32)
        codes = [ref[rows:, 0:LANES].astype(F32) for ref in (a_ref, b_ref)]
        near_codes = two_ref[code_at : code_at + CODE_ROWS, :].astype(F32)

        def shrink(slot, d_ref, e_ref=None, theirs=0):
            at = slice(slot * block_len, (slot + 1) * block_len)
            x = [a_ref[at, :], b_ref[at, :]]
            rhs = d_ref[0:half, :]
            if theirs:
                ref = two_ref if theirs == 1 else three_ref
                near_at = (half, 0, tile_rows)[theirs - 1]
                x.append(
                    jnp.concatenate(
                        [
                            ref[near_at + i * block_len : near_at + (i + 1) * block_len, :]
                            for i in range(tiles)
                        ],
                        axis=1,
                    )
                )
                rhs = jnp.concatenate([rhs, e_ref[...]], axis=1)
            x = jnp.concatenate(x, axis=0)
            low = jnp.dot(x[:, 0:half], rhs, preferred_element_type=F32)
            high = jnp.dot(x[:, half:feats], rhs, preferred_element_type=F32)
            mine = low[:, 0:rank] + high[:, rank : 2 * rank]
            for g in range(groups):
                hit = codes[g][slot : slot + 1, 0:rank] == number
                s_ref[g, at, :] = jnp.where(hit, mine[g * block_len : (g + 1) * block_len, :], 0.0)
            if theirs:
                last = slice(groups * block_len, (groups + 1) * block_len)
                other = (
                    low[last, LANES : LANES + rank] + high[last, LANES + rank : LANES + 2 * rank]
                )
                hit = near_codes[theirs : theirs + 1, 0:rank] == number
                s_ref[2, theirs * block_len : (theirs + 1) * block_len, :] = jnp.where(
                    hit, mine[last, :], other
                )

        return shrink

    def early(ints_ref, a_ref, b_ref, w0, w1, mid, two_ref, d0, e0, part_ref, s_ref):
        columns(a_ref, b_ref, w0, part_ref, 0)
        columns(a_ref, b_ref, w1, part_ref, both)
        is_outer = outer_plane(ints_ref[1])
        shrink = shrinker(ints_ref[0], a_ref, b_ref, two_ref, None, s_ref)
        s_ref[...] = jnp.zeros_like(s_ref)

        @pl.when(is_outer)
        def _():
            columns(a_ref, b_ref, two_ref, part_ref, 2 * both)
            shrink(0, d0)

        @pl.when(jnp.logical_not(is_outer))
        def _():
            columns(a_ref, b_ref, mid, part_ref, 2 * both)
            shrink(0, d0, e0, 1)
            shrink(1, two_ref)

    s_shape = jax.ShapeDtypeStruct((3, rows, rank), F32)
    part, shrunk = call(
        early,
        "early_columns",
        (like(3 * both, LANES, F32), s_shape),
        [VMEM] * 8,
        (in_order, others, own_w, near_w, mid_w, two, own_d, own_e),
    )

    def last_columns(
        ints_ref, a_ref, b_ref, two_ref, three_ref, d2, e2, far, part_ref, s_in,
        keep, away, s_ref, last_ref,
    ):
        here, core = ints_ref[1], ints_ref[2] % 2
        is_outer = outer_plane(here)

        def put(ref, ref_at, holder):
            at = pl.ds(pl.multiple_of((holder // 2) * both, both), both)

            @pl.when(holder % 2 == core)
            def _():
                keep[at, :] = ref[ref_at : ref_at + both, :]

            @pl.when(holder % 2 != core)
            def _():
                away[at, :] = ref[ref_at : ref_at + both, :].astype(BF16)

        pl.when(is_outer)(lambda: columns(a_ref, b_ref, three_ref, last_ref, 0))
        shrink = shrinker(ints_ref[0], a_ref, b_ref, two_ref, three_ref, s_ref)
        s_ref[...] = s_in[...]

        @pl.when(jnp.logical_not(is_outer))
        def _():
            columns(a_ref, b_ref, far, last_ref, 0)
            shrink(2, d2, e2, 2)

        for slot in range(3):
            put(part_ref, slot * both, where_from(here, slot))
        put(last_ref, 0, where_from(here, 3))

    keep, away, shrunk = call(
        last_columns,
        "last_columns",
        (like(pairs * both, LANES, F32), like(pairs * both, LANES), s_shape),
        [VMEM] * 9,
        (in_order, others, two, three, mid_d, mid_e, far_w, part, shrunk),
        [pltpu.VMEM((both, LANES), F32)],
    )
    came = swap(away, lambda a, b, c: (a, b, c ^ 1))

    def last_shrinks(ints_ref, a_ref, b_ref, two_ref, three_ref, d3, e3, s_in, keep, away, s_ref):
        shrink = shrinker(ints_ref[0], a_ref, b_ref, two_ref, three_ref, s_ref)
        s_ref[...] = s_in[...]

        @pl.when(jnp.logical_not(outer_plane(ints_ref[1])))
        def _():
            shrink(3, d3, e3, 3)

        for g in range(3):
            s = jnp.concatenate([s_ref[g, 0:s_msg, :], s_ref[g, s_msg:rows, :]], axis=1)
            keep[g * s_msg : (g + 1) * s_msg, :] = s
            away[g * s_msg : (g + 1) * s_msg, :] = s.astype(BF16)

    s_keep, s_away = call(
        last_shrinks,
        "last_shrinks",
        (like(3 * s_msg, LANES, F32), like(3 * s_msg, LANES)),
        [VMEM] * 7,
        (in_order, others, two, three, far_d, far_e, shrunk),
        [pltpu.VMEM((3, rows, rank), F32)],
    )
    s_came = swap(s_away, lambda a, b, c: (a, b, c ^ 1))

    def add_cores(
        ints_ref, keep_ref, came_ref, s_keep, s_came, mine_out, x_out, y_out, d_out, near_out,
    ):
        side = ints_ref[2] // 2

        def tile(out, side_at, g):
            at = pl.ds(pl.multiple_of(side_at * both + g * rows, rows), rows)
            out[0:rows, :] = (keep_ref[at, :] + came_ref[at, :].astype(F32)).astype(out.dtype)

        def low_rank(out, at, g):
            s = pl.ds(g * s_msg, s_msg)
            out[at : at + s_msg, :] = (s_keep[s, :] + s_came[s, :].astype(F32)).astype(out.dtype)

        tile(mine_out, side, 0)
        tile(x_out, 1 - side, 0)
        tile(y_out, side, 1)
        tile(d_out, 1 - side, 1)
        low_rank(mine_out, rows, 0)
        low_rank(x_out, rows, 0)
        low_rank(y_out, rows, 1)
        low_rank(d_out, rows, 1)
        low_rank(near_out, 0, 2)

    mine, to_x, to_y, to_d, to_near = call(
        add_cores,
        "add_cores",
        (
            like(rows + s_msg, LANES, F32),
            like(rows + s_msg, LANES),
            like(rows + s_msg, LANES),
            like(rows + s_msg, LANES),
            like(s_msg, LANES),
        ),
        [VMEM] * 4,
        (keep, came, s_keep, s_came),
    )
    from_d = swap(to_d, lambda a, b, c: (1 - a, b, c ^ 2))
    from_nearx = swap(to_near, lambda a, b, c: (a, b ^ 1, c ^ 2))
    from_x = swap(to_x, lambda a, b, c: (a, b, c ^ 2))
    from_y = to_group(to_y)
    from_near = to_neighbour(to_near)

    def ups(ints_ref, info_ref, own, near, mid, far, out2, out3, up_ref, mark_ref):
        here = ints_ref[1]
        is_outer = outer_plane(here)

        live_at = dp * blocks
        found = []
        for slot in range(dp):
            which, local_slot = block_at(info_ref, where_from(here, slot))
            found.append(local_slot)
            for k in range(blocks):
                at = slot * blocks + k
                mark_ref[at : at + 1, :] = jnp.full((1, LANES), (which == k).astype(F32), F32)
            live = info_ref[adapters + blocks + which].astype(F32)
            mark_ref[live_at + slot : live_at + slot + 1, :] = jnp.full((1, LANES), live, F32)

        def put(ref, slot):
            at = feats + found[slot] * col_tiles * rank
            up_ref[slot] = ref[pl.ds(pl.multiple_of(at, col_tiles * rank), col_tiles * rank), :]

        put(own, 0)
        put(near, 1)

        @pl.when(is_outer)
        def _():
            put(out2, 2)
            put(out3, 3)

        @pl.when(jnp.logical_not(is_outer))
        def _():
            put(mid, 2)
            put(far, 3)

    up_used, marks = call(
        ups,
        "ups",
        (
            jax.ShapeDtypeStruct((dp, col_tiles * rank, LANES), BF16),
            like(dp * blocks + 2 * dp, LANES, F32),
        ),
        [SMEM] + [VMEM] * 6,
        (info, own_w, near_w, mid_w, far_w, two, three),
    )

    def finish(
        ints_ref, mark_ref, up_ref, mine_ref, x_ref, y_ref, d_ref, n_ref,
        nx_ref, out_ref,
    ):
        me = ints_ref[0]
        ours = mine_ref[0:rows, :] + x_ref[0:rows, :].astype(F32)
        theirs = y_ref[0:rows, :].astype(F32) + d_ref[0:rows, :].astype(F32)
        split = (jnp.where(me == 0, ours, theirs), jnp.where(me == 0, theirs, ours))
        s = mine_ref[rows:, :] + n_ref[...].astype(F32) + nx_ref[...].astype(F32)
        for ref in (x_ref, y_ref, d_ref):
            s = s + ref[rows:, :].astype(F32)
        s = s.astype(BF16)
        per_lane = dp // 2
        row = lax.broadcasted_iota(jnp.int32, (block_len, LANES), 0).astype(F32)
        results = [[None] * col_tiles for _ in range(blocks)]
        for slot in range(dp):
            piece = s[
                (slot % per_lane) * block_len : (slot % per_lane + 1) * block_len,
                (slot // per_lane) * rank : (slot // per_lane + 1) * rank,
            ]
            live_at = dp * blocks + slot
            live = row < mark_ref[live_at : live_at + 1, :]
            for v in range(col_tiles):
                weight = up_ref[slot, v * rank : (v + 1) * rank, :]
                delta = jnp.dot(piece, weight, preferred_element_type=F32)
                base = split[v][slot * block_len : (slot + 1) * block_len, :]
                mixed = jnp.where(live, base + delta.astype(BF16).astype(F32), 0.0)
                for k in range(blocks):
                    at = slot * blocks + k
                    hit = mark_ref[at : at + 1, :] > 0.5
                    before = results[k][v]
                    results[k][v] = mixed if before is None else jnp.where(hit, mixed, before)
        for k in range(blocks):
            for v in range(col_tiles):
                out_ref[
                    k * block_len : (k + 1) * block_len, v * LANES : (v + 1) * LANES
                ] = results[k][v].astype(BF16)

    return call(
        finish,
        "finish",
        like(rows, out_cols),
        [VMEM] * 8,
        (
            marks, up_used, mine, from_x, from_y, from_d,
            from_near, from_nearx,
        ),
    )


def local(
    tokens,
    value_weight,
    adapter_down_weight,
    adapter_up_weight,
    adapter_slot_table,
    adapter_per_block,
    request_rows_per_block,
):
    dp_count = lax.axis_size("dp")
    blocks = adapter_per_block.shape[0]
    tok_rows = tokens.shape[0]
    block_len = tok_rows // blocks
    feature_total = tokens.shape[1]
    adapter_total = adapter_down_weight.shape[0]
    adapter_rank_width = adapter_down_weight.shape[2]
    column_total = adapter_up_weight.shape[2]
    partial_value = jnp.dot(
        tokens,
        lax.all_gather(value_weight, "dp", axis=1, tiled=True),
        preferred_element_type=jnp.float32,
    )
    summed = lax.psum(partial_value.astype(jnp.bfloat16), "tensor").astype(jnp.float32)
    base_cols = lax.dynamic_slice_in_dim(
        summed, lax.axis_index("tensor") * column_total, column_total, 1
    )
    matches = (
        adapter_per_block[:, None]
        == jnp.arange(adapter_slot_table.shape[0], dtype=jnp.int32)[None, :]
    )
    slot_index = jnp.sum(jnp.where(matches, adapter_slot_table[None, :], 0), axis=1)
    holder = slot_index // adapter_total
    local_slot = slot_index % adapter_total
    route_map = (holder[None, :] == jnp.arange(dp_count, dtype=jnp.int32)[:, None]).astype(
        jnp.bfloat16
    )
    local_onehot = (
        local_slot[:, None] == jnp.arange(adapter_total, dtype=jnp.int32)[None, :]
    ).astype(jnp.bfloat16)
    wanted_hot = jnp.dot(route_map, local_onehot, preferred_element_type=jnp.bfloat16)
    block_input = tokens.reshape(blocks, block_len, feature_total)
    sent_x = jnp.dot(
        route_map,
        block_input.reshape(blocks, block_len * feature_total),
        preferred_element_type=jnp.bfloat16,
    )
    sent_x = sent_x.reshape(dp_count, block_len, feature_total)
    recv_x, recv_hot = (
        lax.all_to_all(sent_x, "dp", split_axis=0, concat_axis=0, tiled=True),
        lax.all_to_all(wanted_hot, "dp", split_axis=0, concat_axis=0, tiled=True),
    )
    flat_down_weight = jnp.transpose(adapter_down_weight, (1, 0, 2)).reshape(
        feature_total, adapter_total * adapter_rank_width
    )
    every = jnp.einsum("nbf,fq->nbq", recv_x, flat_down_weight, preferred_element_type=jnp.float32)
    every = every.reshape(dp_count, block_len, adapter_total, adapter_rank_width)
    picked = jnp.sum(every * recv_hot.astype(jnp.float32)[:, None, :, None], axis=2)
    reduced_input = lax.psum(picked.astype(jnp.bfloat16), "tensor")
    spread_rows = (recv_hot[:, None, :, None] * reduced_input[:, :, None, :]).reshape(
        dp_count, block_len, adapter_total * adapter_rank_width
    )
    flat_up_weight = adapter_up_weight.reshape(adapter_total * adapter_rank_width, column_total)
    delta_rows = jnp.einsum(
        "nbq,qc->nbc", spread_rows, flat_up_weight, preferred_element_type=jnp.float32
    ).astype(jnp.bfloat16)
    returned = lax.all_to_all(delta_rows, "dp", split_axis=0, concat_axis=0, tiled=True)
    own_delta = jnp.dot(
        route_map.T,
        returned.reshape(dp_count, block_len * column_total),
        preferred_element_type=jnp.bfloat16,
    )
    own_delta = own_delta.reshape(tok_rows, column_total)
    live_rows = (
        jnp.arange(block_len, dtype=jnp.int32)[None, :] < request_rows_per_block[:, None]
    ).reshape(tok_rows)
    mixed = jnp.where(
        live_rows[:, None], base_cols + own_delta.astype(jnp.float32), jnp.float32(0.0)
    )
    return mixed.astype(jnp.bfloat16)


def solution(mesh):
    placed = (
        P(("groups", "dp"), "tensor"),
        P("tensor", "dp"),
        P("dp", "tensor", None),
        P("dp", None, "tensor"),
        P("groups"),
        P(("groups", "dp")),
        P(("groups", "dp")),
    )
    sizes = tuple(mesh.shape[a] for a in AXES)
    if sizes == (2, 4, 4):
        body = lambda *args: local_line(sizes, *args)
    else:
        body = local
    return jax.shard_map(
        body, mesh=mesh, in_specs=placed, out_specs=P(("groups", "dp"), "tensor"), check_vma=False
    )
```

```python
import jax
import jax.numpy as jnp
from jax import lax
from jax.experimental import pallas as pl
from jax.experimental.pallas import tpu as pltpu
from jax.sharding import PartitionSpec as P

AXES = ("groups", "dp", "tensor")
LANES = 128
CODE_ROWS = 16
F32 = jnp.float32
BF16 = jnp.bfloat16
VMEM = pl.BlockSpec(memory_space=pltpu.VMEM)
SMEM = pl.BlockSpec(memory_space=pltpu.SMEM)
HBM = pl.BlockSpec(memory_space=pltpu.HBM)


class Place:
    def __getitem__(self, n):
        return lax.axis_index(AXES[n]).astype(jnp.int32)


def call(body, name, outs, specs, ins, scratch=(), mib=16):
    return pl.pallas_call(
        lambda *refs: body(Place(), *refs),
        name=name,
        out_shape=outs,
        in_specs=specs,
        out_specs=jax.tree.map(lambda _: VMEM, outs),
        scratch_shapes=scratch,
        compiler_params=pltpu.CompilerParams(vmem_limit_bytes=mib * 2**20),
    )(*ins)


def like(rows, cols, dtype=BF16):
    return jax.ShapeDtypeStruct((rows, cols), dtype)


def local_line(sizes, tokens, value_weight, down, up, slot_table, per_block, live_rows):
    groups, dp, tensor = sizes
    rows, feats = tokens.shape
    blocks = per_block.shape[0]
    block_len = rows // blocks
    per_dev, _, rank = down.shape
    out_cols = up.shape[2]
    half_cols = value_weight.shape[1] // groups
    half = feats // 2
    up_rows = rank * out_cols // LANES
    col_tiles = out_cols // LANES
    pairs = dp // 2
    both = groups * rows
    s_msg = rows // 2

    def device(a, b, c):
        return (a * dp + b) * tensor + c

    def swap(x, where):
        perm = [
            (device(a, b, c), device(*where(a, b, c)))
            for a in range(groups)
            for b in range(dp)
            for c in range(tensor)
        ]
        return lax.ppermute(x, AXES, perm)

    def to_neighbour(x):
        return swap(x, lambda a, b, c: (a, b ^ 1, c))

    def to_middle(x):
        return swap(x, lambda a, b, c: (a, 3 - b, c) if b in (1, 2) else (a, b, c ^ 1))

    def to_group(x):
        return swap(x, lambda a, b, c: (1 - a, b, c))

    def tie(x, *earlier):
        return lax.optimization_barrier((x, *earlier))[0]

    def outer_plane(here):
        return (here == 0) | (here == 3)

    def where_from(here, slot):
        near = here ^ 1
        if slot == 0:
            return here
        if slot == 1:
            return near
        if slot == 2:
            return jnp.where(outer_plane(here), 3 - near, 3 - here)
        return jnp.where(outer_plane(here), 3 - here, 3 - near)

    adapters = slot_table.shape[0]
    info = jnp.concatenate([slot_table, per_block, live_rows])

    def block_at(info_ref, holder):
        which, local_slot = jnp.int32(0), jnp.int32(0)
        for k in range(blocks):
            s = info_ref[info_ref[adapters + k]]
            hit = s // per_dev == holder
            which = jnp.where(hit, k, which)
            local_slot = jnp.where(hit, s % per_dev, local_slot)
        return which, local_slot

    group = lax.axis_index("groups")
    up_mine = lax.dynamic_index_in_dim(up, group, 0, keepdims=False)
    own_w = jnp.concatenate(
        [lax.dynamic_slice_in_dim(value_weight, group * half_cols, half_cols, 1)]
        + [up_mine[:, v * LANES : (v + 1) * LANES] for v in range(col_tiles)]
    )

    tiles = feats // LANES
    tile_rows = tiles * block_len
    wide_rows = feats + up_rows
    code_at = half + tile_rows

    def sort_blocks(ints_ref, info_ref, tok_ref, sorted_ref, sems):
        here = ints_ref[1]
        copies = []
        row = lax.broadcasted_iota(jnp.int32, (CODE_ROWS, LANES), 0)
        code = jnp.zeros((CODE_ROWS, LANES), jnp.int32)
        for slot in range(dp):
            which, local_slot = block_at(info_ref, where_from(here, slot))
            src = tok_ref.at[pl.ds(pl.multiple_of(which * block_len, block_len), block_len)]
            to = sorted_ref.at[pl.ds(slot * block_len, block_len)]
            copies.append(pltpu.make_async_copy(src, to, sems.at[slot]))
            copies[-1].start()
            code = jnp.where(row == slot, local_slot, code)
        sorted_ref[rows:, 0:LANES] = code.astype(F32).astype(BF16)
        for c in copies:
            c.wait()

    in_order = call(
        sort_blocks,
        "sort_blocks",
        like(rows + CODE_ROWS, feats),
        [SMEM, HBM],
        (info, tokens),
        [pltpu.SemaphoreType.DMA((dp,))],
        mib=16,
    )

    def pack_shrinks(ints_ref, sorted_ref, d_ref, own_ref, other_ref, first_ref, second_ref):
        me = ints_ref[0]
        for which, ref in ((me, own_ref), (1 - me, other_ref)):
            d = d_ref[which]
            ref[...] = jnp.concatenate([d[:, 0:half], d[:, half:feats]], axis=0).T
        first_ref[0:half, :] = own_ref[...]
        first_ref[code_at : code_at + CODE_ROWS, :] = sorted_ref[rows:, 0:LANES]
        for n, (ref, at) in enumerate(((first_ref, half), (second_ref, 0), (second_ref, tile_rows))):
            for i in range(tiles):
                ref[at + i * block_len : at + (i + 1) * block_len, :] = sorted_ref[
                    (n + 1) * block_len : (n + 2) * block_len, i * LANES : (i + 1) * LANES
                ]

    own_d, own_e, first, second = call(
        pack_shrinks,
        "pack_shrinks",
        (like(half, LANES), like(half, LANES), like(wide_rows, LANES), like(wide_rows, LANES)),
        [VMEM, VMEM],
        (in_order, jnp.transpose(down, (0, 2, 1))),
    )

    def choose(ints_ref, outer_ref, inner_ref, out_ref):
        is_outer = outer_plane(ints_ref[1])

        @pl.when(is_outer)
        def _():
            out_ref[...] = outer_ref[...]

        @pl.when(jnp.logical_not(is_outer))
        def _():
            out_ref[...] = inner_ref[...]

    def chosen(x, y):
        return call(choose, "choose", like(wide_rows, LANES), [VMEM, VMEM], (x, y))

    near_w = to_neighbour(own_w)
    mid_w = to_middle(own_w)
    others = to_group(in_order)
    two = to_neighbour(chosen(first, mid_w))
    far_w = to_middle(near_w)
    mid_d = to_middle(tie(own_d, near_w))
    three = to_neighbour(chosen(second, far_w))
    near_d = two[0:half]
    mid_e = to_group(tie(mid_d, others, near_d))
    far_d = to_middle(near_d)
    far_e = to_group(tie(far_d, mid_e))

    def columns(a_ref, b_ref, w_ref, out_ref, at):
        for g, x in enumerate((a_ref, b_ref)):
            out_ref[at + g * rows : at + (g + 1) * rows, :] = jnp.dot(
                x[0:rows, :], w_ref[0:feats, :], preferred_element_type=F32
            )

    def shrinker(me, a_ref, b_ref, two_ref, three_ref, s_ref):
        number = me.astype(F32)
        codes = [ref[rows:, 0:LANES].astype(F32) for ref in (a_ref, b_ref)]
        near_codes = two_ref[code_at : code_at + CODE_ROWS, :].astype(F32)

        def shrink(slot, d_ref, e_ref=None, theirs=0):
            at = slice(slot * block_len, (slot + 1) * block_len)
            x = [a_ref[at, :], b_ref[at, :]]
            rhs = d_ref[0:half, :]
            if theirs:
                ref = two_ref if theirs == 1 else three_ref
                near_at = (half, 0, tile_rows)[theirs - 1]
                x.append(
                    jnp.concatenate(
                        [
                            ref[near_at + i * block_len : near_at + (i + 1) * block_len, :]
                            for i in range(tiles)
                        ],
                        axis=1,
                    )
                )
                rhs = jnp.concatenate([rhs, e_ref[...]], axis=1)
            x = jnp.concatenate(x, axis=0)
            low = jnp.dot(x[:, 0:half], rhs, preferred_element_type=F32)
            high = jnp.dot(x[:, half:feats], rhs, preferred_element_type=F32)
            mine = low[:, 0:rank] + high[:, rank : 2 * rank]
            for g in range(groups):
                hit = codes[g][slot : slot + 1, 0:rank] == number
                s_ref[g, at, :] = jnp.where(hit, mine[g * block_len : (g + 1) * block_len, :], 0.0)
            if theirs:
                last = slice(groups * block_len, (groups + 1) * block_len)
                other = (
                    low[last, LANES : LANES + rank] + high[last, LANES + rank : LANES + 2 * rank]
                )
                hit = near_codes[theirs : theirs + 1, 0:rank] == number
                s_ref[2, theirs * block_len : (theirs + 1) * block_len, :] = jnp.where(
                    hit, mine[last, :], other
                )

        return shrink

    def early(ints_ref, a_ref, b_ref, w0, w1, mid, two_ref, d0, e0, part_ref, s_ref):
        columns(a_ref, b_ref, w0, part_ref, 0)
        columns(a_ref, b_ref, w1, part_ref, both)
        is_outer = outer_plane(ints_ref[1])
        shrink = shrinker(ints_ref[0], a_ref, b_ref, two_ref, None, s_ref)
        s_ref[...] = jnp.zeros_like(s_ref)

        @pl.when(is_outer)
        def _():
            columns(a_ref, b_ref, two_ref, part_ref, 2 * both)
            shrink(0, d0)

        @pl.when(jnp.logical_not(is_outer))
        def _():
            columns(a_ref, b_ref, mid, part_ref, 2 * both)
            shrink(0, d0, e0, 1)
            shrink(1, two_ref)

    s_shape = jax.ShapeDtypeStruct((3, rows, rank), F32)
    part, shrunk = call(
        early,
        "early_columns",
        (like(3 * both, LANES, F32), s_shape),
        [VMEM] * 8,
        (in_order, others, own_w, near_w, mid_w, two, own_d, own_e),
    )

    def last_columns(
        ints_ref, a_ref, b_ref, two_ref, three_ref, d2, e2, far, part_ref, s_in,
        keep, away, s_ref, last_ref,
    ):
        here, core = ints_ref[1], ints_ref[2] % 2
        is_outer = outer_plane(here)

        def put(ref, ref_at, holder):
            at = pl.ds(pl.multiple_of((holder // 2) * both, both), both)

            @pl.when(holder % 2 == core)
            def _():
                keep[at, :] = ref[ref_at : ref_at + both, :]

            @pl.when(holder % 2 != core)
            def _():
                away[at, :] = ref[ref_at : ref_at + both, :].astype(BF16)

        pl.when(is_outer)(lambda: columns(a_ref, b_ref, three_ref, last_ref, 0))
        shrink = shrinker(ints_ref[0], a_ref, b_ref, two_ref, three_ref, s_ref)
        s_ref[...] = s_in[...]

        @pl.when(jnp.logical_not(is_outer))
        def _():
            columns(a_ref, b_ref, far, last_ref, 0)
            shrink(2, d2, e2, 2)

        for slot in range(3):
            put(part_ref, slot * both, where_from(here, slot))
        put(last_ref, 0, where_from(here, 3))

    keep, away, shrunk = call(
        last_columns,
        "last_columns",
        (like(pairs * both, LANES, F32), like(pairs * both, LANES), s_shape),
        [VMEM] * 9,
        (in_order, others, two, three, mid_d, mid_e, far_w, part, shrunk),
        [pltpu.VMEM((both, LANES), F32)],
    )
    came = swap(away, lambda a, b, c: (a, b, c ^ 1))

    def last_shrinks(ints_ref, a_ref, b_ref, two_ref, three_ref, d3, e3, s_in, keep, away, s_ref):
        shrink = shrinker(ints_ref[0], a_ref, b_ref, two_ref, three_ref, s_ref)
        s_ref[...] = s_in[...]

        @pl.when(jnp.logical_not(outer_plane(ints_ref[1])))
        def _():
            shrink(3, d3, e3, 3)

        for g in range(3):
            s = jnp.concatenate([s_ref[g, 0:s_msg, :], s_ref[g, s_msg:rows, :]], axis=1)
            keep[g * s_msg : (g + 1) * s_msg, :] = s
            away[g * s_msg : (g + 1) * s_msg, :] = s.astype(BF16)

    s_keep, s_away = call(
        last_shrinks,
        "last_shrinks",
        (like(3 * s_msg, LANES, F32), like(3 * s_msg, LANES)),
        [VMEM] * 7,
        (in_order, others, two, three, far_d, far_e, shrunk),
        [pltpu.VMEM((3, rows, rank), F32)],
    )
    s_came = swap(s_away, lambda a, b, c: (a, b, c ^ 1))

    def add_cores(
        ints_ref, keep_ref, came_ref, s_keep, s_came, mine_out, x_out, y_out, d_out, near_out,
    ):
        side = ints_ref[2] // 2

        def tile(out, side_at, g):
            at = pl.ds(pl.multiple_of(side_at * both + g * rows, rows), rows)
            out[0:rows, :] = (keep_ref[at, :] + came_ref[at, :].astype(F32)).astype(out.dtype)

        def low_rank(out, at, g):
            s = pl.ds(g * s_msg, s_msg)
            out[at : at + s_msg, :] = (s_keep[s, :] + s_came[s, :].astype(F32)).astype(out.dtype)

        tile(mine_out, side, 0)
        tile(x_out, 1 - side, 0)
        tile(y_out, side, 1)
        tile(d_out, 1 - side, 1)
        low_rank(mine_out, rows, 0)
        low_rank(x_out, rows, 0)
        low_rank(y_out, rows, 1)
        low_rank(d_out, rows, 1)
        low_rank(near_out, 0, 2)

    mine, to_x, to_y, to_d, to_near = call(
        add_cores,
        "add_cores",
        (
            like(rows + s_msg, LANES, F32),
            like(rows + s_msg, LANES),
            like(rows + s_msg, LANES),
            like(rows + s_msg, LANES),
            like(s_msg, LANES),
        ),
        [VMEM] * 4,
        (keep, came, s_keep, s_came),
    )
    from_d = swap(to_d, lambda a, b, c: (1 - a, b, c ^ 2))
    from_nearx = swap(to_near, lambda a, b, c: (a, b ^ 1, c ^ 2))
    from_x = swap(to_x, lambda a, b, c: (a, b, c ^ 2))
    from_y = to_group(to_y)
    from_near = to_neighbour(to_near)

    def gather_ups(ints_ref, own, near, mid, far, two, three, out_ref):
        is_outer = outer_plane(ints_ref[1])

        def put(ref, slot):
            out_ref[slot * up_rows : (slot + 1) * up_rows, :] = ref[feats : feats + up_rows, :]

        put(own, 0)
        put(near, 1)

        @pl.when(is_outer)
        def _():
            put(two, 2)
            put(three, 3)

        @pl.when(jnp.logical_not(is_outer))
        def _():
            put(mid, 2)
            put(far, 3)

    ups_mine = call(
        gather_ups,
        "gather_ups",
        like(dp * up_rows, LANES),
        [VMEM] * 6,
        (own_w, near_w, mid_w, far_w, two, three),
    )
    ups_theirs = to_group(ups_mine)

    def ups(ints_ref, info_ref, mine_ref, theirs_ref, up_ref, mark_ref):
        me, here = ints_ref[0], ints_ref[1]
        live_at = dp * blocks
        for slot in range(dp):
            which, local_slot = block_at(info_ref, where_from(here, slot))
            for k in range(blocks):
                at = slot * blocks + k
                mark_ref[at : at + 1, :] = jnp.full((1, LANES), (which == k).astype(F32), F32)
            live = info_ref[adapters + blocks + which].astype(F32)
            mark_ref[live_at + slot : live_at + slot + 1, :] = jnp.full((1, LANES), live, F32)
            rows_at = slice(slot * up_rows, (slot + 1) * up_rows)

            @pl.when(local_slot == me)
            def _():
                up_ref[slot] = mine_ref[rows_at, :]

            @pl.when(local_slot != me)
            def _():
                up_ref[slot] = theirs_ref[rows_at, :]

    up_used, marks = call(
        ups,
        "ups",
        (
            jax.ShapeDtypeStruct((dp, up_rows, LANES), BF16),
            like(dp * blocks + 2 * dp, LANES, F32),
        ),
        [SMEM] + [VMEM] * 2,
        (info, ups_mine, ups_theirs),
    )

    def finish(
        ints_ref, mark_ref, up_ref, mine_ref, x_ref, y_ref, d_ref, n_ref,
        nx_ref, out_ref,
    ):
        me = ints_ref[0]
        ours = mine_ref[0:rows, :] + x_ref[0:rows, :].astype(F32)
        theirs = y_ref[0:rows, :].astype(F32) + d_ref[0:rows, :].astype(F32)
        split = (jnp.where(me == 0, ours, theirs), jnp.where(me == 0, theirs, ours))
        s = mine_ref[rows:, :] + n_ref[...].astype(F32) + nx_ref[...].astype(F32)
        for ref in (x_ref, y_ref, d_ref):
            s = s + ref[rows:, :].astype(F32)
        s = s.astype(BF16)
        per_lane = dp // 2
        row = lax.broadcasted_iota(jnp.int32, (block_len, LANES), 0).astype(F32)
        results = [[None] * col_tiles for _ in range(blocks)]
        for slot in range(dp):
            piece = s[
                (slot % per_lane) * block_len : (slot % per_lane + 1) * block_len,
                (slot // per_lane) * rank : (slot // per_lane + 1) * rank,
            ]
            live_at = dp * blocks + slot
            live = row < mark_ref[live_at : live_at + 1, :]
            for v in range(col_tiles):
                weight = up_ref[slot, v * rank : (v + 1) * rank, :]
                delta = jnp.dot(piece, weight, preferred_element_type=F32)
                base = split[v][slot * block_len : (slot + 1) * block_len, :]
                mixed = jnp.where(live, base + delta.astype(BF16).astype(F32), 0.0)
                for k in range(blocks):
                    at = slot * blocks + k
                    hit = mark_ref[at : at + 1, :] > 0.5
                    before = results[k][v]
                    results[k][v] = mixed if before is None else jnp.where(hit, mixed, before)
        for k in range(blocks):
            for v in range(col_tiles):
                out_ref[
                    k * block_len : (k + 1) * block_len, v * LANES : (v + 1) * LANES
                ] = results[k][v].astype(BF16)

    return call(
        finish,
        "finish",
        like(rows, out_cols),
        [VMEM] * 8,
        (
            marks, up_used, mine, from_x, from_y, from_d,
            from_near, from_nearx,
        ),
    )


def local(
    tokens,
    value_weight,
    adapter_down_weight,
    adapter_up_weight,
    adapter_slot_table,
    adapter_per_block,
    request_rows_per_block,
):
    dp_count = lax.axis_size("dp")
    blocks = adapter_per_block.shape[0]
    tok_rows = tokens.shape[0]
    block_len = tok_rows // blocks
    feature_total = tokens.shape[1]
    adapter_total = adapter_down_weight.shape[0]
    adapter_rank_width = adapter_down_weight.shape[2]
    column_total = adapter_up_weight.shape[2]
    partial_value = jnp.dot(
        tokens,
        lax.all_gather(value_weight, "dp", axis=1, tiled=True),
        preferred_element_type=jnp.float32,
    )
    summed = lax.psum(partial_value.astype(jnp.bfloat16), "tensor").astype(jnp.float32)
    base_cols = lax.dynamic_slice_in_dim(
        summed, lax.axis_index("tensor") * column_total, column_total, 1
    )
    matches = (
        adapter_per_block[:, None]
        == jnp.arange(adapter_slot_table.shape[0], dtype=jnp.int32)[None, :]
    )
    slot_index = jnp.sum(jnp.where(matches, adapter_slot_table[None, :], 0), axis=1)
    holder = slot_index // adapter_total
    local_slot = slot_index % adapter_total
    route_map = (holder[None, :] == jnp.arange(dp_count, dtype=jnp.int32)[:, None]).astype(
        jnp.bfloat16
    )
    local_onehot = (
        local_slot[:, None] == jnp.arange(adapter_total, dtype=jnp.int32)[None, :]
    ).astype(jnp.bfloat16)
    wanted_hot = jnp.dot(route_map, local_onehot, preferred_element_type=jnp.bfloat16)
    block_input = tokens.reshape(blocks, block_len, feature_total)
    sent_x = jnp.dot(
        route_map,
        block_input.reshape(blocks, block_len * feature_total),
        preferred_element_type=jnp.bfloat16,
    )
    sent_x = sent_x.reshape(dp_count, block_len, feature_total)
    recv_x, recv_hot = (
        lax.all_to_all(sent_x, "dp", split_axis=0, concat_axis=0, tiled=True),
        lax.all_to_all(wanted_hot, "dp", split_axis=0, concat_axis=0, tiled=True),
    )
    flat_down_weight = jnp.transpose(adapter_down_weight, (1, 0, 2)).reshape(
        feature_total, adapter_total * adapter_rank_width
    )
    every = jnp.einsum("nbf,fq->nbq", recv_x, flat_down_weight, preferred_element_type=jnp.float32)
    every = every.reshape(dp_count, block_len, adapter_total, adapter_rank_width)
    picked = jnp.sum(every * recv_hot.astype(jnp.float32)[:, None, :, None], axis=2)
    reduced_input = lax.psum(picked.astype(jnp.bfloat16), "tensor")
    spread_rows = (recv_hot[:, None, :, None] * reduced_input[:, :, None, :]).reshape(
        dp_count, block_len, adapter_total * adapter_rank_width
    )
    flat_up_weight = adapter_up_weight.reshape(adapter_total * adapter_rank_width, column_total)
    delta_rows = jnp.einsum(
        "nbq,qc->nbc", spread_rows, flat_up_weight, preferred_element_type=jnp.float32
    ).astype(jnp.bfloat16)
    returned = lax.all_to_all(delta_rows, "dp", split_axis=0, concat_axis=0, tiled=True)
    own_delta = jnp.dot(
        route_map.T,
        returned.reshape(dp_count, block_len * column_total),
        preferred_element_type=jnp.bfloat16,
    )
    own_delta = own_delta.reshape(tok_rows, column_total)
    live_rows = (
        jnp.arange(block_len, dtype=jnp.int32)[None, :] < request_rows_per_block[:, None]
    ).reshape(tok_rows)
    mixed = jnp.where(
        live_rows[:, None], base_cols + own_delta.astype(jnp.float32), jnp.float32(0.0)
    )
    return mixed.astype(jnp.bfloat16)


def solution(mesh):
    placed = (
        P(("groups", "dp"), "tensor"),
        P("tensor", "dp"),
        P("dp", "tensor", None),
        P("dp", None, "tensor"),
        P("groups"),
        P(("groups", "dp")),
        P(("groups", "dp")),
    )
    sizes = tuple(mesh.shape[a] for a in AXES)
    if sizes == (2, 4, 4):
        body = lambda *args: local_line(sizes, *args)
    else:
        body = local
    return jax.shard_map(
        body, mesh=mesh, in_specs=placed, out_specs=P(("groups", "dp"), "tensor"), check_vma=False
    )
```

```python
import jax
import jax.numpy as jnp
from jax import lax
from jax.experimental import pallas as pl
from jax.experimental.pallas import tpu as pltpu
from jax.sharding import PartitionSpec as P

AXES = ("groups", "dp", "tensor")
LANES = 128
CODE_ROWS = 16
F32 = jnp.float32
BF16 = jnp.bfloat16
VMEM = pl.BlockSpec(memory_space=pltpu.VMEM)
SMEM = pl.BlockSpec(memory_space=pltpu.SMEM)
HBM = pl.BlockSpec(memory_space=pltpu.HBM)


class Place:
    def __getitem__(self, n):
        return lax.axis_index(AXES[n]).astype(jnp.int32)


def call(body, name, outs, specs, ins, scratch=(), mib=16):
    return pl.pallas_call(
        lambda *refs: body(Place(), *refs),
        name=name,
        out_shape=outs,
        in_specs=specs,
        out_specs=jax.tree.map(lambda _: VMEM, outs),
        scratch_shapes=scratch,
        compiler_params=pltpu.CompilerParams(vmem_limit_bytes=mib * 2**20),
    )(*ins)


def like(rows, cols, dtype=BF16):
    return jax.ShapeDtypeStruct((rows, cols), dtype)


def local_line(sizes, tokens, value_weight, down, up, slot_table, per_block, live_rows):
    groups, dp, tensor = sizes
    rows, feats = tokens.shape
    blocks = per_block.shape[0]
    block_len = rows // blocks
    per_dev, _, rank = down.shape
    out_cols = up.shape[2]
    half_cols = value_weight.shape[1] // groups
    half = feats // 2
    up_rows = rank * out_cols // LANES
    col_tiles = out_cols // LANES
    pairs = dp // 2
    both = groups * rows
    s_msg = rows // 2

    def device(a, b, c):
        return (a * dp + b) * tensor + c

    def swap(x, where):
        perm = [
            (device(a, b, c), device(*where(a, b, c)))
            for a in range(groups)
            for b in range(dp)
            for c in range(tensor)
        ]
        return lax.ppermute(x, AXES, perm)

    def to_neighbour(x):
        return swap(x, lambda a, b, c: (a, b ^ 1, c))

    def to_middle(x):
        return swap(x, lambda a, b, c: (a, 3 - b, c) if b in (1, 2) else (a, b, c ^ 1))

    def to_group(x):
        return swap(x, lambda a, b, c: (1 - a, b, c))

    def tie(x, *earlier):
        return lax.optimization_barrier((x, *earlier))[0]

    def outer_plane(here):
        return (here == 0) | (here == 3)

    def where_from(here, slot):
        near = here ^ 1
        if slot == 0:
            return here
        if slot == 1:
            return near
        if slot == 2:
            return jnp.where(outer_plane(here), 3 - near, 3 - here)
        return jnp.where(outer_plane(here), 3 - here, 3 - near)

    adapters = slot_table.shape[0]
    info = jnp.concatenate([slot_table, per_block, live_rows])

    def block_at(info_ref, holder):
        which, local_slot = jnp.int32(0), jnp.int32(0)
        for k in range(blocks):
            s = info_ref[info_ref[adapters + k]]
            hit = s // per_dev == holder
            which = jnp.where(hit, k, which)
            local_slot = jnp.where(hit, s % per_dev, local_slot)
        return which, local_slot

    group = lax.axis_index("groups")
    up_mine = lax.dynamic_index_in_dim(up, group, 0, keepdims=False)
    own_w = jnp.concatenate(
        [lax.dynamic_slice_in_dim(value_weight, group * half_cols, half_cols, 1)]
        + [up_mine[:, v * LANES : (v + 1) * LANES] for v in range(col_tiles)]
    )

    tiles = feats // LANES
    tile_rows = tiles * block_len
    wide_rows = feats + up_rows
    code_at = half + tile_rows

    def sort_blocks(ints_ref, info_ref, tok_ref, sorted_ref, sems):
        here = ints_ref[1]
        copies = []
        row = lax.broadcasted_iota(jnp.int32, (CODE_ROWS, LANES), 0)
        code = jnp.zeros((CODE_ROWS, LANES), jnp.int32)
        for slot in range(dp):
            which, local_slot = block_at(info_ref, where_from(here, slot))
            src = tok_ref.at[pl.ds(pl.multiple_of(which * block_len, block_len), block_len)]
            to = sorted_ref.at[pl.ds(slot * block_len, block_len)]
            copies.append(pltpu.make_async_copy(src, to, sems.at[slot]))
            copies[-1].start()
            code = jnp.where(row == slot, local_slot, code)
        sorted_ref[rows:, 0:LANES] = code.astype(F32).astype(BF16)
        for c in copies:
            c.wait()

    in_order = call(
        sort_blocks,
        "sort_blocks",
        like(rows + CODE_ROWS, feats),
        [SMEM, HBM],
        (info, tokens),
        [pltpu.SemaphoreType.DMA((dp,))],
        mib=16,
    )

    def pack_shrinks(ints_ref, sorted_ref, d_ref, own_ref, other_ref, first_ref, second_ref):
        me = ints_ref[0]
        for which, ref in ((me, own_ref), (1 - me, other_ref)):
            d = d_ref[which]
            ref[...] = jnp.concatenate([d[:, 0:half], d[:, half:feats]], axis=0).T
        first_ref[0:half, :] = own_ref[...]
        first_ref[code_at : code_at + CODE_ROWS, :] = sorted_ref[rows:, 0:LANES]
        for n, (ref, at) in enumerate(((first_ref, half), (second_ref, 0), (second_ref, tile_rows))):
            for i in range(tiles):
                ref[at + i * block_len : at + (i + 1) * block_len, :] = sorted_ref[
                    (n + 1) * block_len : (n + 2) * block_len, i * LANES : (i + 1) * LANES
                ]

    own_d, own_e, first, second = call(
        pack_shrinks,
        "pack_shrinks",
        (like(half, LANES), like(half, LANES), like(wide_rows, LANES), like(wide_rows, LANES)),
        [VMEM, VMEM],
        (in_order, jnp.transpose(down, (0, 2, 1))),
    )

    def choose(ints_ref, outer_ref, inner_ref, out_ref):
        is_outer = outer_plane(ints_ref[1])

        @pl.when(is_outer)
        def _():
            out_ref[...] = outer_ref[...]

        @pl.when(jnp.logical_not(is_outer))
        def _():
            out_ref[...] = inner_ref[...]

    def chosen(x, y):
        return call(choose, "choose", like(wide_rows, LANES), [VMEM, VMEM], (x, y))

    near_w = to_neighbour(own_w)
    mid_w = to_middle(own_w)
    others = to_group(in_order)
    two = to_neighbour(chosen(first, mid_w))
    far_w = to_middle(near_w)
    mid_d = to_middle(tie(own_d, near_w))
    three = to_neighbour(chosen(second, tie(far_w, two)))
    near_d = two[0:half]
    mid_e = to_group(tie(mid_d, others, near_d))
    far_d = to_middle(near_d)
    far_e = to_group(tie(far_d, mid_e))

    def columns(a_ref, b_ref, w_ref, out_ref, at):
        for g, x in enumerate((a_ref, b_ref)):
            out_ref[at + g * rows : at + (g + 1) * rows, :] = jnp.dot(
                x[0:rows, :], w_ref[0:feats, :], preferred_element_type=F32
            )

    def shrinker(me, a_ref, b_ref, two_ref, three_ref, s_ref):
        number = me.astype(F32)
        codes = [ref[rows:, 0:LANES].astype(F32) for ref in (a_ref, b_ref)]
        near_codes = two_ref[code_at : code_at + CODE_ROWS, :].astype(F32)

        def shrink(slot, d_ref, e_ref=None, theirs=0):
            at = slice(slot * block_len, (slot + 1) * block_len)
            x = [a_ref[at, :], b_ref[at, :]]
            rhs = d_ref[0:half, :]
            if theirs:
                ref = two_ref if theirs == 1 else three_ref
                near_at = (half, 0, tile_rows)[theirs - 1]
                x.append(
                    jnp.concatenate(
                        [
                            ref[near_at + i * block_len : near_at + (i + 1) * block_len, :]
                            for i in range(tiles)
                        ],
                        axis=1,
                    )
                )
                rhs = jnp.concatenate([rhs, e_ref[...]], axis=1)
            x = jnp.concatenate(x, axis=0)
            low = jnp.dot(x[:, 0:half], rhs, preferred_element_type=F32)
            high = jnp.dot(x[:, half:feats], rhs, preferred_element_type=F32)
            mine = low[:, 0:rank] + high[:, rank : 2 * rank]
            for g in range(groups):
                hit = codes[g][slot : slot + 1, 0:rank] == number
                s_ref[g, at, :] = jnp.where(hit, mine[g * block_len : (g + 1) * block_len, :], 0.0)
            if theirs:
                last = slice(groups * block_len, (groups + 1) * block_len)
                other = (
                    low[last, LANES : LANES + rank] + high[last, LANES + rank : LANES + 2 * rank]
                )
                hit = near_codes[theirs : theirs + 1, 0:rank] == number
                s_ref[2, theirs * block_len : (theirs + 1) * block_len, :] = jnp.where(
                    hit, mine[last, :], other
                )

        return shrink

    def early(ints_ref, a_ref, b_ref, w0, w1, mid, two_ref, d0, e0, part_ref, s_ref):
        columns(a_ref, b_ref, w0, part_ref, 0)
        columns(a_ref, b_ref, w1, part_ref, both)
        is_outer = outer_plane(ints_ref[1])
        shrink = shrinker(ints_ref[0], a_ref, b_ref, two_ref, None, s_ref)
        s_ref[...] = jnp.zeros_like(s_ref)

        @pl.when(is_outer)
        def _():
            columns(a_ref, b_ref, two_ref, part_ref, 2 * both)
            shrink(0, d0)

        @pl.when(jnp.logical_not(is_outer))
        def _():
            columns(a_ref, b_ref, mid, part_ref, 2 * both)
            shrink(0, d0, e0, 1)
            shrink(1, two_ref)

    s_shape = jax.ShapeDtypeStruct((3, rows, rank), F32)
    part, shrunk = call(
        early,
        "early_columns",
        (like(3 * both, LANES, F32), s_shape),
        [VMEM] * 8,
        (in_order, others, own_w, near_w, mid_w, two, own_d, own_e),
    )

    def last_columns(
        ints_ref, a_ref, b_ref, two_ref, three_ref, d2, e2, far, part_ref, s_in,
        keep, away, s_ref, last_ref,
    ):
        here, core = ints_ref[1], ints_ref[2] % 2
        is_outer = outer_plane(here)

        def put(ref, ref_at, holder):
            at = pl.ds(pl.multiple_of((holder // 2) * both, both), both)

            @pl.when(holder % 2 == core)
            def _():
                keep[at, :] = ref[ref_at : ref_at + both, :]

            @pl.when(holder % 2 != core)
            def _():
                away[at, :] = ref[ref_at : ref_at + both, :].astype(BF16)

        pl.when(is_outer)(lambda: columns(a_ref, b_ref, three_ref, last_ref, 0))
        shrink = shrinker(ints_ref[0], a_ref, b_ref, two_ref, three_ref, s_ref)
        s_ref[...] = s_in[...]

        @pl.when(jnp.logical_not(is_outer))
        def _():
            columns(a_ref, b_ref, far, last_ref, 0)
            shrink(2, d2, e2, 2)

        for slot in range(3):
            put(part_ref, slot * both, where_from(here, slot))
        put(last_ref, 0, where_from(here, 3))

    keep, away, shrunk = call(
        last_columns,
        "last_columns",
        (like(pairs * both, LANES, F32), like(pairs * both, LANES), s_shape),
        [VMEM] * 9,
        (in_order, others, two, three, mid_d, mid_e, far_w, part, shrunk),
        [pltpu.VMEM((both, LANES), F32)],
    )
    came = swap(away, lambda a, b, c: (a, b, c ^ 1))

    def last_shrinks(ints_ref, a_ref, b_ref, two_ref, three_ref, d3, e3, s_in, keep, away, s_ref):
        shrink = shrinker(ints_ref[0], a_ref, b_ref, two_ref, three_ref, s_ref)
        s_ref[...] = s_in[...]

        @pl.when(jnp.logical_not(outer_plane(ints_ref[1])))
        def _():
            shrink(3, d3, e3, 3)

        for g in range(3):
            s = jnp.concatenate([s_ref[g, 0:s_msg, :], s_ref[g, s_msg:rows, :]], axis=1)
            keep[g * s_msg : (g + 1) * s_msg, :] = s
            away[g * s_msg : (g + 1) * s_msg, :] = s.astype(BF16)

    s_keep, s_away = call(
        last_shrinks,
        "last_shrinks",
        (like(3 * s_msg, LANES, F32), like(3 * s_msg, LANES)),
        [VMEM] * 7,
        (in_order, others, two, three, far_d, far_e, shrunk),
        [pltpu.VMEM((3, rows, rank), F32)],
    )
    s_came = swap(s_away, lambda a, b, c: (a, b, c ^ 1))

    def add_cores(
        ints_ref, keep_ref, came_ref, s_keep, s_came, mine_out, x_out, y_out, d_out, near_out,
    ):
        side = ints_ref[2] // 2

        def tile(out, side_at, g):
            at = pl.ds(pl.multiple_of(side_at * both + g * rows, rows), rows)
            out[0:rows, :] = (keep_ref[at, :] + came_ref[at, :].astype(F32)).astype(out.dtype)

        def low_rank(out, at, g):
            s = pl.ds(g * s_msg, s_msg)
            out[at : at + s_msg, :] = (s_keep[s, :] + s_came[s, :].astype(F32)).astype(out.dtype)

        tile(mine_out, side, 0)
        tile(x_out, 1 - side, 0)
        tile(y_out, side, 1)
        tile(d_out, 1 - side, 1)
        low_rank(mine_out, rows, 0)
        low_rank(x_out, rows, 0)
        low_rank(y_out, rows, 1)
        low_rank(d_out, rows, 1)
        low_rank(near_out, 0, 2)

    mine, to_x, to_y, to_d, to_near = call(
        add_cores,
        "add_cores",
        (
            like(rows + s_msg, LANES, F32),
            like(rows + s_msg, LANES),
            like(rows + s_msg, LANES),
            like(rows + s_msg, LANES),
            like(s_msg, LANES),
        ),
        [VMEM] * 4,
        (keep, came, s_keep, s_came),
    )
    from_d = swap(to_d, lambda a, b, c: (1 - a, b, c ^ 2))
    from_nearx = swap(to_near, lambda a, b, c: (a, b ^ 1, c ^ 2))
    from_x = swap(to_x, lambda a, b, c: (a, b, c ^ 2))
    from_y = to_group(to_y)
    from_near = to_neighbour(to_near)

    def gather_ups(ints_ref, own, near, mid, far, two, three, out_ref):
        is_outer = outer_plane(ints_ref[1])

        def put(ref, slot):
            out_ref[slot * up_rows : (slot + 1) * up_rows, :] = ref[feats : feats + up_rows, :]

        put(own, 0)
        put(near, 1)

        @pl.when(is_outer)
        def _():
            put(two, 2)
            put(three, 3)

        @pl.when(jnp.logical_not(is_outer))
        def _():
            put(mid, 2)
            put(far, 3)

    ups_mine = call(
        gather_ups,
        "gather_ups",
        like(dp * up_rows, LANES),
        [VMEM] * 6,
        (own_w, near_w, mid_w, far_w, two, three),
    )
    ups_theirs = to_group(ups_mine)

    def ups(ints_ref, info_ref, mine_ref, theirs_ref, up_ref, mark_ref):
        me, here = ints_ref[0], ints_ref[1]
        live_at = dp * blocks
        for slot in range(dp):
            which, local_slot = block_at(info_ref, where_from(here, slot))
            for k in range(blocks):
                at = slot * blocks + k
                mark_ref[at : at + 1, :] = jnp.full((1, LANES), (which == k).astype(F32), F32)
            live = info_ref[adapters + blocks + which].astype(F32)
            mark_ref[live_at + slot : live_at + slot + 1, :] = jnp.full((1, LANES), live, F32)
            rows_at = slice(slot * up_rows, (slot + 1) * up_rows)

            @pl.when(local_slot == me)
            def _():
                up_ref[slot] = mine_ref[rows_at, :]

            @pl.when(local_slot != me)
            def _():
                up_ref[slot] = theirs_ref[rows_at, :]

    up_used, marks = call(
        ups,
        "ups",
        (
            jax.ShapeDtypeStruct((dp, up_rows, LANES), BF16),
            like(dp * blocks + 2 * dp, LANES, F32),
        ),
        [SMEM] + [VMEM] * 2,
        (info, ups_mine, ups_theirs),
    )

    def finish(
        ints_ref, mark_ref, up_ref, mine_ref, x_ref, y_ref, d_ref, n_ref,
        nx_ref, out_ref,
    ):
        me = ints_ref[0]
        ours = mine_ref[0:rows, :] + x_ref[0:rows, :].astype(F32)
        theirs = y_ref[0:rows, :].astype(F32) + d_ref[0:rows, :].astype(F32)
        split = (jnp.where(me == 0, ours, theirs), jnp.where(me == 0, theirs, ours))
        s = mine_ref[rows:, :] + n_ref[...].astype(F32) + nx_ref[...].astype(F32)
        for ref in (x_ref, y_ref, d_ref):
            s = s + ref[rows:, :].astype(F32)
        s = s.astype(BF16)
        per_lane = dp // 2
        row = lax.broadcasted_iota(jnp.int32, (block_len, LANES), 0).astype(F32)
        results = [[None] * col_tiles for _ in range(blocks)]
        for slot in range(dp):
            piece = s[
                (slot % per_lane) * block_len : (slot % per_lane + 1) * block_len,
                (slot // per_lane) * rank : (slot // per_lane + 1) * rank,
            ]
            live_at = dp * blocks + slot
            live = row < mark_ref[live_at : live_at + 1, :]
            for v in range(col_tiles):
                weight = up_ref[slot, v * rank : (v + 1) * rank, :]
                delta = jnp.dot(piece, weight, preferred_element_type=F32)
                base = split[v][slot * block_len : (slot + 1) * block_len, :]
                mixed = jnp.where(live, base + delta.astype(BF16).astype(F32), 0.0)
                for k in range(blocks):
                    at = slot * blocks + k
                    hit = mark_ref[at : at + 1, :] > 0.5
                    before = results[k][v]
                    results[k][v] = mixed if before is None else jnp.where(hit, mixed, before)
        for k in range(blocks):
            for v in range(col_tiles):
                out_ref[
                    k * block_len : (k + 1) * block_len, v * LANES : (v + 1) * LANES
                ] = results[k][v].astype(BF16)

    return call(
        finish,
        "finish",
        like(rows, out_cols),
        [VMEM] * 8,
        (
            marks, up_used, mine, from_x, from_y, from_d,
            from_near, from_nearx,
        ),
    )


def local(
    tokens,
    value_weight,
    adapter_down_weight,
    adapter_up_weight,
    adapter_slot_table,
    adapter_per_block,
    request_rows_per_block,
):
    dp_count = lax.axis_size("dp")
    blocks = adapter_per_block.shape[0]
    tok_rows = tokens.shape[0]
    block_len = tok_rows // blocks
    feature_total = tokens.shape[1]
    adapter_total = adapter_down_weight.shape[0]
    adapter_rank_width = adapter_down_weight.shape[2]
    column_total = adapter_up_weight.shape[2]
    partial_value = jnp.dot(
        tokens,
        lax.all_gather(value_weight, "dp", axis=1, tiled=True),
        preferred_element_type=jnp.float32,
    )
    summed = lax.psum(partial_value.astype(jnp.bfloat16), "tensor").astype(jnp.float32)
    base_cols = lax.dynamic_slice_in_dim(
        summed, lax.axis_index("tensor") * column_total, column_total, 1
    )
    matches = (
        adapter_per_block[:, None]
        == jnp.arange(adapter_slot_table.shape[0], dtype=jnp.int32)[None, :]
    )
    slot_index = jnp.sum(jnp.where(matches, adapter_slot_table[None, :], 0), axis=1)
    holder = slot_index // adapter_total
    local_slot = slot_index % adapter_total
    route_map = (holder[None, :] == jnp.arange(dp_count, dtype=jnp.int32)[:, None]).astype(
        jnp.bfloat16
    )
    local_onehot = (
        local_slot[:, None] == jnp.arange(adapter_total, dtype=jnp.int32)[None, :]
    ).astype(jnp.bfloat16)
    wanted_hot = jnp.dot(route_map, local_onehot, preferred_element_type=jnp.bfloat16)
    block_input = tokens.reshape(blocks, block_len, feature_total)
    sent_x = jnp.dot(
        route_map,
        block_input.reshape(blocks, block_len * feature_total),
        preferred_element_type=jnp.bfloat16,
    )
    sent_x = sent_x.reshape(dp_count, block_len, feature_total)
    recv_x, recv_hot = (
        lax.all_to_all(sent_x, "dp", split_axis=0, concat_axis=0, tiled=True),
        lax.all_to_all(wanted_hot, "dp", split_axis=0, concat_axis=0, tiled=True),
    )
    flat_down_weight = jnp.transpose(adapter_down_weight, (1, 0, 2)).reshape(
        feature_total, adapter_total * adapter_rank_width
    )
    every = jnp.einsum("nbf,fq->nbq", recv_x, flat_down_weight, preferred_element_type=jnp.float32)
    every = every.reshape(dp_count, block_len, adapter_total, adapter_rank_width)
    picked = jnp.sum(every * recv_hot.astype(jnp.float32)[:, None, :, None], axis=2)
    reduced_input = lax.psum(picked.astype(jnp.bfloat16), "tensor")
    spread_rows = (recv_hot[:, None, :, None] * reduced_input[:, :, None, :]).reshape(
        dp_count, block_len, adapter_total * adapter_rank_width
    )
    flat_up_weight = adapter_up_weight.reshape(adapter_total * adapter_rank_width, column_total)
    delta_rows = jnp.einsum(
        "nbq,qc->nbc", spread_rows, flat_up_weight, preferred_element_type=jnp.float32
    ).astype(jnp.bfloat16)
    returned = lax.all_to_all(delta_rows, "dp", split_axis=0, concat_axis=0, tiled=True)
    own_delta = jnp.dot(
        route_map.T,
        returned.reshape(dp_count, block_len * column_total),
        preferred_element_type=jnp.bfloat16,
    )
    own_delta = own_delta.reshape(tok_rows, column_total)
    live_rows = (
        jnp.arange(block_len, dtype=jnp.int32)[None, :] < request_rows_per_block[:, None]
    ).reshape(tok_rows)
    mixed = jnp.where(
        live_rows[:, None], base_cols + own_delta.astype(jnp.float32), jnp.float32(0.0)
    )
    return mixed.astype(jnp.bfloat16)


def solution(mesh):
    placed = (
        P(("groups", "dp"), "tensor"),
        P("tensor", "dp"),
        P("dp", "tensor", None),
        P("dp", None, "tensor"),
        P("groups"),
        P(("groups", "dp")),
        P(("groups", "dp")),
    )
    sizes = tuple(mesh.shape[a] for a in AXES)
    if sizes == (2, 4, 4):
        body = lambda *args: local_line(sizes, *args)
    else:
        body = local
    return jax.shard_map(
        body, mesh=mesh, in_specs=placed, out_specs=P(("groups", "dp"), "tensor"), check_vma=False
    )
```

```python
import jax
import jax.numpy as jnp
from jax import lax
from jax.experimental import pallas as pl
from jax.experimental.pallas import tpu as pltpu
from jax.sharding import PartitionSpec as P

AXES = ("groups", "dp", "tensor")
LANES = 128
CODE_ROWS = 16
F32 = jnp.float32
BF16 = jnp.bfloat16
VMEM = pl.BlockSpec(memory_space=pltpu.VMEM)
SMEM = pl.BlockSpec(memory_space=pltpu.SMEM)
HBM = pl.BlockSpec(memory_space=pltpu.HBM)


class Place:
    def __getitem__(self, n):
        return lax.axis_index(AXES[n]).astype(jnp.int32)


def call(body, name, outs, specs, ins, scratch=(), mib=16):
    return pl.pallas_call(
        lambda *refs: body(Place(), *refs),
        name=name,
        out_shape=outs,
        in_specs=specs,
        out_specs=jax.tree.map(lambda _: VMEM, outs),
        scratch_shapes=scratch,
        compiler_params=pltpu.CompilerParams(vmem_limit_bytes=mib * 2**20),
    )(*ins)


def like(rows, cols, dtype=BF16):
    return jax.ShapeDtypeStruct((rows, cols), dtype)


def local_line(sizes, tokens, value_weight, down, up, slot_table, per_block, live_rows):
    groups, dp, tensor = sizes
    rows, feats = tokens.shape
    blocks = per_block.shape[0]
    block_len = rows // blocks
    per_dev, _, rank = down.shape
    out_cols = up.shape[2]
    half_cols = value_weight.shape[1] // groups
    half = feats // 2
    up_rows = rank * out_cols // LANES
    col_tiles = out_cols // LANES
    pairs = dp // 2
    both = groups * rows
    s_msg = rows // 2

    def device(a, b, c):
        return (a * dp + b) * tensor + c

    def swap(x, where):
        perm = [
            (device(a, b, c), device(*where(a, b, c)))
            for a in range(groups)
            for b in range(dp)
            for c in range(tensor)
        ]
        return lax.ppermute(x, AXES, perm)

    def to_neighbour(x):
        return swap(x, lambda a, b, c: (a, b ^ 1, c))

    def to_middle(x):
        return swap(x, lambda a, b, c: (a, 3 - b, c) if b in (1, 2) else (a, b, c ^ 1))

    def to_group(x):
        return swap(x, lambda a, b, c: (1 - a, b, c))

    def tie(x, *earlier):
        return lax.optimization_barrier((x, *earlier))[0]

    def outer_plane(here):
        return (here == 0) | (here == 3)

    def where_from(here, slot):
        near = here ^ 1
        if slot == 0:
            return here
        if slot == 1:
            return near
        if slot == 2:
            return jnp.where(outer_plane(here), 3 - near, 3 - here)
        return jnp.where(outer_plane(here), 3 - here, 3 - near)

    adapters = slot_table.shape[0]
    info = jnp.concatenate([slot_table, per_block, live_rows])

    def block_at(info_ref, holder):
        which, local_slot = jnp.int32(0), jnp.int32(0)
        for k in range(blocks):
            s = info_ref[info_ref[adapters + k]]
            hit = s // per_dev == holder
            which = jnp.where(hit, k, which)
            local_slot = jnp.where(hit, s % per_dev, local_slot)
        return which, local_slot

    group = lax.axis_index("groups")
    up_mine = lax.dynamic_index_in_dim(up, group, 0, keepdims=False)
    own_w = jnp.concatenate(
        [lax.dynamic_slice_in_dim(value_weight, group * half_cols, half_cols, 1)]
        + [up_mine[:, v * LANES : (v + 1) * LANES] for v in range(col_tiles)]
    )

    tiles = feats // LANES
    tile_rows = tiles * block_len
    wide_rows = feats + up_rows
    code_at = half + tile_rows

    def sort_blocks(ints_ref, info_ref, tok_ref, sorted_ref, sems):
        here = ints_ref[1]
        copies = []
        row = lax.broadcasted_iota(jnp.int32, (CODE_ROWS, LANES), 0)
        code = jnp.zeros((CODE_ROWS, LANES), jnp.int32)
        for slot in range(dp):
            which, local_slot = block_at(info_ref, where_from(here, slot))
            src = tok_ref.at[pl.ds(pl.multiple_of(which * block_len, block_len), block_len)]
            to = sorted_ref.at[pl.ds(slot * block_len, block_len)]
            copies.append(pltpu.make_async_copy(src, to, sems.at[slot]))
            copies[-1].start()
            code = jnp.where(row == slot, local_slot, code)
        sorted_ref[rows:, 0:LANES] = code.astype(F32).astype(BF16)
        for c in copies:
            c.wait()

    in_order = call(
        sort_blocks,
        "sort_blocks",
        like(rows + CODE_ROWS, feats),
        [SMEM, HBM],
        (info, tokens),
        [pltpu.SemaphoreType.DMA((dp,))],
        mib=16,
    )

    def pack_shrinks(ints_ref, sorted_ref, d_ref, own_ref, other_ref, first_ref, second_ref):
        me = ints_ref[0]
        for which, ref in ((me, own_ref), (1 - me, other_ref)):
            d = d_ref[which]
            ref[...] = jnp.concatenate([d[:, 0:half], d[:, half:feats]], axis=0).T
        first_ref[0:half, :] = own_ref[...]
        first_ref[code_at : code_at + CODE_ROWS, :] = sorted_ref[rows:, 0:LANES]
        for n, (ref, at) in enumerate(((first_ref, half), (second_ref, 0), (second_ref, tile_rows))):
            for i in range(tiles):
                ref[at + i * block_len : at + (i + 1) * block_len, :] = sorted_ref[
                    (n + 1) * block_len : (n + 2) * block_len, i * LANES : (i + 1) * LANES
                ]

    own_d, own_e, first, second = call(
        pack_shrinks,
        "pack_shrinks",
        (like(half, LANES), like(half, LANES), like(wide_rows, LANES), like(wide_rows, LANES)),
        [VMEM, VMEM],
        (in_order, jnp.transpose(down, (0, 2, 1))),
    )

    def choose(ints_ref, outer_ref, inner_ref, out_ref):
        is_outer = outer_plane(ints_ref[1])

        @pl.when(is_outer)
        def _():
            out_ref[...] = outer_ref[...]

        @pl.when(jnp.logical_not(is_outer))
        def _():
            out_ref[...] = inner_ref[...]

    def chosen(x, y):
        return call(choose, "choose", like(wide_rows, LANES), [VMEM, VMEM], (x, y))

    near_w = to_neighbour(own_w)
    mid_w = to_middle(own_w)
    others = to_group(in_order)
    two = to_neighbour(chosen(first, mid_w))
    far_w = to_middle(near_w)
    mid_d = to_middle(tie(own_d, mid_w))
    three = to_neighbour(chosen(second, far_w))
    near_d = two[0:half]
    mid_e = to_group(tie(mid_d, others, near_d))
    far_d = to_middle(near_d)
    far_e = to_group(tie(far_d, mid_e))

    def columns(a_ref, b_ref, w_ref, out_ref, at):
        for g, x in enumerate((a_ref, b_ref)):
            out_ref[at + g * rows : at + (g + 1) * rows, :] = jnp.dot(
                x[0:rows, :], w_ref[0:feats, :], preferred_element_type=F32
            )

    def shrinker(me, a_ref, b_ref, two_ref, three_ref, s_ref):
        number = me.astype(F32)
        codes = [ref[rows:, 0:LANES].astype(F32) for ref in (a_ref, b_ref)]
        near_codes = two_ref[code_at : code_at + CODE_ROWS, :].astype(F32)

        def shrink(slot, d_ref, e_ref=None, theirs=0):
            at = slice(slot * block_len, (slot + 1) * block_len)
            x = [a_ref[at, :], b_ref[at, :]]
            rhs = d_ref[0:half, :]
            if theirs:
                ref = two_ref if theirs == 1 else three_ref
                near_at = (half, 0, tile_rows)[theirs - 1]
                x.append(
                    jnp.concatenate(
                        [
                            ref[near_at + i * block_len : near_at + (i + 1) * block_len, :]
                            for i in range(tiles)
                        ],
                        axis=1,
                    )
                )
                rhs = jnp.concatenate([rhs, e_ref[...]], axis=1)
            x = jnp.concatenate(x, axis=0)
            low = jnp.dot(x[:, 0:half], rhs, preferred_element_type=F32)
            high = jnp.dot(x[:, half:feats], rhs, preferred_element_type=F32)
            mine = low[:, 0:rank] + high[:, rank : 2 * rank]
            for g in range(groups):
                hit = codes[g][slot : slot + 1, 0:rank] == number
                s_ref[g, at, :] = jnp.where(hit, mine[g * block_len : (g + 1) * block_len, :], 0.0)
            if theirs:
                last = slice(groups * block_len, (groups + 1) * block_len)
                other = (
                    low[last, LANES : LANES + rank] + high[last, LANES + rank : LANES + 2 * rank]
                )
                hit = near_codes[theirs : theirs + 1, 0:rank] == number
                s_ref[2, theirs * block_len : (theirs + 1) * block_len, :] = jnp.where(
                    hit, mine[last, :], other
                )

        return shrink

    def early(ints_ref, a_ref, b_ref, w0, w1, mid, two_ref, d0, e0, part_ref, s_ref):
        columns(a_ref, b_ref, w0, part_ref, 0)
        columns(a_ref, b_ref, w1, part_ref, both)
        is_outer = outer_plane(ints_ref[1])
        shrink = shrinker(ints_ref[0], a_ref, b_ref, two_ref, None, s_ref)
        s_ref[...] = jnp.zeros_like(s_ref)

        @pl.when(is_outer)
        def _():
            columns(a_ref, b_ref, two_ref, part_ref, 2 * both)
            shrink(0, d0)

        @pl.when(jnp.logical_not(is_outer))
        def _():
            columns(a_ref, b_ref, mid, part_ref, 2 * both)
            shrink(0, d0, e0, 1)
            shrink(1, two_ref)

    s_shape = jax.ShapeDtypeStruct((3, rows, rank), F32)
    part, shrunk = call(
        early,
        "early_columns",
        (like(3 * both, LANES, F32), s_shape),
        [VMEM] * 8,
        (in_order, others, own_w, near_w, mid_w, two, own_d, own_e),
    )

    def last_columns(
        ints_ref, a_ref, b_ref, two_ref, three_ref, d2, e2, far, part_ref, s_in,
        keep, away, s_ref, last_ref,
    ):
        here, core = ints_ref[1], ints_ref[2] % 2
        is_outer = outer_plane(here)

        def put(ref, ref_at, holder):
            at = pl.ds(pl.multiple_of((holder // 2) * both, both), both)

            @pl.when(holder % 2 == core)
            def _():
                keep[at, :] = ref[ref_at : ref_at + both, :]

            @pl.when(holder % 2 != core)
            def _():
                away[at, :] = ref[ref_at : ref_at + both, :].astype(BF16)

        pl.when(is_outer)(lambda: columns(a_ref, b_ref, three_ref, last_ref, 0))
        shrink = shrinker(ints_ref[0], a_ref, b_ref, two_ref, three_ref, s_ref)
        s_ref[...] = s_in[...]

        @pl.when(jnp.logical_not(is_outer))
        def _():
            columns(a_ref, b_ref, far, last_ref, 0)
            shrink(2, d2, e2, 2)

        for slot in range(3):
            put(part_ref, slot * both, where_from(here, slot))
        put(last_ref, 0, where_from(here, 3))

    keep, away, shrunk = call(
        last_columns,
        "last_columns",
        (like(pairs * both, LANES, F32), like(pairs * both, LANES), s_shape),
        [VMEM] * 9,
        (in_order, others, two, three, mid_d, mid_e, far_w, part, shrunk),
        [pltpu.VMEM((both, LANES), F32)],
    )
    came = swap(away, lambda a, b, c: (a, b, c ^ 1))

    def last_shrinks(ints_ref, a_ref, b_ref, two_ref, three_ref, d3, e3, s_in, keep, away, s_ref):
        shrink = shrinker(ints_ref[0], a_ref, b_ref, two_ref, three_ref, s_ref)
        s_ref[...] = s_in[...]

        @pl.when(jnp.logical_not(outer_plane(ints_ref[1])))
        def _():
            shrink(3, d3, e3, 3)

        for g in range(3):
            s = jnp.concatenate([s_ref[g, 0:s_msg, :], s_ref[g, s_msg:rows, :]], axis=1)
            keep[g * s_msg : (g + 1) * s_msg, :] = s
            away[g * s_msg : (g + 1) * s_msg, :] = s.astype(BF16)

    s_keep, s_away = call(
        last_shrinks,
        "last_shrinks",
        (like(3 * s_msg, LANES, F32), like(3 * s_msg, LANES)),
        [VMEM] * 7,
        (in_order, others, two, three, far_d, far_e, shrunk),
        [pltpu.VMEM((3, rows, rank), F32)],
    )
    s_came = swap(s_away, lambda a, b, c: (a, b, c ^ 1))

    def add_cores(
        ints_ref, keep_ref, came_ref, s_keep, s_came, mine_out, x_out, y_out, d_out, near_out,
    ):
        side = ints_ref[2] // 2

        def tile(out, side_at, g):
            at = pl.ds(pl.multiple_of(side_at * both + g * rows, rows), rows)
            out[0:rows, :] = (keep_ref[at, :] + came_ref[at, :].astype(F32)).astype(out.dtype)

        def low_rank(out, at, g):
            s = pl.ds(g * s_msg, s_msg)
            out[at : at + s_msg, :] = (s_keep[s, :] + s_came[s, :].astype(F32)).astype(out.dtype)

        tile(mine_out, side, 0)
        tile(x_out, 1 - side, 0)
        tile(y_out, side, 1)
        tile(d_out, 1 - side, 1)
        low_rank(mine_out, rows, 0)
        low_rank(x_out, rows, 0)
        low_rank(y_out, rows, 1)
        low_rank(d_out, rows, 1)
        low_rank(near_out, 0, 2)

    mine, to_x, to_y, to_d, to_near = call(
        add_cores,
        "add_cores",
        (
            like(rows + s_msg, LANES, F32),
            like(rows + s_msg, LANES),
            like(rows + s_msg, LANES),
            like(rows + s_msg, LANES),
            like(s_msg, LANES),
        ),
        [VMEM] * 4,
        (keep, came, s_keep, s_came),
    )
    from_d = swap(to_d, lambda a, b, c: (1 - a, b, c ^ 2))
    from_nearx = swap(to_near, lambda a, b, c: (a, b ^ 1, c ^ 2))
    from_x = swap(to_x, lambda a, b, c: (a, b, c ^ 2))
    from_y = to_group(to_y)
    from_near = to_neighbour(to_near)

    def gather_ups(ints_ref, own, near, mid, far, two, three, out_ref):
        is_outer = outer_plane(ints_ref[1])

        def put(ref, slot):
            out_ref[slot * up_rows : (slot + 1) * up_rows, :] = ref[feats : feats + up_rows, :]

        put(own, 0)
        put(near, 1)

        @pl.when(is_outer)
        def _():
            put(two, 2)
            put(three, 3)

        @pl.when(jnp.logical_not(is_outer))
        def _():
            put(mid, 2)
            put(far, 3)

    ups_mine = call(
        gather_ups,
        "gather_ups",
        like(dp * up_rows, LANES),
        [VMEM] * 6,
        (own_w, near_w, mid_w, far_w, two, three),
    )
    ups_theirs = to_group(ups_mine)

    def ups(ints_ref, info_ref, mine_ref, theirs_ref, up_ref, mark_ref):
        me, here = ints_ref[0], ints_ref[1]
        live_at = dp * blocks
        for slot in range(dp):
            which, local_slot = block_at(info_ref, where_from(here, slot))
            for k in range(blocks):
                at = slot * blocks + k
                mark_ref[at : at + 1, :] = jnp.full((1, LANES), (which == k).astype(F32), F32)
            live = info_ref[adapters + blocks + which].astype(F32)
            mark_ref[live_at + slot : live_at + slot + 1, :] = jnp.full((1, LANES), live, F32)
            rows_at = slice(slot * up_rows, (slot + 1) * up_rows)

            @pl.when(local_slot == me)
            def _():
                up_ref[slot] = mine_ref[rows_at, :]

            @pl.when(local_slot != me)
            def _():
                up_ref[slot] = theirs_ref[rows_at, :]

    up_used, marks = call(
        ups,
        "ups",
        (
            jax.ShapeDtypeStruct((dp, up_rows, LANES), BF16),
            like(dp * blocks + 2 * dp, LANES, F32),
        ),
        [SMEM] + [VMEM] * 2,
        (info, ups_mine, ups_theirs),
    )

    def finish(
        ints_ref, mark_ref, up_ref, mine_ref, x_ref, y_ref, d_ref, n_ref,
        nx_ref, out_ref,
    ):
        me = ints_ref[0]
        ours = mine_ref[0:rows, :] + x_ref[0:rows, :].astype(F32)
        theirs = y_ref[0:rows, :].astype(F32) + d_ref[0:rows, :].astype(F32)
        split = (jnp.where(me == 0, ours, theirs), jnp.where(me == 0, theirs, ours))
        s = mine_ref[rows:, :] + n_ref[...].astype(F32) + nx_ref[...].astype(F32)
        for ref in (x_ref, y_ref, d_ref):
            s = s + ref[rows:, :].astype(F32)
        s = s.astype(BF16)
        per_lane = dp // 2
        row = lax.broadcasted_iota(jnp.int32, (block_len, LANES), 0).astype(F32)
        results = [[None] * col_tiles for _ in range(blocks)]
        for slot in range(dp):
            piece = s[
                (slot % per_lane) * block_len : (slot % per_lane + 1) * block_len,
                (slot // per_lane) * rank : (slot // per_lane + 1) * rank,
            ]
            live_at = dp * blocks + slot
            live = row < mark_ref[live_at : live_at + 1, :]
            for v in range(col_tiles):
                weight = up_ref[slot, v * rank : (v + 1) * rank, :]
                delta = jnp.dot(piece, weight, preferred_element_type=F32)
                base = split[v][slot * block_len : (slot + 1) * block_len, :]
                mixed = jnp.where(live, base + delta.astype(BF16).astype(F32), 0.0)
                for k in range(blocks):
                    at = slot * blocks + k
                    hit = mark_ref[at : at + 1, :] > 0.5
                    before = results[k][v]
                    results[k][v] = mixed if before is None else jnp.where(hit, mixed, before)
        for k in range(blocks):
            for v in range(col_tiles):
                out_ref[
                    k * block_len : (k + 1) * block_len, v * LANES : (v + 1) * LANES
                ] = results[k][v].astype(BF16)

    return call(
        finish,
        "finish",
        like(rows, out_cols),
        [VMEM] * 8,
        (
            marks, up_used, mine, from_x, from_y, from_d,
            from_near, from_nearx,
        ),
    )


def local(
    tokens,
    value_weight,
    adapter_down_weight,
    adapter_up_weight,
    adapter_slot_table,
    adapter_per_block,
    request_rows_per_block,
):
    dp_count = lax.axis_size("dp")
    blocks = adapter_per_block.shape[0]
    tok_rows = tokens.shape[0]
    block_len = tok_rows // blocks
    feature_total = tokens.shape[1]
    adapter_total = adapter_down_weight.shape[0]
    adapter_rank_width = adapter_down_weight.shape[2]
    column_total = adapter_up_weight.shape[2]
    partial_value = jnp.dot(
        tokens,
        lax.all_gather(value_weight, "dp", axis=1, tiled=True),
        preferred_element_type=jnp.float32,
    )
    summed = lax.psum(partial_value.astype(jnp.bfloat16), "tensor").astype(jnp.float32)
    base_cols = lax.dynamic_slice_in_dim(
        summed, lax.axis_index("tensor") * column_total, column_total, 1
    )
    matches = (
        adapter_per_block[:, None]
        == jnp.arange(adapter_slot_table.shape[0], dtype=jnp.int32)[None, :]
    )
    slot_index = jnp.sum(jnp.where(matches, adapter_slot_table[None, :], 0), axis=1)
    holder = slot_index // adapter_total
    local_slot = slot_index % adapter_total
    route_map = (holder[None, :] == jnp.arange(dp_count, dtype=jnp.int32)[:, None]).astype(
        jnp.bfloat16
    )
    local_onehot = (
        local_slot[:, None] == jnp.arange(adapter_total, dtype=jnp.int32)[None, :]
    ).astype(jnp.bfloat16)
    wanted_hot = jnp.dot(route_map, local_onehot, preferred_element_type=jnp.bfloat16)
    block_input = tokens.reshape(blocks, block_len, feature_total)
    sent_x = jnp.dot(
        route_map,
        block_input.reshape(blocks, block_len * feature_total),
        preferred_element_type=jnp.bfloat16,
    )
    sent_x = sent_x.reshape(dp_count, block_len, feature_total)
    recv_x, recv_hot = (
        lax.all_to_all(sent_x, "dp", split_axis=0, concat_axis=0, tiled=True),
        lax.all_to_all(wanted_hot, "dp", split_axis=0, concat_axis=0, tiled=True),
    )
    flat_down_weight = jnp.transpose(adapter_down_weight, (1, 0, 2)).reshape(
        feature_total, adapter_total * adapter_rank_width
    )
    every = jnp.einsum("nbf,fq->nbq", recv_x, flat_down_weight, preferred_element_type=jnp.float32)
    every = every.reshape(dp_count, block_len, adapter_total, adapter_rank_width)
    picked = jnp.sum(every * recv_hot.astype(jnp.float32)[:, None, :, None], axis=2)
    reduced_input = lax.psum(picked.astype(jnp.bfloat16), "tensor")
    spread_rows = (recv_hot[:, None, :, None] * reduced_input[:, :, None, :]).reshape(
        dp_count, block_len, adapter_total * adapter_rank_width
    )
    flat_up_weight = adapter_up_weight.reshape(adapter_total * adapter_rank_width, column_total)
    delta_rows = jnp.einsum(
        "nbq,qc->nbc", spread_rows, flat_up_weight, preferred_element_type=jnp.float32
    ).astype(jnp.bfloat16)
    returned = lax.all_to_all(delta_rows, "dp", split_axis=0, concat_axis=0, tiled=True)
    own_delta = jnp.dot(
        route_map.T,
        returned.reshape(dp_count, block_len * column_total),
        preferred_element_type=jnp.bfloat16,
    )
    own_delta = own_delta.reshape(tok_rows, column_total)
    live_rows = (
        jnp.arange(block_len, dtype=jnp.int32)[None, :] < request_rows_per_block[:, None]
    ).reshape(tok_rows)
    mixed = jnp.where(
        live_rows[:, None], base_cols + own_delta.astype(jnp.float32), jnp.float32(0.0)
    )
    return mixed.astype(jnp.bfloat16)


def solution(mesh):
    placed = (
        P(("groups", "dp"), "tensor"),
        P("tensor", "dp"),
        P("dp", "tensor", None),
        P("dp", None, "tensor"),
        P("groups"),
        P(("groups", "dp")),
        P(("groups", "dp")),
    )
    sizes = tuple(mesh.shape[a] for a in AXES)
    if sizes == (2, 4, 4):
        body = lambda *args: local_line(sizes, *args)
    else:
        body = local
    return jax.shard_map(
        body, mesh=mesh, in_specs=placed, out_specs=P(("groups", "dp"), "tensor"), check_vma=False
    )
```
